32 devices in a mesh: dp: 16 (over z, x, core), mp: 2 (over y).
Axes of the slice: x: 2, y: 2, z: 4, core: 2. Of those that a mesh axis runs over, the one named last changes fastest.
Arguments:
- patches: bfloat16 [32, 1024, 768], P('dp'), may hold values from -6 to 6
- extra_tokens: bfloat16 [32, 2, 768], P('dp'), may hold values from -6 to 6
- visible: int32 [32, 256], P('dp'), may hold values from 0 to 1023, as said below
- qkv_weight: bfloat16 [3, 768, 768], P(None, None, 'mp'), may hold values from -0.21875 to 0.21875
- out_weight: bfloat16 [768, 768], P('mp'), may hold values from -1.75 to 1.75
- out_bias: float32 [768], replicated, may hold values from -3 to 3
- up_weight: bfloat16 [768, 3072], P(None, 'mp'), may hold values from -0.21875 to 0.21875
- up_bias: float32 [3072], P('mp'), may hold values from -3 to 3
- down_weight: bfloat16 [3072, 768], P('mp'), may hold values from -0.109375 to 0.109375
- down_bias: float32 [768], replicated, may hold values from -3 to 3
- first_gain: float32 [768], replicated, may hold values from 0.5 to 1.5
- first_shift: float32 [768], replicated, may hold values from -3 to 3
- second_gain: float32 [768], replicated, may hold values from 0.5 to 1.5
- second_shift: float32 [768], replicated, may hold values from -3 to 3
- cotangent: bfloat16 [32, 258, 768], P('dp'), may hold values from -6 to 6
Outputs:
- output: bfloat16 [32, 258, 768], P('dp')
- input_grad: float32 [32, 258, 768], P('dp')
- qkv_grad: float32 [3, 768, 768], P(None, 'dp', 'mp')
- out_grad: float32 [768, 768], P('mp', 'dp')
- out_bias_grad: float32 [768], replicated
- up_grad: float32 [768, 3072], P('dp', 'mp')
- up_bias_grad: float32 [3072], P('mp')
- down_grad: float32 [3072, 768], P('mp', 'dp')
- down_bias_grad: float32 [768], replicated
- first_gain_grad: float32 [768], replicated
- first_shift_grad: float32 [768], replicated
- second_gain_grad: float32 [768], replicated
- second_shift_grad: float32 [768], replicated
The draws below stay inside these ranges and needn't reach their ends.
Inputs may be any that keep to these rules, and one draw needn't show every extreme that they name: `visible`: each row names 256 different patches of its image.
All inputs are finite; a program needn't handle non-finite values.
Results may differ from the reference program's by a relative error of at most 0.012.
Values sent between devices are 32-bit elements; how exact they have to be, the bound alone decides.
No kernel may reach another device: no remote copies, remote signals or barrier semaphores. Data moves between devices by JAX's collectives and lax.ppermute only.
A program may use at most 128 MiB of HBM per device.

```python
import jax
import jax.numpy as jnp
from jax import lax

D = 768
HEADS = 12
HEAD_DIM = 64
FF = 3072
NP = 1024
VIS = 256
LEN = 258
IMAGES = 32


def draw_visible(key, part):
    keys = jax.random.split(key, IMAGES)
    orders = jax.vmap(lambda single: jax.random.permutation(single, NP))(keys)
    return orders[:, :VIS].astype(jnp.int32)


def raised(values, key, source, target, blocks, factor):
    def block_of(position):
        return (jnp.arange(values.shape[position]) // (values.shape[position] // blocks)).reshape((-1,) + (1,) * (values.ndim - 1 - position))

    first = jax.random.permutation(key, blocks)[block_of(target)]
    far = (block_of(target) + blocks // 2) % blocks
    return jnp.where((block_of(source) == first) | (block_of(source) == far), factor * values, values)


def block_levels(stream_key, shape, shards, smallest, high):
    def one(position, parts):
        steps = jax.random.uniform(jax.random.fold_in(jax.random.fold_in(stream_key, 6), position), (parts,), jnp.float32, smallest / len(shards), high / len(shards))
        return jnp.repeat(jnp.exp(steps), shape[position] // parts).reshape((-1,) + (1,) * (len(shape) - position - 1))

    level = one(*shards[0])
    for cut in shards[1:]:
        level = level * one(*cut)
    return level


def noise(own_key, shape, deviation, reach, cuts=(), kind=jnp.bfloat16):
    entries = deviation * jax.random.normal(own_key, shape, jnp.float32)
    if cuts:
        entries = entries * block_levels(own_key, shape, cuts, -0.22, 0.18)
    return jnp.clip(entries, -reach, reach).astype(kind)


def bell_draw_with(stream_key, dims, width, most, cuts, heavy, kind=jnp.bfloat16):
    drawn = width * jax.random.normal(stream_key, dims, jnp.float32)
    if cuts:
        drawn = drawn * block_levels(stream_key, dims, cuts, -0.22, 0.18)
    return jnp.clip(raised(drawn, jax.random.fold_in(stream_key, 3), *heavy), -most, most).astype(kind)


def setup_inputs(seed: int = 0) -> dict:
    arg_keys = jax.random.split(jax.random.key(seed), 16)
    patches = noise(arg_keys[0], (IMAGES, NP, D), 1.0, 6.0, ((0, 16),))
    extra_tokens = noise(arg_keys[1], (IMAGES, 2, D), 1.0, 6.0, ((0, 16),))
    visible = draw_visible(jax.random.fold_in(arg_keys[15], 71), 0)
    qkv_weight = noise(arg_keys[3], (3, D, D), D ** -0.5, 0.21875, ((2, 2),))
    out_weight = noise(arg_keys[4], (D, D), (D // 64) ** -0.5, 1.75, ((0, 2),))
    out_bias = noise(arg_keys[5], (D,), 0.5, 3.0, (), jnp.float32)
    up_weight = noise(arg_keys[6], (D, FF), D ** -0.5, 0.21875, ((1, 2),))
    up_bias = noise(arg_keys[7], (FF,), 0.5, 3.0, ((0, 2),), jnp.float32)
    down_weight = noise(arg_keys[8], (FF, D), FF ** -0.5, 0.109375, ((0, 2),))
    down_bias = noise(arg_keys[9], (D,), 0.5, 3.0, (), jnp.float32)
    first_gain = jnp.clip(1.0 + 0.1 * jax.random.normal(arg_keys[10], (D,), jnp.float32), 0.5, 1.5)
    first_shift = noise(arg_keys[11], (D,), 0.5, 3.0, (), jnp.float32)
    second_gain = jnp.clip(1.0 + 0.1 * jax.random.normal(arg_keys[12], (D,), jnp.float32), 0.5, 1.5)
    second_shift = noise(arg_keys[13], (D,), 0.5, 3.0, (), jnp.float32)
    cotangent = bell_draw_with(arg_keys[14], (IMAGES, LEN, D), 1.0, 6.0, ((0, 16),), (0, 2, 16, 2.0))
    return dict(patches=patches, extra_tokens=extra_tokens, visible=visible, qkv_weight=qkv_weight, out_weight=out_weight, out_bias=out_bias, up_weight=up_weight, up_bias=up_bias, down_weight=down_weight, down_bias=down_bias, first_gain=first_gain, first_shift=first_shift, second_gain=second_gain, second_shift=second_shift, cotangent=cotangent)


@jax.custom_vjp
def low(v):
    return lax.optimization_barrier(v.astype(jnp.bfloat16)).astype(jnp.float32)

@jax.custom_vjp
def low_back(v):
    return v

def low_keep(v):
    return (low(v), None)

def low_pass(kept, grad):
    return (grad,)

def back_keep(v):
    return (v, None)

def back_low(kept, grad):
    return (low(grad),)
low.defvjp(low_keep, low_pass)
low_back.defvjp(back_keep, back_low)

def layer_norm(values, gain, shift):
    center = values - lax.optimization_barrier(jnp.mean(values, -1, keepdims=True))
    spread = lax.optimization_barrier(jnp.mean(center * center, -1, keepdims=True))
    return center * lax.rsqrt(spread + 1e-06) * gain + shift

def forward(seq, qkv_weight, out_weight, out_bias, up_weight, up_bias, down_weight, down_bias, first_gain, first_shift, second_gain, second_shift):
    highest = lax.Precision.HIGHEST
    first_norm = low(layer_norm(seq, first_gain, first_shift))
    qkv = low_back(low(jnp.einsum('ld,jde->jle', first_norm, qkv_weight, precision=highest)))
    query = qkv[0].reshape(LEN, HEADS, HEAD_DIM)
    keys = qkv[1].reshape(LEN, HEADS, HEAD_DIM)
    values = qkv[2].reshape(LEN, HEADS, HEAD_DIM)
    scores = low_back(jnp.einsum('lhe,mhe->hlm', query, keys, precision=highest) * HEAD_DIM ** (-0.5))
    top = lax.optimization_barrier(jnp.max(scores, -1, keepdims=True))
    expo = jnp.exp(scores - top)
    probs = low(expo / lax.optimization_barrier(jnp.sum(expo, -1, keepdims=True)))
    mixed = low_back(low(jnp.einsum('hlm,mhe->lhe', probs, values, precision=highest).reshape(LEN, D)))
    attn = low_back(jnp.dot(mixed, out_weight, precision=highest) + out_bias)
    middle = seq + attn
    second_norm = low(layer_norm(middle, second_gain, second_shift))
    upper = low_back(jnp.dot(second_norm, up_weight, precision=highest) + up_bias)
    hidden = low(jax.nn.gelu(upper, approximate=False))
    branch = low_back(jnp.dot(hidden, down_weight, precision=highest) + down_bias)
    return middle + branch

def reference(patches, extra_tokens, visible, qkv_weight, out_weight, out_bias, up_weight, up_bias, down_weight, down_bias, first_gain, first_shift, second_gain, second_shift, cotangent):
    params = (qkv_weight.astype(jnp.float32), out_weight.astype(jnp.float32), out_bias, up_weight.astype(jnp.float32), up_bias, down_weight.astype(jnp.float32), down_bias, first_gain, first_shift, second_gain, second_shift)

    def one_image(totals, item):
        patch_rows, extra_rows, picks, cot = item
        chosen = jnp.take(patch_rows, picks.astype(jnp.int32), axis=0)
        seq = jnp.concatenate([extra_rows, chosen], 0).astype(jnp.float32)
        result, pull = jax.vjp(forward, seq, *params)
        grads = pull(cot.astype(jnp.float32))
        summed = tuple((total + grad for total, grad in zip(totals, grads[1:])))
        return (summed, (result.astype(jnp.bfloat16), grads[0]))
    start = tuple((jnp.zeros_like(param) for param in params))
    totals, (output, input_grad) = lax.scan(one_image, start, (patches, extra_tokens, visible, cotangent))
    return (output, input_grad, totals[0], totals[1], totals[2], totals[3], totals[4], totals[5], totals[6], totals[7], totals[8], totals[9], totals[10])
```

```python
from functools import partial

import jax
import jax.numpy as jnp
from jax import lax
from jax.experimental import pallas as pl
from jax.experimental.pallas import tpu as pltpu
from jax.sharding import PartitionSpec as P

HEAD_DIM = 64
PAIR = 2 * HEAD_DIM
F32 = jnp.float32
BF16 = jnp.bfloat16
MIB = 1 << 20
SWAP = ((0, 1), (1, 0))


def mm(a, b):
    return lax.dot_general(a, b, (((1,), (0,)), ((), ())), preferred_element_type=F32)


def mm_nt(a, b):
    return lax.dot_general(a, b, (((1,), (1,)), ((), ())), preferred_element_type=F32)


def mm_tn(a, b):
    return lax.dot_general(a, b, (((0,), (0,)), ((), ())), preferred_element_type=F32)


def normed(values):
    center = values - jnp.mean(values, -1, keepdims=True)
    rate = lax.rsqrt(jnp.mean(center * center, -1, keepdims=True) + 1e-06)
    return center * rate, rate


def norm_back(grad, hat, rate, gain):
    scaled = grad * gain
    return rate * (
        scaled
        - jnp.mean(scaled, -1, keepdims=True)
        - hat * jnp.mean(scaled * hat, -1, keepdims=True)
    )


def shape(dims, dtype=F32):
    return jax.ShapeDtypeStruct(tuple(dims), dtype)


def whole(x):
    return pl.BlockSpec(x.shape, lambda i: (0,) * len(x.shape))


def one_of(x, image):
    return pl.BlockSpec((None,) + x.shape[1:], lambda i: (image,) + (0,) * (x.ndim - 1))


def scalars():
    return pl.BlockSpec(memory_space=pltpu.SMEM)


def call(body, args, specs, outs, flops, vmem, name):
    moved = sum(a.size * a.dtype.itemsize for a in args) + sum(
        o.size * o.dtype.itemsize for o in outs
    )
    return pl.pallas_call(
        body,
        grid=(1,),
        out_shape=tuple(outs),
        in_specs=specs,
        out_specs=tuple(whole(o) for o in outs),
        compiler_params=pltpu.CompilerParams(vmem_limit_bytes=vmem * MIB),
        cost_estimate=pl.CostEstimate(flops=int(flops), bytes_accessed=int(moved), transcendentals=0),
        name=name,
    )(*args)


def side_masks():
    lane = lax.broadcasted_iota(jnp.int32, (1, PAIR), 1)
    low = jnp.where(lane < HEAD_DIM, 1.0, 0.0)
    return low.astype(BF16), (1.0 - low).astype(BF16)


def attend_body(pick, patch, extra, weight, gain, shift, seq_out, first_out, qkv_out, mixed_out, log_out):
    rows, width = seq_out.shape
    inner = mixed_out.shape[1]
    hot = lax.broadcasted_iota(jnp.int32, (rows, patch.shape[0]), 1) == pick[...]
    seq_out[...] = mm(jnp.where(hot, 1.0, 0.0).astype(BF16), patch[...])
    seq_out[0 : extra.shape[0], :] = extra[...].astype(F32)
    hat, _ = normed(seq_out[...])
    first = (hat * gain[...] + shift[...]).astype(BF16)
    first_out[...] = first
    for j in range(3):
        qkv_out[:, j * inner : (j + 1) * inner] = mm(first, weight[j]).astype(BF16)
    masks = side_masks()
    lane = lax.broadcasted_iota(jnp.int32, (rows, PAIR), 1)
    logs = jnp.zeros((rows, PAIR), F32)
    for pair in range(inner // PAIR):
        q = qkv_out[:, pair * PAIR : (pair + 1) * PAIR]
        k = qkv_out[:, inner + pair * PAIR : inner + (pair + 1) * PAIR]
        v = qkv_out[:, 2 * inner + pair * PAIR : 2 * inner + (pair + 1) * PAIR]
        sides = []
        for side in range(2):
            scores = mm_nt(q * masks[side], k) * (HEAD_DIM**-0.5)
            top = jnp.max(scores, -1, keepdims=True)
            expo = jnp.exp(scores - top)
            total = jnp.sum(expo, -1, keepdims=True)
            sides.append(mm((expo / total).astype(BF16), v))
            logs = jnp.where(lane == 2 * pair + side, top + jnp.log(total), logs)
        mixed = jnp.where(lane < HEAD_DIM, sides[0], sides[1]).astype(BF16)
        mixed_out[:, pair * PAIR : (pair + 1) * PAIR] = mixed.astype(F32)
    log_out[...] = logs


def join_body(ids, mine, near, far, full_out):
    half = mine.shape[0]
    part = near.shape[0]
    mp = ids[3]
    core = ids[0]
    own = pl.multiple_of(mp * half, part)
    other = pl.multiple_of((1 - mp) * half, part)
    full_out[pl.ds(own, half), :] = mine[...]
    full_out[pl.ds(pl.multiple_of(other + core * part, part), part), :] = near[...].astype(BF16)
    full_out[pl.ds(pl.multiple_of(other + (1 - core) * part, part), part), :] = far[...].astype(BF16)


def forward_body(
    ids, seq, mine, other, full, out_bias, gain, shift, up, up_bias, down, dy,
    middle_out, second_out, hidden_out, upper_out, norm_out, small_out,
):
    rows, width = seq.shape
    inner = mine.shape[1]
    first_half = ids[3] == 0
    left = jnp.where(first_half, mine[...], other[...]).astype(BF16)
    right = jnp.where(first_half, other[...], mine[...]).astype(BF16)
    attn = mm(left, full[0:inner, :]) + mm(right, full[inner:, :]) + out_bias[...]
    middle = seq[...] + attn
    middle_out[...] = middle
    hat, _ = normed(middle)
    second = (hat * gain[...] + shift[...]).astype(BF16)
    second_out[...] = second
    grad = dy[...]
    small_out[...] = jnp.zeros_like(small_out)
    chunk = 512
    norm = jnp.zeros((rows, width), F32)
    for start in range(0, up.shape[1], chunk):
        cols = slice(start, start + chunk)
        upper = mm(second, up[:, cols]) + up_bias[:, cols]
        phi = 0.5 + 0.5 * lax.erf(upper * (0.5**0.5))
        hidden_out[:, cols] = (upper * phi).astype(BF16)
        slope = phi + upper * (jnp.exp(-0.5 * upper * upper) * 0.3989422804014327)
        back = (mm_nt(grad, down[cols, :]) * slope).astype(BF16)
        upper_out[:, cols] = back
        small_out[0:1, cols] = jnp.sum(back.astype(F32), 0, keepdims=True)
        norm = norm + mm_nt(back, up[:, cols])
    norm_out[...] = norm
    small_out[1:2, 0:width] = jnp.sum(norm * hat, 0, keepdims=True)
    small_out[1:2, width:] = jnp.sum(norm, 0, keepdims=True)
    small_out[2:3, 0:width] = jnp.sum(grad.astype(F32), 0, keepdims=True)


def backward_body(
    mine, other, middle, dy, gain, out_weight, qkv, logs, weight, seq,
    grad_out, attn_out, back_out, part_out, small_out,
):
    rows, width = middle.shape
    inner = out_weight.shape[0]
    hat, rate = normed(middle[...])
    total = mine[...] + other[...]
    grad = dy[...].astype(F32) + norm_back(total, hat, rate, gain[...])
    grad_out[...] = grad
    attn = grad.astype(BF16)
    attn_out[...] = attn
    small_out[...] = jnp.zeros_like(small_out)
    small_out[2:3, width:] = jnp.sum(attn.astype(F32), 0, keepdims=True)
    mixed = mm_nt(attn, out_weight[...]).astype(BF16)
    masks = side_masks()
    lane = lax.broadcasted_iota(jnp.int32, (rows, PAIR), 1)
    scale = HEAD_DIM**-0.5
    for pair in range(inner // PAIR):
        cols = slice(pair * PAIR, (pair + 1) * PAIR)
        q = qkv[:, cols]
        k = qkv[:, inner + pair * PAIR : inner + (pair + 1) * PAIR]
        v = qkv[:, 2 * inner + pair * PAIR : 2 * inner + (pair + 1) * PAIR]
        dm = mixed[:, cols]
        q_t = q.astype(F32).T.astype(BF16)
        dm_t = dm.astype(F32).T.astype(BF16)
        dq, dk, dv = [], [], []
        for side in range(2):
            half = slice(side * HEAD_DIM, (side + 1) * HEAD_DIM)
            head = 2 * pair + side
            scores = mm_nt(q * masks[side], k) * scale
            probs = jnp.exp(scores - logs[:, head : head + 1])
            dv.append(mm(dm_t[half, :], probs.astype(BF16)))
            prob_grad = mm_nt(dm * masks[side], v)
            score = probs * (prob_grad - jnp.sum(prob_grad * probs, -1, keepdims=True))
            score = score.astype(BF16)
            dq.append(mm(score, k))
            dk.append(mm(q_t[half, :], score))
        back_out[:, cols] = (jnp.where(lane < HEAD_DIM, dq[0], dq[1]) * scale).astype(BF16)
        back_out[:, inner + pair * PAIR : inner + (pair + 1) * PAIR] = (
            jnp.concatenate(dk, 0) * scale
        ).T.astype(BF16)
        back_out[:, 2 * inner + pair * PAIR : 2 * inner + (pair + 1) * PAIR] = (
            jnp.concatenate(dv, 0).T.astype(BF16)
        )
    part = mm_nt(back_out[:, 0:inner], weight[0])
    for j in range(1, 3):
        part = part + mm_nt(back_out[:, j * inner : (j + 1) * inner], weight[j])
    part_out[...] = part
    first_hat, _ = normed(seq[...])
    small_out[3:4, 0:width] = jnp.sum(part * first_hat, 0, keepdims=True)
    small_out[3:4, width:] = jnp.sum(part, 0, keepdims=True)


def branch_body(*refs):
    (*hiddens, down, part_out) = refs
    for image, hidden in enumerate(hiddens):
        part_out[image] = mm(hidden[...], down[...])


def output_body(images, down_mine, down_other, bias, *refs):
    middles, out = refs[:images], refs[images]
    for image in range(images):
        branch = down_mine[image] + down_other[image] + bias[...]
        out[image] = (middles[image][...] + branch).astype(BF16)


def input_body(images, gain, *refs):
    out = refs[4 * images]
    for image in range(images):
        mine, other, grad, seq = (refs[4 * image + i][...] for i in range(4))
        hat, rate = normed(seq)
        out[image] = grad + norm_back(mine + other, hat, rate, gain[...])


def products(sets, start, size):
    blocks = []
    at = 0
    for lefts, rights in sets:
        columns = rights[0].shape[1]
        lo, hi = max(start, at), min(start + size, at + columns)
        if lo < hi:
            total = None
            for left, right in zip(lefts, rights):
                one = mm_tn(left[...], right[:, lo - at : hi - at])
                total = one if total is None else total + one
            blocks.append((lo - start, total))
        at += columns
    return blocks


def read_sets(refs, layout):
    sets, at = [], 0
    for images in layout:
        sets.append((refs[at : at + images], refs[at + images : at + 2 * images]))
        at += 2 * images
    return sets, refs[at:]


def grads_body(layout, dims, ids, *refs):
    sets, (send, keep) = read_sets(refs, layout)
    width, columns = send.shape[0] * 2, send.shape[1]
    size = width // (2 * dims[0] * dims[1])
    even = ids[0] == 0
    for start in range(0, columns, 384):
        for offset, block in products(sets, start, 384):
            cols = slice(start + offset, start + offset + block.shape[1])
            for x in range(dims[1]):
                for z in range(dims[0]):
                    source = (z * dims[1] + x) * 2 * size
                    zero = block[source : source + size, :]
                    one = block[source + size : source + 2 * size, :]
                    rows = slice((x * dims[0] + z) * size, (x * dims[0] + z + 1) * size)
                    keep[rows, cols] = jnp.where(even, zero, one)
                    send[rows, cols] = jnp.where(even, one, zero)


def plain_grads_body(layout, *refs):
    sets, (out,) = read_sets(refs, layout)
    columns = out.shape[1]
    for start in range(0, columns, 384):
        for offset, block in products(sets, start, 384):
            out[:, start + offset : start + offset + block.shape[1]] = block


def across_body(ids, kept, got, keep, send):
    size = keep.shape[0]
    own = pl.ds(pl.multiple_of(ids[1] * size, 8), size)
    away = pl.ds(pl.multiple_of((1 - ids[1]) * size, 8), size)
    send[...] = kept[away, :] + got[away, :]
    keep[...] = kept[own, :] + got[own, :]


def along_body(ids, kept, got, *outs):
    size = outs[0].shape[0]
    for step, out in enumerate(outs):
        rows = pl.ds(pl.multiple_of((ids[2] ^ step) * size, 8), size)
        out[...] = kept[rows, :] + got[rows, :]


def last_body(*refs):
    total = refs[0][...] + refs[1][...]
    for ref in refs[2:-1]:
        total = total + ref[...]
    refs[-1][...] = total


def weight_sum(sets, ids, dp, name):
    layout = tuple(len(lefts) for lefts, _ in sets)
    args = [a for lefts, rights in sets for a in (*lefts, *rights)]
    width = sets[0][0][0].shape[1]
    columns = sum(rights[0].shape[1] for _, rights in sets)
    flops = sum(
        2 * width * right.size for _, rights in sets for right in rights
    )
    size = width // dp
    if dp % 4 or size % 8:
        (full,) = call(
            partial(plain_grads_body, layout), args, [whole(a) for a in args],
            [shape((width, columns))], flops, 40, f"{name}_grads",
        )
        return lax.psum_scatter(full, "dp", scatter_dimension=0, tiled=True)
    dims = (dp // 4, 2)
    send, keep = call(
        partial(grads_body, layout, dims), [ids, *args], [scalars()] + [whole(a) for a in args],
        [shape((width // 2, columns))] * 2, flops, 40, f"{name}_grads",
    )
    got = lax.ppermute(send, "dp", [(i, i ^ 1) for i in range(dp)])
    keep, send = call(
        across_body, [ids, keep, got], [scalars(), whole(keep), whole(got)],
        [shape((width // 4, columns))] * 2, 0, 24, f"{name}_across",
    )
    got = lax.ppermute(send, "dp", [(i, i ^ 2) for i in range(dp)])
    mine, *sends = call(
        along_body, [ids, keep, got], [scalars(), whole(keep), whole(got)],
        [shape((size, columns))] * dims[0], 0, 16, f"{name}_along",
    )
    parts = [mine] + [
        lax.ppermute(s, "dp", [(i, i ^ (4 * step)) for i in range(dp)])
        for step, s in enumerate(sends, 1)
    ]
    (total,) = call(
        last_body, parts, [whole(a) for a in parts], [shape((size, columns))], 0, 16, f"{name}_last"
    )
    return total


def small_sum(values, dp):
    over = jnp.stack([values[1], values[3]])
    over = over + lax.ppermute(over, "mp", SWAP)
    total = jnp.stack([values[0], over[0], values[2], over[1]])
    if dp & (dp - 1):
        return lax.psum(total, "dp")
    step = 1
    while step < dp:
        total = total + lax.ppermute(total, "dp", [(i, i ^ step) for i in range(dp)])
        step *= 2
    return total


def per_device(
    dp,
    patches,
    extra_tokens,
    visible,
    qkv_weight,
    out_weight,
    out_bias,
    up_weight,
    up_bias,
    down_weight,
    down_bias,
    first_gain,
    first_shift,
    second_gain,
    second_shift,
    cotangent,
):
    images, _, width = patches.shape
    extras = extra_tokens.shape[1]
    rows = visible.shape[1] + extras
    inner = qkv_weight.shape[2]
    hidden_width = up_weight.shape[1]
    place = lax.axis_index("dp")
    core = place % 2
    ids = jnp.stack([core, place // 2 % 2, place // 4, lax.axis_index("mp")]).astype(jnp.int32)
    row = lambda v: v.reshape(1, -1)
    pick = jnp.pad(visible, ((0, 0), (extras, 0)), constant_values=-1)[:, :, None]

    quarter = inner // 2
    piece = lax.dynamic_slice_in_dim(out_weight, core * quarter, quarter, 0).astype(F32)
    near = lax.ppermute(piece, "mp", SWAP)
    far = lax.ppermute(near, "dp", [(i, i ^ 1) for i in range(dp)])
    (full,) = call(
        join_body, [ids, out_weight, near, far],
        [scalars(), whole(out_weight), whole(near), whole(far)],
        [shape((2 * inner, width), BF16)], 0, 16, "join",
    )

    seqs, firsts, qkvs, mixeds, logs = [], [], [], [], []
    for b in range(images):
        args = [pick, patches, extra_tokens, qkv_weight, row(first_gain), row(first_shift)]
        got = call(
            attend_body, args,
            [one_of(a, b) for a in args[:3]] + [whole(a) for a in args[3:]],
            [shape((rows, width)), shape((rows, width), BF16), shape((rows, 3 * inner), BF16),
             shape((rows, inner)), shape((rows, PAIR))],
            2 * rows * width * (patches.shape[1] + 3 * inner), 32, f"attend{b}",
        )
        for kept, one in zip((seqs, firsts, qkvs, mixeds, logs), got):
            kept.append(one)

    middles, seconds, hiddens, uppers, norms, smalls = [], [], [], [], [], []
    for b in range(images):
        other = lax.ppermute(mixeds[b], "mp", SWAP)
        args = [seqs[b], mixeds[b], other, full, row(out_bias), row(second_gain), row(second_shift),
                up_weight, row(up_bias), down_weight]
        got = call(
            forward_body, [ids, *args, cotangent],
            [scalars()] + [whole(a) for a in args] + [one_of(cotangent, b)],
            [shape((rows, width)), shape((rows, width), BF16), shape((rows, hidden_width), BF16),
             shape((rows, hidden_width), BF16), shape((rows, width)), shape((8, hidden_width))],
            2 * rows * width * (width + 3 * hidden_width), 40, f"forward{b}",
        )
        for kept, one in zip((middles, seconds, hiddens, uppers, norms, smalls), got):
            kept.append(one)

    grads, attns, backs, firsts_part = [], [], [], []
    for b in range(images):
        other = lax.ppermute(norms[b], "mp", SWAP)
        args = [out_weight, qkvs[b], logs[b], qkv_weight, seqs[b]]
        got = call(
            backward_body, [norms[b], other, middles[b], cotangent, row(second_gain), *args],
            [whole(norms[b]), whole(other), whole(middles[b]), one_of(cotangent, b), whole(row(second_gain))]
            + [whole(a) for a in args],
            [shape((rows, width)), shape((rows, width), BF16), shape((rows, 3 * inner), BF16),
             shape((rows, width)), shape((8, hidden_width))],
            2 * rows * width * 4 * inner, 40, f"backward{b}",
        )
        for kept, one in zip((grads, attns, backs, firsts_part, smalls), got):
            kept.append(one)

    dys = [cotangent[b] for b in range(images)]
    mixed_low = [m.astype(BF16) for m in mixeds]
    down_sum = weight_sum([(dys, hiddens)], ids, dp, "down")
    up_sum = weight_sum([(seconds, uppers)], ids, dp, "up")
    last_sum = weight_sum([(attns, mixed_low), (firsts, backs)], ids, dp, "last")

    args = [*hiddens, down_weight]
    (down_part,) = call(
        branch_body, args, [whole(a) for a in args], [shape((images, rows, width))],
        2 * images * rows * width * hidden_width, 32, "branch",
    )
    down_other = lax.ppermute(down_part, "mp", SWAP)
    args = [down_part, down_other, row(down_bias), *middles]
    (output,) = call(
        partial(output_body, images), args, [whole(a) for a in args],
        [shape((images, rows, width), BF16)], 0, 32, "output",
    )

    args = [row(first_gain)]
    for b in range(images):
        args += [firsts_part[b], lax.ppermute(firsts_part[b], "mp", SWAP), grads[b], seqs[b]]
    (input_grad,) = call(
        partial(input_body, images), args, [whole(a) for a in args],
        [shape((images, rows, width))], 0, 32, "input",
    )

    small = small_sum(sum(smalls), dp)
    return (
        output,
        input_grad,
        last_sum[:, inner:].reshape(-1, 3, inner).transpose(1, 0, 2),
        last_sum[:, :inner].T,
        small[2, width:],
        up_sum,
        small[0],
        down_sum.T,
        small[2, :width],
        small[3, :width],
        small[3, width:],
        small[1, :width],
        small[1, width:],
    )


def solution(mesh):
    return jax.shard_map(
        partial(per_device, mesh.shape["dp"]),
        mesh=mesh,
        in_specs=(
            P("dp", None, None),
            P("dp", None, None),
            P("dp", None),
            P(None, None, "mp"),
            P("mp", None),
            P(),
            P(None, "mp"),
            P("mp"),
            P("mp", None),
            P(),
            P(),
            P(),
            P(),
            P(),
            P("dp", None, None),
        ),
        out_specs=(
            P("dp", None, None),
            P("dp", None, None),
            P(None, "dp", "mp"),
            P("mp", "dp"),
            P(),
            P("dp", "mp"),
            P("mp"),
            P("mp", "dp"),
            P(),
            P(),
            P(),
            P(),
            P(),
        ),
        check_vma=False,
    )
```

```python
from functools import partial

import jax
import jax.numpy as jnp
from jax import lax
from jax.experimental import pallas as pl
from jax.experimental.pallas import tpu as pltpu
from jax.sharding import PartitionSpec as P

HEAD_DIM = 64
PAIR = 2 * HEAD_DIM
F32 = jnp.float32
BF16 = jnp.bfloat16
MIB = 1 << 20
SWAP = ((0, 1), (1, 0))


def mm(a, b):
    return lax.dot_general(a, b, (((1,), (0,)), ((), ())), preferred_element_type=F32)


def mm_nt(a, b):
    return lax.dot_general(a, b, (((1,), (1,)), ((), ())), preferred_element_type=F32)


def mm_tn(a, b):
    return lax.dot_general(a, b, (((0,), (0,)), ((), ())), preferred_element_type=F32)


def normed(values):
    center = values - jnp.mean(values, -1, keepdims=True)
    rate = lax.rsqrt(jnp.mean(center * center, -1, keepdims=True) + 1e-06)
    return center * rate, rate


def norm_back(grad, hat, rate, gain):
    scaled = grad * gain
    return rate * (
        scaled
        - jnp.mean(scaled, -1, keepdims=True)
        - hat * jnp.mean(scaled * hat, -1, keepdims=True)
    )


def shape(dims, dtype=F32):
    return jax.ShapeDtypeStruct(tuple(dims), dtype)


def far(dims, dtype=F32):
    return pltpu.HBM(tuple(dims), dtype)


def whole(x):
    return pl.BlockSpec(x.shape, lambda i: (0,) * len(x.shape))


def one_of(x, image):
    return pl.BlockSpec((None,) + x.shape[1:], lambda i: (image,) + (0,) * (x.ndim - 1))


def scalars():
    return pl.BlockSpec(memory_space=pltpu.SMEM)


ANYWHERE = pl.BlockSpec(memory_space=pl.ANY)


class Chain:
    def __init__(self):
        self.token = jnp.zeros((8, 128), F32)

    def call(self, body, args, specs, outs, vmem, name, grid=1, out_specs=None, scratch=(), deep=()):
        taken, given = len(args), len(outs)
        args = [pltpu.with_memory_space_constraint(a, pltpu.HBM) if i in deep else a for i, a in enumerate(args)]

        def without_tokens(*refs):
            return body(*refs[:taken], *refs[taken + 1 : taken + 1 + given], *refs[taken + 2 + given :])

        *got, self.token = pl.pallas_call(
            without_tokens,
            grid=(grid,),
            out_shape=(*outs, shape((8, 128))),
            in_specs=[*specs, ANYWHERE],
            out_specs=(*(out_specs or [whole(o) for o in outs]), ANYWHERE),
            scratch_shapes=list(scratch),
            compiler_params=pltpu.CompilerParams(vmem_limit_bytes=vmem * MIB),
            cost_estimate=pl.CostEstimate(flops=1 << 31, bytes_accessed=1, transcendentals=0),
            name=name,
        )(*args, self.token)
        return got

    def at_once(self, ids, moves, *values):
        outs = jax.eval_shape(moves, *values)
        moved = lambda token, *vs: (token, *moves(*vs))
        never = lambda token, *vs: (token, *(jnp.zeros(o.shape, o.dtype) for o in outs))
        self.token, *got = lax.cond(ids[0] >= 0, moved, never, self.token, *values)
        return got


def line(vector):
    return vector[...].reshape(1, -1)


def side_masks():
    lane = lax.broadcasted_iota(jnp.int32, (1, PAIR), 1)
    low = jnp.where(lane < HEAD_DIM, 1.0, 0.0)
    return low.astype(BF16), (1.0 - low).astype(BF16)


def attend_body(images, pick, patch, extra, weight, gain, shift, *refs):
    seq_out, first_out, qkv_out, log_out, *mixed_outs = refs
    rows, width = seq_out.shape
    inner = mixed_outs[0].shape[1]
    image = pl.program_id(0)
    extras, picks = extra.shape[1], pick.shape[1]
    spread = jnp.broadcast_to(pick[pl.ds(image, 1), :].astype(F32), (128, picks))
    column = spread.T[:, 0:1].astype(jnp.int32)
    hot = lax.broadcasted_iota(jnp.int32, (picks, patch.shape[0]), 1) == column
    seq_out[extras:, :] = mm(jnp.where(hot, 1.0, 0.0).astype(BF16), patch[...])
    seq_out[0:extras, :] = extra[image].astype(F32)
    hat, _ = normed(seq_out[...])
    first = (hat * line(gain) + line(shift)).astype(BF16)
    first_out[...] = first
    for j in range(3):
        qkv_out[:, j * inner : (j + 1) * inner] = mm(first, weight[j]).astype(BF16)
    masks = side_masks()
    lane = lax.broadcasted_iota(jnp.int32, (rows, PAIR), 1)
    logs = jnp.zeros((rows, PAIR), F32)
    for pair in range(inner // PAIR):
        q = qkv_out[:, pair * PAIR : (pair + 1) * PAIR]
        k = qkv_out[:, inner + pair * PAIR : inner + (pair + 1) * PAIR]
        v = qkv_out[:, 2 * inner + pair * PAIR : 2 * inner + (pair + 1) * PAIR]
        sides = []
        for side in range(2):
            scores = mm_nt(q * masks[side], k) * (HEAD_DIM**-0.5)
            top = jnp.max(scores, -1, keepdims=True)
            expo = jnp.exp(scores - top)
            total = jnp.sum(expo, -1, keepdims=True)
            sides.append(mm((expo / total).astype(BF16), v))
            logs = jnp.where(lane == 2 * pair + side, top + jnp.log(total), logs)
        mixed = jnp.where(lane < HEAD_DIM, sides[0], sides[1]).astype(BF16).astype(F32)
        for b, out in enumerate(mixed_outs):
            @pl.when(image == b)
            def _(out=out, mixed=mixed, pair=pair):
                out[:, pair * PAIR : (pair + 1) * PAIR] = mixed
    log_out[...] = logs


def join_body(ids, mine, near, far, full_out):
    half = mine.shape[0]
    part = near.shape[0]
    mp = ids[4]
    core = ids[0]
    own = pl.multiple_of(mp * half, part)
    other = pl.multiple_of((1 - mp) * half, part)
    full_out[pl.ds(own, half), :] = mine[...]
    full_out[pl.ds(pl.multiple_of(other + core * part, part), part), :] = near[...].astype(BF16)
    full_out[pl.ds(pl.multiple_of(other + (1 - core) * part, part), part), :] = far[...].astype(BF16)


def forward_body(
    ids, seq, dy, out_bias, gain, shift, up_bias, mine, other, full, up, down,
    middle_out, second_out, hidden_out, upper_out, norm_out, small_out,
):
    rows, width = seq.shape
    inner = mine.shape[1]
    first_half = ids[4] == 0
    left = jnp.where(first_half, mine[...], other[...]).astype(BF16)
    right = jnp.where(first_half, other[...], mine[...]).astype(BF16)
    attn = mm(left, full[0:inner, :]) + mm(right, full[inner:, :]) + line(out_bias)
    middle = seq[...] + attn
    middle_out[...] = middle
    hat, _ = normed(middle)
    second = (hat * line(gain) + line(shift)).astype(BF16)
    second_out[...] = second
    grad = dy[...].astype(BF16)
    small_out[...] = jnp.zeros_like(small_out)
    chunk = 512
    biases = line(up_bias)
    norm = jnp.zeros((rows, width), F32)
    for start in range(0, up.shape[1], chunk):
        cols = slice(start, start + chunk)
        upper = mm(second, up[:, cols]) + biases[:, cols]
        phi = 0.5 + 0.5 * lax.erf(upper * (0.5**0.5))
        hidden_out[:, cols] = (upper * phi).astype(BF16)
        slope = phi + upper * (jnp.exp(-0.5 * upper * upper) * 0.3989422804014327)
        back = (mm_nt(grad, down[cols, :]) * slope).astype(BF16)
        upper_out[:, cols] = back
        total = jnp.sum(back.astype(F32), 0, keepdims=True)
        for at in range(start, start + chunk, 256):
            row, place = divmod(at, width)
            small_out[row : row + 1, place : place + 256] = total[:, at - start : at - start + 256]
        norm = norm + mm_nt(back, up[:, cols])
    norm_out[...] = norm
    small_out[4:5, :] = jnp.sum(grad.astype(F32), 0, keepdims=True)


def backward_body(mine, other, middle, qkv, logs, seq, dy, gain, out_weight, weight, *refs):
    (*before, grad_out, attn_out, back, part_out, small_out, cross_out) = refs
    before = before[0] if before else None
    rows, width = middle.shape
    inner = out_weight.shape[0]
    hat, rate = normed(middle[...])
    total = mine[...] + other[...]
    grad = dy[...].astype(F32) + norm_back(total, hat, rate, line(gain))
    grad_out[...] = grad
    attn = grad.astype(BF16)
    attn_out[...] = attn
    small_out[...] = jnp.zeros_like(small_out)
    small_out[2:3, :] = jnp.sum(total * hat, 0, keepdims=True)
    small_out[3:4, :] = jnp.sum(total, 0, keepdims=True)
    small_out[5:6, :] = jnp.sum(attn.astype(F32), 0, keepdims=True)
    mixed = mm_nt(attn, out_weight[...]).astype(BF16)
    masks = side_masks()
    lane = lax.broadcasted_iota(jnp.int32, (rows, PAIR), 1)
    scale = HEAD_DIM**-0.5
    for pair in range(inner // PAIR):
        cols = slice(pair * PAIR, (pair + 1) * PAIR)
        q = qkv[:, cols]
        k = qkv[:, inner + pair * PAIR : inner + (pair + 1) * PAIR]
        v = qkv[:, 2 * inner + pair * PAIR : 2 * inner + (pair + 1) * PAIR]
        dm = mixed[:, cols]
        q_t = q.astype(F32).T.astype(BF16)
        dm_t = dm.astype(F32).T.astype(BF16)
        dq, dk, dv = [], [], []
        for side in range(2):
            half = slice(side * HEAD_DIM, (side + 1) * HEAD_DIM)
            head = 2 * pair + side
            scores = mm_nt(q * masks[side], k) * scale
            probs = jnp.exp(scores - logs[:, head : head + 1])
            dv.append(mm(dm_t[half, :], probs.astype(BF16)))
            prob_grad = mm_nt(dm * masks[side], v)
            score = probs * (prob_grad - jnp.sum(prob_grad * probs, -1, keepdims=True))
            score = score.astype(BF16)
            dq.append(mm(score, k))
            dk.append(mm(q_t[half, :], score))
        parts = (
            jnp.where(lane < HEAD_DIM, dq[0], dq[1]) * scale,
            (jnp.concatenate(dk, 0) * scale).T,
            jnp.concatenate(dv, 0).T,
        )
        for j, value in enumerate(parts):
            start = j * inner + pair * PAIR
            back[:, start : start + PAIR] = value.astype(BF16)
    part = mm_nt(back[:, 0:inner], weight[0])
    for j in range(1, 3):
        part = part + mm_nt(back[:, j * inner : (j + 1) * inner], weight[j])
    part_out[...] = part
    first_hat, _ = normed(seq[...])
    cross_out[...] = jnp.zeros_like(cross_out) if before is None else before[...]
    cross_out[6:7, 0:width] += jnp.sum(part * first_hat, 0, keepdims=True)
    cross_out[7:8, 0:width] += jnp.sum(part, 0, keepdims=True)


def branch_body(*refs):
    (*hiddens, down, part_out) = refs
    rows, size = hiddens[0].shape[0], part_out.shape[0] // len(hiddens)
    for image, hidden in enumerate(hiddens):
        part_out[(image + 1) * size - 8 : (image + 1) * size, :] = jnp.zeros((8, part_out.shape[1]), F32)
        part_out[image * size : image * size + rows, :] = mm(hidden[...], down[...])


def output_body(images, down_mine, down_other, bias, *refs):
    middles, out = refs[:images], refs[images]
    rows, size = middles[0].shape[0], down_mine.shape[0] // images
    for image in range(images):
        own = slice(image * size, image * size + rows)
        branch = down_mine[own, :] + down_other[own, :] + line(bias)
        out[image] = (middles[image][...] + branch).astype(BF16)


def input_body(gain, seq, mine, other, grad, out):
    hat, rate = normed(seq[...])
    out[...] = grad[...] + norm_back(mine[...] + other[...], hat, rate, line(gain))


def grads_body(layout, order, chunk, smalls, ids, *refs):
    lefts, rights, at = [], [], 0
    for images, _ in layout:
        lefts.append(refs[at : at + images])
        rights.append(refs[at + images : at + 2 * images])
        at += 2 * images
    small_refs = refs[at : at + smalls]
    keep, send, turned, stacked, tail = refs[at + smalls :]
    width = lefts[0][0].shape[1]
    size, half = width // 16, width // 2
    main = lefts[0][0].shape[0] // 8 * 8
    spare = lefts[0][0].shape[0] - main
    step = pl.program_id(0)
    even = ids[0] == 0

    def turn(value, start):
        columns = value.astype(F32).T
        stop = start + value.shape[0]
        for place in range(8):
            source = 0
            for digit, bit in enumerate(order):
                source |= ((place >> (2 - digit)) & 1) << bit
            zero = columns[source * size : (source + 1) * size, :]
            one = columns[(source + 1) * size : (source + 2) * size, :]
            rows = slice(place * size, (place + 1) * size)
            turned[rows, start:stop] = jnp.where(even, zero, one).astype(BF16)
            rows = slice(half + place * size, half + (place + 1) * size)
            turned[rows, start:stop] = jnp.where(even, one, zero).astype(BF16)

    begin = 0
    for (images, steps), left, right in zip(layout, lefts, rights):
        @pl.when(step == begin)
        def _(left=left, images=images):
            tail[...] = jnp.zeros_like(tail)
            for i, ref in enumerate(left):
                turn(ref[0:main, :], i * main)
                tail[i * spare : (i + 1) * spare, 0:width] = ref[main:, :].astype(F32)
            turn(tail[:, 0:width], images * main)

        @pl.when((step >= begin) & (step < begin + steps))
        def _(right=right, images=images):
            tail[...] = jnp.zeros_like(tail)
            for i, ref in enumerate(right):
                stacked[i * main : (i + 1) * main, :] = ref[0:main, :].astype(BF16)
                tail[i * spare : (i + 1) * spare, 0:chunk] = ref[main:, :].astype(F32)
            stacked[images * main :, :] = tail[:, 0:chunk].astype(BF16)

        begin += steps
    total = mm(turned[...], stacked[...])
    keep[0:half, :] = total[0:half, :]
    send[0:half, :] = total[half:, :]
    if smalls:
        keep[half:, :] = jnp.zeros_like(keep[half:, :])
        send[half:, :] = jnp.zeros_like(send[half:, :])
        for place in range(width // chunk):
            @pl.when(step == place)
            def _(place=place):
                cols = slice(place * chunk, (place + 1) * chunk)
                small = small_refs[0][:, cols]
                for ref in small_refs[1:]:
                    small = small + ref[:, cols]
                keep[half:, :] = small
                send[half:, :] = small


def fold_body(size, bit, ids, kept, got, *refs):
    *cross, keep, send = refs
    own = pl.ds(pl.multiple_of(ids[bit] * size, 8), size)
    away = pl.ds(pl.multiple_of((1 - ids[bit]) * size, 8), size)
    send[0:size, :] = kept[away, :] + got[away, :]
    keep[0:size, :] = kept[own, :] + got[own, :]
    if keep.shape[0] > size:
        small = kept[2 * size :, :] + got[2 * size :, :]
        if cross:
            small = small + (cross[0][...] + cross[1][...])
        send[size:, :] = small
        keep[size:, :] = small


def last_body(size, kept, got, out, *small):
    out[...] = kept[0:size, :] + got[0:size, :]
    for ref in small:
        ref[...] = kept[size:, :] + got[size:, :]


class WeightSum:
    def __init__(self, chain, ids, dp, name, order, chunk):
        self.chain, self.ids, self.dp, self.name, self.order, self.chunk = chain, ids, dp, name, order, chunk
        self.plain = not folded(dp)

    def start(self, sets, small=()):
        width = sets[0][0][0].shape[1]
        self.columns = columns = sum(rights[0].shape[1] for _, rights in sets)
        self.size = width // self.dp
        self.extra = 8 if small else 0
        if self.plain:
            products = [
                sum(mm_tn(left, right.astype(BF16)) for left, right in zip(*pair)) for pair in sets
            ]
            self.full = jnp.concatenate(products, 1)
            self.part = sum(small)
            return
        chunk, args, specs, layout, begin = self.chunk, [], [], [], 0
        for lefts, rights in sets:
            steps = rights[0].shape[1] // chunk
            args += [*lefts, *rights]
            specs += [whole(v) for v in lefts]
            for v in rights:
                block = lambda j, begin=begin, steps=steps: (0, jnp.clip(j - begin, 0, steps - 1))
                specs.append(pl.BlockSpec((v.shape[0], chunk), block))
            layout.append((len(lefts), steps))
            begin += steps
        images, rows = len(sets[0][0]), sets[0][0][0].shape[0]
        spare = 8 * pl.cdiv(images * (rows % 8), 8)
        depth = images * (rows // 8 * 8) + spare
        self.rows = width // 2
        dims = (self.rows + self.extra, columns)
        block = pl.BlockSpec((self.rows + self.extra, chunk), lambda j: (0, j))
        self.keep, send = self.chain.call(
            partial(grads_body, layout, self.order, chunk, len(small)), [self.ids, *args, *small],
            [scalars(), *specs] + [whole(v) for v in small], [far(dims), far(dims)], 32,
            f"{self.name}_grads", grid=begin, out_specs=[block, block],
            scratch=[
                pltpu.VMEM((width, depth), BF16),
                pltpu.VMEM((depth, chunk), BF16),
                pltpu.VMEM((spare, max(width, chunk)), F32),
            ],
            deep=range(1, 1 + len(args)),
        )
        (self.got,) = self.chain.at_once(
            self.ids, lambda v: (lax.ppermute(v, "dp", flips(self.dp, 0)),), send
        )
        self.at = 0

    def fold(self, *cross):
        if self.plain:
            return
        bit = self.order[self.at]
        self.at += 1
        self.rows //= 2
        args = [self.ids, self.keep, self.got, *cross]
        out = shape((self.rows + self.extra, self.columns))
        if self.at == 1:
            block = lambda v: pl.BlockSpec((v.shape[0], 512), lambda j: (0, j))
            specs = [block(v) for v in args[1:]]
            more = dict(grid=self.columns // 512, out_specs=[block(out)] * 2, deep=range(1, len(args)))
        else:
            specs, more = [whole(v) for v in args[1:]], {}
        self.keep, send = self.chain.call(
            partial(fold_body, self.rows, bit), args, [scalars(), *specs],
            [far(out.shape), out] if self.at == 1 else [out, out], 16, f"{self.name}_fold{bit}", **more,
        )
        self.got = lax.ppermute(send, "dp", flips(self.dp, bit))

    def finish(self):
        if self.plain:
            return lax.psum_scatter(self.full, "dp", scatter_dimension=0, tiled=True)
        outs = [shape((self.size, self.columns))]
        if self.extra:
            outs.append(shape((self.extra, self.columns)))
        got = self.chain.call(
            partial(last_body, self.size), [self.keep, self.got],
            [whole(self.keep), whole(self.got)], outs, 16, f"{self.name}_last",
        )
        if self.extra:
            self.small = got[1]
        return got[0]


def folded(dp):
    return dp == 16


def flips(dp, bit):
    return [(i, i ^ (1 << bit)) for i in range(dp)]


def per_device(
    dp,
    patches,
    extra_tokens,
    visible,
    qkv_weight,
    out_weight,
    out_bias,
    up_weight,
    up_bias,
    down_weight,
    down_bias,
    first_gain,
    first_shift,
    second_gain,
    second_shift,
    cotangent,
):
    images, _, width = patches.shape
    rows = visible.shape[1] + extra_tokens.shape[1]
    inner = qkv_weight.shape[2]
    hidden_width = up_weight.shape[1]
    place = lax.axis_index("dp")
    core = place % 2
    ids = jnp.stack([core] + [(place >> bit) & 1 for bit in (1, 2, 3)] + [lax.axis_index("mp")])
    ids = lax.optimization_barrier(ids.astype(jnp.int32))
    across = lambda v: lax.ppermute(v, "mp", SWAP)

    core_swap = lambda v: (lax.ppermute(v, "dp", flips(dp, 0)),)
    chain = Chain()

    quarter = inner // 2
    piece = lax.dynamic_slice_in_dim(out_weight, core * quarter, quarter, 0).astype(F32)
    near = across(piece)

    every = range(images)
    args = [visible, patches, extra_tokens, qkv_weight, first_gain, first_shift]
    each = lambda dims: pl.BlockSpec((None, *dims[1:]), lambda j: (j,) + (0,) * (len(dims) - 1))
    stacks = [
        far((images, rows, width)), far((images, rows, width), BF16), far((images, rows, 3 * inner), BF16),
        far((images, rows, PAIR)),
    ]
    flat = [shape((rows, inner))] * images
    seqs, firsts, qkvs, logs, *mixeds = chain.call(
        partial(attend_body, images), args,
        [whole(visible), each(patches.shape)] + [whole(a) for a in args[2:]],
        stacks + flat, 40, "attend", grid=images,
        out_specs=[each(o.shape) for o in stacks] + [whole(o) for o in flat], deep=range(6),
    )
    mixed_others = [across(m) for m in mixeds]
    (distant,) = chain.at_once(ids, core_swap, near)
    (full,) = chain.call(
        join_body, [ids, out_weight, near, distant],
        [scalars(), whole(out_weight), whole(near), whole(distant)],
        [shape((2 * inner, width), BF16)], 16, "join",
    )

    middles, seconds, hiddens, uppers, norms, smalls, norm_others = [], [], [], [], [], [], []
    for b in every:
        args = [ids, seqs, cotangent, out_bias, second_gain, second_shift, up_bias,
                mixeds[b], mixed_others[b], full, up_weight, down_weight]
        got = chain.call(
            forward_body, args,
            [scalars(), one_of(seqs, b), one_of(cotangent, b)] + [whole(a) for a in args[3:]],
            [far((rows, width)), far((rows, width), BF16), far((rows, hidden_width), BF16),
             far((rows, hidden_width), BF16), shape((rows, width)), far((8, width))],
            44, f"forward{b}", deep=(1, 3, 4, 5, 6),
        )
        for kept, one in zip((middles, seconds, hiddens, uppers, norms, smalls), got):
            kept.append(one)
        norm_others.append(across(norms[b]))

    down_sum, up_sum, last_sum = (
        WeightSum(chain, ids, dp, *how)
        for how in (("down", (1, 2, 3), 512), ("up", (2, 3, 1), 512), ("last", (1, 2, 3), 384))
    )
    down_sum.start([([cotangent[b] for b in every], hiddens)])
    down_sum.fold()

    grads, attns, backs, firsts_part, crosses, part_others = [], [], [], [], [], []
    for b in every:
        args = [norms[b], norm_others[b], middles[b], qkvs, logs, seqs, cotangent, second_gain,
                out_weight, qkv_weight, *crosses[-1:]]
        specs = [whole(a) for a in args]
        for i in (3, 4, 5, 6):
            specs[i] = one_of(args[i], b)
        got = chain.call(
            backward_body, args, specs,
            [far((rows, width)), far((rows, width), BF16), far((rows, 3 * inner), BF16),
             shape((rows, width)), far((8, width)), shape((8, hidden_width))],
            44, f"backward{b}", deep=(2, 3, 4, 5, 7),
        )
        for kept, one in zip((grads, attns, backs, firsts_part, smalls, crosses), got):
            kept.append(one)
        if b < images - 1:
            part_others.append(across(firsts_part[b]))
        if b == 0:
            up_sum.start([(seconds, uppers)])
            up_sum.fold()
    last_sum.start(
        [(attns, mixeds), ([firsts[b] for b in every], backs)], [*smalls, crosses[-1][:, :width]]
    )
    down_sum.fold()
    pairs = [((d, m), (d ^ 1, m ^ 1)) for d in range(dp) for m in range(2)]
    corners = [(2 * p[0] + p[1], 2 * q[0] + q[1]) for p, q in pairs]
    cross = chain.at_once(
        ids, lambda v: (across(v), lax.ppermute(v, ("dp", "mp"), corners)), crosses[-1]
    )
    firsts_part[-1], chain.token = lax.optimization_barrier((firsts_part[-1], chain.token))
    part_others.append(across(firsts_part[-1]))

    def input_of(b):
        args = [first_gain, seqs, firsts_part[b], part_others[b], grads[b]]
        specs = [whole(a) for a in args]
        specs[1] = one_of(seqs, b)
        return chain.call(
            input_body, args, specs, [shape((rows, width))], 32, f"input{b}", deep=(0, 1, 4)
        )[0]

    input_grads = [input_of(b) for b in range(images - 1)]
    last_sum.fold(*cross)
    up_sum.fold()
    padded = images * 8 * pl.cdiv(rows, 8)
    (down_part,) = chain.call(
        branch_body, [*hiddens, down_weight], [whole(a) for a in (*hiddens, down_weight)],
        [shape((padded, width))], 32, "branch",
    )
    down_other = across(down_part)
    down_sum.fold()
    input_grads.append(input_of(images - 1))
    down_total = down_sum.finish()
    last_sum.fold()
    up_sum.fold()
    last_sum.fold()
    up_total = up_sum.finish()
    args = [down_part, down_other, down_bias, *middles]
    (output,) = chain.call(
        partial(output_body, images), args, [whole(a) for a in args],
        [shape((images, rows, width), BF16)], 32, "output", deep=(2,),
    )
    last_total = last_sum.finish()
    if last_sum.plain:
        last_sum.small = lax.psum(last_sum.part + across(crosses[-1][:, :width]), "dp")
    small = last_sum.small[:, :width]
    return (
        output,
        jnp.stack(input_grads),
        last_total[:, inner:].reshape(-1, 3, inner).transpose(1, 0, 2),
        last_total[:, :inner].T,
        small[5],
        up_total,
        small[0:2].reshape(-1),
        down_total.T,
        small[4],
        small[6],
        small[7],
        small[2],
        small[3],
    )


def solution(mesh):
    return jax.shard_map(
        partial(per_device, mesh.shape["dp"]),
        mesh=mesh,
        in_specs=(
            P("dp", None, None),
            P("dp", None, None),
            P("dp", None),
            P(None, None, "mp"),
            P("mp", None),
            P(),
            P(None, "mp"),
            P("mp"),
            P("mp", None),
            P(),
            P(),
            P(),
            P(),
            P(),
            P("dp", None, None),
        ),
        out_specs=(
            P("dp", None, None),
            P("dp", None, None),
            P(None, "dp", "mp"),
            P("mp", "dp"),
            P(),
            P("dp", "mp"),
            P("mp"),
            P("mp", "dp"),
            P(),
            P(),
            P(),
            P(),
            P(),
        ),
        check_vma=False,
    )
```

```python
from functools import partial

import jax
import jax.numpy as jnp
from jax import lax
from jax.experimental import pallas as pl
from jax.experimental.pallas import tpu as pltpu
from jax.sharding import PartitionSpec as P

HEAD_DIM = 64
PAIR = 2 * HEAD_DIM
F32 = jnp.float32
BF16 = jnp.bfloat16
MIB = 1 << 20
SWAP = ((0, 1), (1, 0))


def mm(a, b):
    return lax.dot_general(a, b, (((1,), (0,)), ((), ())), preferred_element_type=F32)


def mm_nt(a, b):
    return lax.dot_general(a, b, (((1,), (1,)), ((), ())), preferred_element_type=F32)


def mm_tn(a, b):
    return lax.dot_general(a, b, (((0,), (0,)), ((), ())), preferred_element_type=F32)


def normed(values):
    center = values - jnp.mean(values, -1, keepdims=True)
    rate = lax.rsqrt(jnp.mean(center * center, -1, keepdims=True) + 1e-06)
    return center * rate, rate


def norm_back(grad, hat, rate, gain):
    scaled = grad * gain
    return rate * (
        scaled
        - jnp.mean(scaled, -1, keepdims=True)
        - hat * jnp.mean(scaled * hat, -1, keepdims=True)
    )


def shape(dims, dtype=F32):
    return jax.ShapeDtypeStruct(tuple(dims), dtype)


def far(dims, dtype=F32):
    return pltpu.HBM(tuple(dims), dtype)


def whole(x):
    return pl.BlockSpec(x.shape, lambda i, *_: (0,) * len(x.shape))


def one_of(x, image):
    return pl.BlockSpec((None,) + x.shape[1:], lambda i, *_: (image,) + (0,) * (x.ndim - 1))


def scalars():
    return pl.BlockSpec(memory_space=pltpu.SMEM)


ANYWHERE = pl.BlockSpec(memory_space=pl.ANY)


def kernel(body, args, specs, outs, vmem, name, grid=1, out_specs=None, scratch=(), deep=(), scalar=0):
    args = [pltpu.with_memory_space_constraint(a, pltpu.HBM) if i in deep else a for i, a in enumerate(args)]
    return pl.pallas_call(
        body,
        out_shape=tuple(outs),
        grid_spec=pltpu.PrefetchScalarGridSpec(
            num_scalar_prefetch=scalar,
            grid=(grid,),
            in_specs=specs,
            out_specs=tuple(out_specs or [whole(o) for o in outs]),
            scratch_shapes=list(scratch),
        ),
        compiler_params=pltpu.CompilerParams(vmem_limit_bytes=vmem * MIB),
        cost_estimate=pl.CostEstimate(flops=1 << 31, bytes_accessed=1, transcendentals=0),
        name=name,
    )(*args)


class Chain:
    def __init__(self):
        self.token = jnp.zeros((8, 128), F32)

    def call(self, body, args, specs, outs, vmem, name, out_specs=None, **more):
        taken, given = len(args), len(outs)

        def without_tokens(*refs):
            return body(*refs[:taken], *refs[taken + 1 : taken + 1 + given], *refs[taken + 2 + given :])

        *got, self.token = kernel(
            without_tokens, [*args, self.token], [*specs, ANYWHERE], [*outs, shape((8, 128))], vmem, name,
            out_specs=[*(out_specs or [whole(o) for o in outs]), ANYWHERE], **more,
        )
        return got

    def hold(self, value):
        value, self.token = lax.optimization_barrier((value, self.token))
        return value

    def at_once(self, ids, moves, *values):
        outs = jax.eval_shape(moves, *values)
        moved = lambda token, *vs: (token, *moves(*vs))
        never = lambda token, *vs: (token, *(jnp.zeros(o.shape, o.dtype) for o in outs))
        self.token, *got = lax.cond(ids[0] >= 0, moved, never, self.token, *values)
        return got


def line(vector):
    return vector[...].reshape(1, -1)


def side_masks():
    lane = lax.broadcasted_iota(jnp.int32, (1, PAIR), 1)
    low = jnp.where(lane < HEAD_DIM, 1.0, 0.0)
    return low.astype(BF16), (1.0 - low).astype(BF16)


def attend_body(images, pick, patch, extra, weight, gain, shift, *refs):
    seq_out, first_out, qkv_out, log_out, *mixed_outs = refs
    rows, width = seq_out.shape
    inner = mixed_outs[0].shape[1]
    image = pl.program_id(0)
    extras, picks = extra.shape[1], pick.shape[1]
    spread = jnp.broadcast_to(pick[pl.ds(image, 1), :].astype(F32), (128, picks))
    column = spread.T[:, 0:1].astype(jnp.int32)
    hot = lax.broadcasted_iota(jnp.int32, (picks, patch.shape[0]), 1) == column
    seq_out[extras:, :] = mm(jnp.where(hot, 1.0, 0.0).astype(BF16), patch[...])
    seq_out[0:extras, :] = extra[image].astype(F32)
    hat, _ = normed(seq_out[...])
    first = (hat * line(gain) + line(shift)).astype(BF16)
    first_out[...] = first
    for j in range(3):
        qkv_out[:, j * inner : (j + 1) * inner] = mm(first, weight[j]).astype(BF16)
    masks = side_masks()
    lane = lax.broadcasted_iota(jnp.int32, (rows, PAIR), 1)
    logs = jnp.zeros((rows, PAIR), F32)
    for pair in range(inner // PAIR):
        q = qkv_out[:, pair * PAIR : (pair + 1) * PAIR]
        k = qkv_out[:, inner + pair * PAIR : inner + (pair + 1) * PAIR]
        v = qkv_out[:, 2 * inner + pair * PAIR : 2 * inner + (pair + 1) * PAIR]
        sides = []
        for side in range(2):
            scores = mm_nt(q * masks[side], k) * (HEAD_DIM**-0.5)
            top = jnp.max(scores, -1, keepdims=True)
            expo = jnp.exp(scores - top)
            total = jnp.sum(expo, -1, keepdims=True)
            sides.append(mm((expo / total).astype(BF16), v))
            logs = jnp.where(lane == 2 * pair + side, top + jnp.log(total), logs)
        mixed = jnp.where(lane < HEAD_DIM, sides[0], sides[1]).astype(BF16).astype(F32)
        for b, out in enumerate(mixed_outs):
            @pl.when(image == b)
            def _(out=out, mixed=mixed, pair=pair):
                out[:, pair * PAIR : (pair + 1) * PAIR] = mixed
    log_out[...] = logs


def join_body(ids, mine, near, far, full_out):
    half = mine.shape[0]
    part = near.shape[0]
    mp = ids[4]
    core = ids[0]
    own = pl.multiple_of(mp * half, part)
    other = pl.multiple_of((1 - mp) * half, part)
    full_out[pl.ds(own, half), :] = mine[...]
    full_out[pl.ds(pl.multiple_of(other + core * part, part), part), :] = near[...].astype(BF16)
    full_out[pl.ds(pl.multiple_of(other + (1 - core) * part, part), part), :] = far[...].astype(BF16)


def forward_body(
    ids, seq, dy, out_bias, gain, shift, up_bias, mine, other, full, up, down,
    middle_out, second_out, hidden_out, upper_out, norm_out, small_out,
):
    rows, width = seq.shape
    inner = mine.shape[1]
    first_half = ids[4] == 0
    left = jnp.where(first_half, mine[...], other[...]).astype(BF16)
    right = jnp.where(first_half, other[...], mine[...]).astype(BF16)
    attn = mm(left, full[0:inner, :]) + mm(right, full[inner:, :]) + line(out_bias)
    middle = seq[...] + attn
    middle_out[...] = middle
    hat, _ = normed(middle)
    second = (hat * line(gain) + line(shift)).astype(BF16)
    second_out[...] = second
    grad = dy[...].astype(BF16)
    small_out[...] = jnp.zeros_like(small_out)
    chunk = 512
    biases = line(up_bias)
    norm = jnp.zeros((rows, width), F32)
    for start in range(0, up.shape[1], chunk):
        cols = slice(start, start + chunk)
        upper = mm(second, up[:, cols]) + biases[:, cols]
        phi = 0.5 + 0.5 * lax.erf(upper * (0.5**0.5))
        hidden_out[:, cols] = (upper * phi).astype(BF16)
        slope = phi + upper * (jnp.exp(-0.5 * upper * upper) * 0.3989422804014327)
        back = (mm_nt(grad, down[cols, :]) * slope).astype(BF16)
        upper_out[:, cols] = back
        total = jnp.sum(back.astype(F32), 0, keepdims=True)
        for at in range(start, start + chunk, 256):
            row, place = divmod(at, width)
            small_out[row : row + 1, place : place + 256] = total[:, at - start : at - start + 256]
        norm = norm + mm_nt(back, up[:, cols])
    norm_out[...] = norm
    small_out[4:5, :] = jnp.sum(grad.astype(F32), 0, keepdims=True)


def backward_body(mine, other, middle, qkv, logs, seq, dy, gain, out_weight, weight, *refs):
    (*before, grad_out, attn_out, back, part_out, small_out, cross_out) = refs
    before = before[0] if before else None
    rows, width = middle.shape
    inner = out_weight.shape[0]
    hat, rate = normed(middle[...])
    total = mine[...] + other[...]
    grad = dy[...].astype(F32) + norm_back(total, hat, rate, line(gain))
    grad_out[...] = grad
    attn = grad.astype(BF16)
    attn_out[...] = attn
    small_out[...] = jnp.zeros_like(small_out)
    small_out[2:3, :] = jnp.sum(total * hat, 0, keepdims=True)
    small_out[3:4, :] = jnp.sum(total, 0, keepdims=True)
    small_out[5:6, :] = jnp.sum(attn.astype(F32), 0, keepdims=True)
    mixed = mm_nt(attn, out_weight[...]).astype(BF16)
    masks = side_masks()
    lane = lax.broadcasted_iota(jnp.int32, (rows, PAIR), 1)
    scale = HEAD_DIM**-0.5
    for pair in range(inner // PAIR):
        cols = slice(pair * PAIR, (pair + 1) * PAIR)
        q = qkv[:, cols]
        k = qkv[:, inner + pair * PAIR : inner + (pair + 1) * PAIR]
        v = qkv[:, 2 * inner + pair * PAIR : 2 * inner + (pair + 1) * PAIR]
        dm = mixed[:, cols]
        q_t = q.astype(F32).T.astype(BF16)
        dm_t = dm.astype(F32).T.astype(BF16)
        dq, dk, dv = [], [], []
        for side in range(2):
            half = slice(side * HEAD_DIM, (side + 1) * HEAD_DIM)
            head = 2 * pair + side
            scores = mm_nt(q * masks[side], k) * scale
            probs = jnp.exp(scores - logs[:, head : head + 1])
            dv.append(mm(dm_t[half, :], probs.astype(BF16)))
            prob_grad = mm_nt(dm * masks[side], v)
            score = probs * (prob_grad - jnp.sum(prob_grad * probs, -1, keepdims=True))
            score = score.astype(BF16)
            dq.append(mm(score, k))
            dk.append(mm(q_t[half, :], score))
        parts = (
            jnp.where(lane < HEAD_DIM, dq[0], dq[1]) * scale,
            (jnp.concatenate(dk, 0) * scale).T,
            jnp.concatenate(dv, 0).T,
        )
        for j, value in enumerate(parts):
            start = j * inner + pair * PAIR
            back[:, start : start + PAIR] = value.astype(BF16)
    part = mm_nt(back[:, 0:inner], weight[0])
    for j in range(1, 3):
        part = part + mm_nt(back[:, j * inner : (j + 1) * inner], weight[j])
    part_out[...] = part
    first_hat, _ = normed(seq[...])
    cross_out[...] = jnp.zeros_like(cross_out) if before is None else before[...]
    cross_out[6:7, 0:width] += jnp.sum(part * first_hat, 0, keepdims=True)
    cross_out[7:8, 0:width] += jnp.sum(part, 0, keepdims=True)


def branch_body(*refs):
    (*hiddens, down, part_out) = refs
    rows, size = hiddens[0].shape[0], part_out.shape[0] // len(hiddens)
    for image, hidden in enumerate(hiddens):
        part_out[(image + 1) * size - 8 : (image + 1) * size, :] = jnp.zeros((8, part_out.shape[1]), F32)
        part_out[image * size : image * size + rows, :] = mm(hidden[...], down[...])


def output_body(images, down_mine, down_other, bias, *refs):
    middles, out = refs[:images], refs[images]
    rows, size = middles[0].shape[0], down_mine.shape[0] // images
    for image in range(images):
        own = slice(image * size, image * size + rows)
        branch = down_mine[own, :] + down_other[own, :] + line(bias)
        out[image] = (middles[image][...] + branch).astype(BF16)


def input_body(gain, seq, mine, other, grad, out):
    hat, rate = normed(seq[...])
    out[...] = grad[...] + norm_back(mine[...] + other[...], hat, rate, line(gain))


def grads_body(layout, order, chunk, smalls, ids, *refs):
    lefts, rights, at = [], [], 0
    for images, _ in layout:
        lefts.append(refs[at : at + images])
        rights.append(refs[at + images : at + 2 * images])
        at += 2 * images
    small_refs = refs[at : at + smalls]
    keep, send, turned, stacked, tail = refs[at + smalls :]
    width = lefts[0][0].shape[1]
    size, half = width // 16, width // 2
    main = lefts[0][0].shape[0] // 8 * 8
    spare = lefts[0][0].shape[0] - main
    step = pl.program_id(0)
    even = ids[0] == 0

    def turn(value, start):
        columns = value.astype(F32).T
        stop = start + value.shape[0]
        for place in range(8):
            source = 0
            for digit, bit in enumerate(order):
                source |= ((place >> (2 - digit)) & 1) << bit
            zero = columns[source * size : (source + 1) * size, :]
            one = columns[(source + 1) * size : (source + 2) * size, :]
            rows = slice(place * size, (place + 1) * size)
            turned[rows, start:stop] = jnp.where(even, zero, one).astype(BF16)
            rows = slice(half + place * size, half + (place + 1) * size)
            turned[rows, start:stop] = jnp.where(even, one, zero).astype(BF16)

    begin = 0
    for (images, steps), left, right in zip(layout, lefts, rights):
        @pl.when(step == begin)
        def _(left=left, images=images):
            tail[...] = jnp.zeros_like(tail)
            for i, ref in enumerate(left):
                turn(ref[0:main, :], i * main)
                tail[i * spare : (i + 1) * spare, 0:width] = ref[main:, :].astype(F32)
            turn(tail[:, 0:width], images * main)

        @pl.when((step >= begin) & (step < begin + steps))
        def _(right=right, images=images):
            tail[...] = jnp.zeros_like(tail)
            for i, ref in enumerate(right):
                stacked[i * main : (i + 1) * main, :] = ref[0:main, :].astype(BF16)
                tail[i * spare : (i + 1) * spare, 0:chunk] = ref[main:, :].astype(F32)
            stacked[images * main :, :] = tail[:, 0:chunk].astype(BF16)

        begin += steps
    total = mm(turned[...], stacked[...])
    keep[0:half, :] = total[0:half, :]
    send[0:half, :] = total[half:, :]
    if smalls:
        keep[half:, :] = jnp.zeros_like(keep[half:, :])
        send[half:, :] = jnp.zeros_like(send[half:, :])
        for place in range(width // chunk):
            @pl.when(step == place)
            def _(place=place):
                cols = slice(place * chunk, (place + 1) * chunk)
                small = small_refs[0][:, cols]
                for ref in small_refs[1:]:
                    small = small + ref[:, cols]
                keep[half:, :] = small
                send[half:, :] = small


def sum_body(count, smalls, ids, *refs):
    blocks, small_refs, outs = refs[:count], refs[count : count + smalls], refs[count + smalls :]
    size = blocks[0].shape[0]
    total = blocks[0][...] + blocks[1][...]
    for ref in blocks[2:]:
        total = total + ref[...]
    outs[0][0:size, :] = total
    if smalls:
        kept, got, near, far_one, *rest = (ref[...] for ref in small_refs)
        small = (kept + got) + (near + far_one)
        for one in rest:
            small = small + one
        if len(outs) == 1:
            outs[0][size:, :] = small
        else:
            outs[1][...] = small


class Part:
    def __init__(self, chain, ids, dp, name, order, arrays, columns, at, cross):
        self.chain, self.ids, self.dp, self.name, self.order = chain, ids, dp, name, order
        self.columns, self.at, self.cross = columns, at, cross
        self.arrays = [(array, 0) for array in arrays]
        self.half = arrays[0].shape[0] // 8 * 8 if cross is None else arrays[0].shape[0] - 8
        self.steps = 0

    def add(self, digits, flip, outs, name):
        size = self.half >> digits
        args, specs = [self.ids], []

        def rows_of(level):
            def index(j, ids):
                at = 0
                for digit in range(level, digits):
                    bit = ids[self.order[digit]]
                    at = 2 * at + ((1 - bit) if flip and digit == digits - 1 else bit)
                return (at, self.at if level == 0 else 0)
            return index

        for array, level in self.arrays:
            args.append(array)
            specs.append(pl.BlockSpec((size, self.columns), rows_of(level)))
        smalls = 0
        if self.cross is not None:
            small = [(array, (self.half >> level) // 8) for array, level in self.arrays]
            small[2:2] = [(array, 0) for array in self.cross]
            for array, row in small:
                args.append(array)
                specs.append(pl.BlockSpec((8, self.columns), lambda j, ids, row=row: (row, 0)))
            smalls = len(small)
        return self.chain.call(
            partial(sum_body, len(self.arrays), smalls), args, specs, outs, 16, f"{self.name}_{name}",
            scalar=1, deep=(1, 2) if digits == 1 else (1,),
        )

    def step(self):
        if self.arrays is None:
            return
        bit = self.order[self.steps]
        self.steps += 1
        extra = 0 if self.cross is None else 8
        out = shape(((self.half >> self.steps) + extra, self.columns))
        (send,) = self.add(self.steps, True, [out], f"step{bit}")
        self.arrays.append((lax.ppermute(send, "dp", flips(self.dp, bit)), self.steps))

    def finish(self):
        outs = [shape((self.half >> self.steps, self.columns))]
        if self.cross is not None:
            outs.append(shape((8, self.columns)))
        return self.add(self.steps, False, outs, "last")


class Plain:
    def __init__(self, full, small):
        self.full, self.small = full, small

    def step(self):
        pass

    def finish(self):
        total = lax.psum_scatter(self.full, "dp", scatter_dimension=0, tiled=True)
        return [total] if self.small is None else [total, lax.psum(self.small, "dp")]


def weight_sum(chain, ids, dp, name, chunk, sets, smalls=(), cross=None, beside=None, parts=1, order=(1, 2, 3)):
    width = sets[0][0][0].shape[1]
    columns = sum(rights[0].shape[1] for _, rights in sets)
    size = columns // parts
    if not folded(dp):
        products = [sum(mm_tn(left, right.astype(BF16)) for left, right in zip(*pair)) for pair in sets]
        full = jnp.concatenate(products, 1)
        small = sum(smalls) + cross if smalls else None
        pieces = [
            Plain(full[:, i * size : (i + 1) * size], small if i == 0 else None) for i in range(parts)
        ]
        return pieces, beside() if beside else None
    args, specs, layout, begin = [], [], [], 0
    for lefts, rights in sets:
        steps = rights[0].shape[1] // chunk
        args += [*lefts, *rights]
        specs += [whole(v) for v in lefts]
        for v in rights:
            block = lambda j, begin=begin, steps=steps: (0, jnp.clip(j - begin, 0, steps - 1))
            specs.append(pl.BlockSpec((v.shape[0], chunk), block))
        layout.append((len(lefts), steps))
        begin += steps
    images, rows = len(sets[0][0]), sets[0][0][0].shape[0]
    spare = 8 * pl.cdiv(images * (rows % 8), 8)
    depth = images * (rows // 8 * 8) + spare
    dims = (width // 2 + (8 if smalls else 0), columns)
    block = pl.BlockSpec((dims[0], chunk), lambda j: (0, j))
    keep, send = chain.call(
        partial(grads_body, layout, order, chunk, len(smalls)), [ids, *args, *smalls],
        [scalars(), *specs] + [whole(v) for v in smalls], [far(dims), far(dims)], 32,
        f"{name}_grads", grid=begin, out_specs=[block, block],
        scratch=[
            pltpu.VMEM((width, depth), BF16),
            pltpu.VMEM((depth, chunk), BF16),
            pltpu.VMEM((spare, max(width, chunk)), F32),
        ],
        deep=range(1, 1 + len(args)),
    )
    swap = lambda v: lax.ppermute(v, "dp", flips(dp, 0))
    if cross is not None:
        got, distant = chain.at_once(ids, lambda v, c: (swap(v), swap(c)), send, cross)
        crosses, done = (cross, distant), None
    elif beside:
        got, done = chain.at_once(ids, lambda v: (swap(v), beside()), send)
        crosses = None
    else:
        (got,) = chain.at_once(ids, lambda v: (swap(v),), send)
        crosses, done = None, None
    pieces = [
        Part(chain, ids, dp, f"{name}{i}", order, [keep, got], size, i, crosses if i == 0 else None)
        for i in range(parts)
    ]
    for piece in pieces:
        piece.half = width // 2
    return pieces, done


def folded(dp):
    return dp == 16


def flips(dp, bit):
    return [(i, i ^ (1 << bit)) for i in range(dp)]


def per_device(
    dp,
    patches,
    extra_tokens,
    visible,
    qkv_weight,
    out_weight,
    out_bias,
    up_weight,
    up_bias,
    down_weight,
    down_bias,
    first_gain,
    first_shift,
    second_gain,
    second_shift,
    cotangent,
):
    images, _, width = patches.shape
    rows = visible.shape[1] + extra_tokens.shape[1]
    inner = qkv_weight.shape[2]
    hidden_width = up_weight.shape[1]
    place = lax.axis_index("dp")
    core = place % 2
    ids = jnp.stack([core] + [(place >> bit) & 1 for bit in (1, 2, 3)] + [lax.axis_index("mp")])
    ids = lax.optimization_barrier(ids.astype(jnp.int32))
    across = lambda v: lax.ppermute(v, "mp", SWAP)

    core_swap = lambda v: (lax.ppermute(v, "dp", flips(dp, 0)),)
    chain = Chain()

    quarter = inner // 2
    piece = lax.dynamic_slice_in_dim(out_weight, core * quarter, quarter, 0).astype(F32)
    near = across(piece)

    every = range(images)
    args = [visible, patches, extra_tokens, qkv_weight, first_gain, first_shift]
    each = lambda dims: pl.BlockSpec((None, *dims[1:]), lambda j: (j,) + (0,) * (len(dims) - 1))
    stacks = [
        far((images, rows, width)), far((images, rows, width), BF16), far((images, rows, 3 * inner), BF16),
        far((images, rows, PAIR)),
    ]
    flat = [shape((rows, inner))] * images
    seqs, firsts, qkvs, logs, *mixeds = chain.call(
        partial(attend_body, images), args,
        [whole(visible), each(patches.shape)] + [whole(a) for a in args[2:]],
        stacks + flat, 40, "attend", grid=images,
        out_specs=[each(o.shape) for o in stacks] + [whole(o) for o in flat], deep=range(6),
    )
    mixed_others = [across(m) for m in mixeds]
    (distant,) = chain.at_once(ids, core_swap, near)
    (full,) = chain.call(
        join_body, [ids, out_weight, near, distant],
        [scalars(), whole(out_weight), whole(near), whole(distant)],
        [shape((2 * inner, width), BF16)], 16, "join",
    )

    middles, seconds, hiddens, uppers, norms, smalls, norm_others = [], [], [], [], [], [], []
    for b in every:
        args = [ids, seqs, cotangent, out_bias, second_gain, second_shift, up_bias,
                mixeds[b], mixed_others[b], full, up_weight, down_weight]
        got = chain.call(
            forward_body, args,
            [scalars(), one_of(seqs, b), one_of(cotangent, b)] + [whole(a) for a in args[3:]],
            [far((rows, width)), far((rows, width), BF16), far((rows, hidden_width), BF16),
             far((rows, hidden_width), BF16), shape((rows, width)), far((8, width))],
            44, f"forward{b}", deep=(1, 3, 4, 5, 6),
        )
        for kept, one in zip((middles, seconds, hiddens, uppers, norms, smalls), got):
            kept.append(one)
        norm_others.append(across(norms[b]))

    padded = images * 8 * pl.cdiv(rows, 8)

    def branch():
        return kernel(
            branch_body, [*hiddens, down_weight], [whole(a) for a in (*hiddens, down_weight)],
            [shape((padded, width))], 32, "branch",
        )[0]

    dys = [cotangent[b] for b in every]
    (down_sum,), down_part = weight_sum(chain, ids, dp, "down", 512, [(dys, hiddens)], beside=branch)
    down_sum.step()

    grads, attns, backs, firsts_part, crosses, part_others = [], [], [], [], [], []
    for b in every:
        args = [norms[b], norm_others[b], middles[b], qkvs, logs, seqs, cotangent, second_gain,
                out_weight, qkv_weight, *crosses[-1:]]
        specs = [whole(a) for a in args]
        for i in (3, 4, 5, 6):
            specs[i] = one_of(args[i], b)
        got = chain.call(
            backward_body, args, specs,
            [far((rows, width)), far((rows, width), BF16), far((rows, 3 * inner), BF16),
             shape((rows, width)), far((8, width)), shape((8, hidden_width))],
            44, f"backward{b}", deep=(2, 3, 4, 5, 7),
        )
        for kept, one in zip((grads, attns, backs, firsts_part, smalls, crosses), got):
            kept.append(one)
        if b == images - 1:
            cross = across(crosses[-1])
        part_others.append(across(firsts_part[b]))
        if b == 0:
            (up_sum,), _ = weight_sum(chain, ids, dp, "up", 512, [(seconds, uppers)])
            up_sum.step()
    part_others[0] = chain.hold(part_others[0])
    down_sum.step()
    down_part = chain.hold(down_part)
    down_other = across(down_part)
    sets = [(attns, mixeds), ([firsts[b] for b in every], backs)]
    (out_sum, qkv_sum), _ = weight_sum(
        chain, ids, dp, "last", 384, sets, [*smalls, crosses[-1][:, :width]],
        cross if folded(dp) else cross[:, :width], parts=2,
    )

    def input_of(b):
        args = [first_gain, seqs, firsts_part[b], part_others[b], grads[b]]
        specs = [whole(a) for a in args]
        specs[1] = one_of(seqs, b)
        return chain.call(
            input_body, args, specs, [shape((rows, width))], 32, f"input{b}", deep=(0, 1, 4)
        )[0]

    out_sum.step()
    qkv_sum.step()
    input_grads = [input_of(b) for b in range(images - 1)]
    down_sum.step()
    up_sum.step()
    input_grads.append(input_of(images - 1))
    (down_total,) = down_sum.finish()
    out_sum.step()
    up_sum.step()
    qkv_sum.step()
    out_sum.step()
    (up_total,) = up_sum.finish()
    qkv_sum.step()
    out_total, small = out_sum.finish()
    args = [down_part, down_other, down_bias, *middles]
    (output,) = chain.call(
        partial(output_body, images), args, [whole(a) for a in args],
        [shape((images, rows, width), BF16)], 32, "output", deep=(2,),
    )
    (qkv_total,) = qkv_sum.finish()
    small = small[:, :width]
    return (
        output,
        jnp.stack(input_grads),
        jnp.stack([out_total[:, inner:], qkv_total[:, :inner], qkv_total[:, inner:]]),
        out_total[:, :inner].T,
        small[5],
        up_total,
        small[0:2].reshape(-1),
        down_total.T,
        small[4],
        small[6],
        small[7],
        small[2],
        small[3],
    )


def solution(mesh):
    return jax.shard_map(
        partial(per_device, mesh.shape["dp"]),
        mesh=mesh,
        in_specs=(
            P("dp", None, None),
            P("dp", None, None),
            P("dp", None),
            P(None, None, "mp"),
            P("mp", None),
            P(),
            P(None, "mp"),
            P("mp"),
            P("mp", None),
            P(),
            P(),
            P(),
            P(),
            P(),
            P("dp", None, None),
        ),
        out_specs=(
            P("dp", None, None),
            P("dp", None, None),
            P(None, "dp", "mp"),
            P("mp", "dp"),
            P(),
            P("dp", "mp"),
            P("mp"),
            P("mp", "dp"),
            P(),
            P(),
            P(),
            P(),
            P(),
        ),
        check_vma=False,
    )
```

```python
from functools import partial

import jax
import jax.numpy as jnp
from jax import lax
from jax.experimental import pallas as pl
from jax.experimental.pallas import tpu as pltpu
from jax.sharding import PartitionSpec as P

HEAD_DIM = 64
PAIR = 2 * HEAD_DIM
F32 = jnp.float32
BF16 = jnp.bfloat16
MIB = 1 << 20
SWAP = ((0, 1), (1, 0))


def mm(a, b):
    return lax.dot_general(a, b, (((1,), (0,)), ((), ())), preferred_element_type=F32)


def mm_nt(a, b):
    return lax.dot_general(a, b, (((1,), (1,)), ((), ())), preferred_element_type=F32)


def mm_tn(a, b):
    return lax.dot_general(a, b, (((0,), (0,)), ((), ())), preferred_element_type=F32)


def normed(values):
    center = values - jnp.mean(values, -1, keepdims=True)
    rate = lax.rsqrt(jnp.mean(center * center, -1, keepdims=True) + 1e-06)
    return center * rate, rate


def norm_back(grad, hat, rate, gain):
    scaled = grad * gain
    return rate * (
        scaled
        - jnp.mean(scaled, -1, keepdims=True)
        - hat * jnp.mean(scaled * hat, -1, keepdims=True)
    )


def shape(dims, dtype=F32):
    return jax.ShapeDtypeStruct(tuple(dims), dtype)


def far(dims, dtype=F32):
    return pltpu.HBM(tuple(dims), dtype)


def whole(x):
    return pl.BlockSpec(x.shape, lambda i, *_: (0,) * len(x.shape))


def one_of(x, image):
    return pl.BlockSpec((None,) + x.shape[1:], lambda i, *_: (image,) + (0,) * (x.ndim - 1))


def scalars():
    return pl.BlockSpec(memory_space=pltpu.SMEM)


ANYWHERE = pl.BlockSpec(memory_space=pl.ANY)


def kernel(body, args, specs, outs, vmem, name, grid=1, out_specs=None, scratch=(), deep=(), scalar=0, cost=31):
    args = [pltpu.with_memory_space_constraint(a, pltpu.HBM) if i in deep else a for i, a in enumerate(args)]
    return pl.pallas_call(
        body,
        out_shape=tuple(outs),
        grid_spec=pltpu.PrefetchScalarGridSpec(
            num_scalar_prefetch=scalar,
            grid=(grid,),
            in_specs=specs,
            out_specs=tuple(out_specs or [whole(o) for o in outs]),
            scratch_shapes=list(scratch),
        ),
        compiler_params=pltpu.CompilerParams(vmem_limit_bytes=vmem * MIB),
        cost_estimate=pl.CostEstimate(flops=1 << cost, bytes_accessed=1, transcendentals=0),
        name=name,
    )(*args)


class Chain:
    def __init__(self):
        self.token = jnp.zeros((8, 128), F32)

    def call(self, body, args, specs, outs, vmem, name, out_specs=None, **more):
        taken, given = len(args), len(outs)

        def without_tokens(*refs):
            return body(*refs[:taken], *refs[taken + 1 : taken + 1 + given], *refs[taken + 2 + given :])

        *got, self.token = kernel(
            without_tokens, [*args, self.token], [*specs, ANYWHERE], [*outs, shape((8, 128))], vmem, name,
            out_specs=[*(out_specs or [whole(o) for o in outs]), ANYWHERE], **more,
        )
        return got

    def hold(self, value):
        value, self.token = lax.optimization_barrier((value, self.token))
        return value

    def at_once(self, ids, moves, *values):
        outs = jax.eval_shape(moves, *values)
        moved = lambda token, *vs: (token, *moves(*vs))
        never = lambda token, *vs: (token, *(jnp.zeros(o.shape, o.dtype) for o in outs))
        self.token, *got = lax.cond(ids[0] >= 0, moved, never, self.token, *values)
        return got


def line(vector):
    return vector[...].reshape(1, -1)


def side_masks(value=1.0):
    lane = lax.broadcasted_iota(jnp.int32, (1, PAIR), 1)
    low = jnp.where(lane < HEAD_DIM, value, 0.0)
    return low.astype(BF16), (value - low).astype(BF16)


def attend_body(images, pick, patch, extra, weight, gain, shift, *refs):
    seq_out, first_out, qkv_out, log_out, *mixed_outs = refs
    rows, width = seq_out.shape
    inner = mixed_outs[0].shape[1]
    image = pl.program_id(0)
    extras, picks = extra.shape[1], pick.shape[1]
    spread = jnp.broadcast_to(pick[pl.ds(image, 1), :].astype(F32), (128, picks))
    column = spread.T[:, 0:1].astype(jnp.int32)
    hot = lax.broadcasted_iota(jnp.int32, (picks, patch.shape[0]), 1) == column
    seq_out[extras:, :] = mm(jnp.where(hot, 1.0, 0.0).astype(BF16), patch[...])
    seq_out[0:extras, :] = extra[image].astype(F32)
    hat, _ = normed(seq_out[...])
    first = (hat * line(gain) + line(shift)).astype(BF16)
    first_out[...] = first
    for j in range(3):
        qkv_out[:, j * inner : (j + 1) * inner] = mm(first, weight[j]).astype(BF16)
    masks = side_masks(HEAD_DIM**-0.5)
    lane = lax.broadcasted_iota(jnp.int32, (rows, PAIR), 1)
    logs = jnp.zeros((rows, PAIR), F32)
    for pair in range(inner // PAIR):
        q = qkv_out[:, pair * PAIR : (pair + 1) * PAIR]
        k = qkv_out[:, inner + pair * PAIR : inner + (pair + 1) * PAIR]
        v = qkv_out[:, 2 * inner + pair * PAIR : 2 * inner + (pair + 1) * PAIR]
        sides = []
        for side in range(2):
            scores = mm_nt(q * masks[side], k)
            top = jnp.max(scores, -1, keepdims=True)
            expo = jnp.exp(scores - top)
            total = jnp.sum(expo, -1, keepdims=True)
            sides.append(mm((expo * (1.0 / total)).astype(BF16), v))
            logs = jnp.where(lane == 2 * pair + side, top + jnp.log(total), logs)
        mixed = jnp.where(lane < HEAD_DIM, sides[0], sides[1]).astype(BF16).astype(F32)
        for b, out in enumerate(mixed_outs):
            @pl.when(image == b)
            def _(out=out, mixed=mixed, pair=pair):
                out[:, pair * PAIR : (pair + 1) * PAIR] = mixed
    log_out[...] = logs


def join_body(ids, mine, near, far, full_out):
    half = mine.shape[0]
    part = near.shape[0]
    mp = ids[4]
    core = ids[0]
    own = pl.multiple_of(mp * half, part)
    other = pl.multiple_of((1 - mp) * half, part)
    full_out[pl.ds(own, half), :] = mine[...]
    full_out[pl.ds(pl.multiple_of(other + core * part, part), part), :] = near[...].astype(BF16)
    full_out[pl.ds(pl.multiple_of(other + (1 - core) * part, part), part), :] = far[...].astype(BF16)


def forward_body(
    ids, seq, dy, out_bias, gain, shift, up_bias, mine, other, full, up, down,
    middle_out, second_out, hidden_out, upper_out, norm_out, small_out,
):
    rows, width = seq.shape
    inner = mine.shape[1]
    first_half = ids[4] == 0
    left = jnp.where(first_half, mine[...], other[...]).astype(BF16)
    right = jnp.where(first_half, other[...], mine[...]).astype(BF16)
    attn = mm(left, full[0:inner, :]) + mm(right, full[inner:, :]) + line(out_bias)
    middle = seq[...] + attn
    middle_out[...] = middle
    hat, _ = normed(middle)
    second = (hat * line(gain) + line(shift)).astype(BF16)
    second_out[...] = second
    grad = dy[...].astype(BF16)
    small_out[...] = jnp.zeros_like(small_out)
    chunk = 512
    biases = line(up_bias)
    norm = jnp.zeros((rows, width), F32)
    for start in range(0, up.shape[1], chunk):
        cols = slice(start, start + chunk)
        upper = mm(second, up[:, cols]) + biases[:, cols]
        phi = 0.5 + 0.5 * lax.erf(upper * (0.5**0.5))
        hidden_out[:, cols] = (upper * phi).astype(BF16)
        slope = phi + upper * (jnp.exp(-0.5 * upper * upper) * 0.3989422804014327)
        back = (mm_nt(grad, down[cols, :]) * slope).astype(BF16)
        upper_out[:, cols] = back
        total = jnp.sum(back.astype(F32), 0, keepdims=True)
        for at in range(start, start + chunk, 256):
            row, place = divmod(at, width)
            small_out[row : row + 1, place : place + 256] = total[:, at - start : at - start + 256]
        norm = norm + mm_nt(back, up[:, cols])
    norm_out[...] = norm
    small_out[4:5, :] = jnp.sum(grad.astype(F32), 0, keepdims=True)


def backward_body(mine, other, middle, qkv, logs, seq, dy, gain, out_weight, weight, *refs):
    (*before, grad_out, attn_out, back, part_out, small_out, cross_out) = refs
    before = before[0] if before else None
    rows, width = middle.shape
    inner = out_weight.shape[0]
    hat, rate = normed(middle[...])
    total = mine[...] + other[...]
    grad = dy[...].astype(F32) + norm_back(total, hat, rate, line(gain))
    grad_out[...] = grad
    attn = grad.astype(BF16)
    attn_out[...] = attn
    small_out[...] = jnp.zeros_like(small_out)
    small_out[2:3, :] = jnp.sum(total * hat, 0, keepdims=True)
    small_out[3:4, :] = jnp.sum(total, 0, keepdims=True)
    small_out[5:6, :] = jnp.sum(attn.astype(F32), 0, keepdims=True)
    mixed = mm_nt(attn, out_weight[...]).astype(BF16)
    masks = side_masks()
    scaled = side_masks(HEAD_DIM**-0.5)
    lane = lax.broadcasted_iota(jnp.int32, (rows, PAIR), 1)
    scale = HEAD_DIM**-0.5
    for pair in range(inner // PAIR):
        cols = slice(pair * PAIR, (pair + 1) * PAIR)
        q = qkv[:, cols]
        k = qkv[:, inner + pair * PAIR : inner + (pair + 1) * PAIR]
        v = qkv[:, 2 * inner + pair * PAIR : 2 * inner + (pair + 1) * PAIR]
        dm = mixed[:, cols]
        q_t = q.astype(F32).T.astype(BF16)
        dm_t = dm.astype(F32).T.astype(BF16)
        dq, dk, dv = [], [], []
        for side in range(2):
            half = slice(side * HEAD_DIM, (side + 1) * HEAD_DIM)
            head = 2 * pair + side
            scores = mm_nt(q * scaled[side], k)
            probs = jnp.exp(scores - logs[:, head : head + 1])
            dv.append(mm(dm_t[half, :], probs.astype(BF16)))
            prob_grad = mm_nt(dm * masks[side], v)
            score = probs * (prob_grad - jnp.sum(prob_grad * probs, -1, keepdims=True))
            score = score.astype(BF16)
            dq.append(mm(score, k))
            dk.append(mm(q_t[half, :], score))
        parts = (
            jnp.where(lane < HEAD_DIM, dq[0], dq[1]) * scale,
            (jnp.concatenate(dk, 0) * scale).T,
            jnp.concatenate(dv, 0).T,
        )
        for j, value in enumerate(parts):
            start = j * inner + pair * PAIR
            back[:, start : start + PAIR] = value.astype(BF16)
    part = mm_nt(back[:, 0:inner], weight[0])
    for j in range(1, 3):
        part = part + mm_nt(back[:, j * inner : (j + 1) * inner], weight[j])
    part_out[...] = part
    first_hat, _ = normed(seq[...])
    cross_out[...] = jnp.zeros_like(cross_out) if before is None else before[...]
    cross_out[6:7, 0:width] += jnp.sum(part * first_hat, 0, keepdims=True)
    cross_out[7:8, 0:width] += jnp.sum(part, 0, keepdims=True)


def branch_body(*refs):
    (*hiddens, down, part_out) = refs
    rows, size = hiddens[0].shape[0], part_out.shape[0] // len(hiddens)
    for image, hidden in enumerate(hiddens):
        part_out[(image + 1) * size - 8 : (image + 1) * size, :] = jnp.zeros((8, part_out.shape[1]), F32)
        part_out[image * size : image * size + rows, :] = mm(hidden[...], down[...])


def output_body(images, down_mine, down_other, bias, *refs):
    middles, out = refs[:images], refs[images]
    rows, size = middles[0].shape[0], down_mine.shape[0] // images
    for image in range(images):
        own = slice(image * size, image * size + rows)
        branch = down_mine[own, :] + down_other[own, :] + line(bias)
        out[image] = (middles[image][...] + branch).astype(BF16)


def input_body(gain, seq, mine, other, grad, out):
    hat, rate = normed(seq[...])
    out[...] = grad[...] + norm_back(mine[...] + other[...], hat, rate, line(gain))


def grads_body(layout, order, chunk, smalls, ids, *refs):
    lefts, rights, at = [], [], 0
    for images, _ in layout:
        lefts.append(refs[at : at + images])
        rights.append(refs[at + images : at + 2 * images])
        at += 2 * images
    small_refs = refs[at : at + smalls]
    keep, send, turned, stacked, tail = refs[at + smalls :]
    width = lefts[0][0].shape[1]
    size, half = width // 16, width // 2
    main = lefts[0][0].shape[0] // 8 * 8
    spare = lefts[0][0].shape[0] - main
    step = pl.program_id(0)
    even = ids[0] == 0

    def turn(value, start):
        columns = value.astype(F32).T
        stop = start + value.shape[0]
        for place in range(8):
            source = 0
            for digit, bit in enumerate(order):
                source |= ((place >> (2 - digit)) & 1) << bit
            zero = columns[source * size : (source + 1) * size, :]
            one = columns[(source + 1) * size : (source + 2) * size, :]
            rows = slice(place * size, (place + 1) * size)
            turned[rows, start:stop] = jnp.where(even, zero, one).astype(BF16)
            rows = slice(half + place * size, half + (place + 1) * size)
            turned[rows, start:stop] = jnp.where(even, one, zero).astype(BF16)

    begin = 0
    for (images, steps), left, right in zip(layout, lefts, rights):
        @pl.when(step == begin)
        def _(left=left, images=images):
            tail[...] = jnp.zeros_like(tail)
            for i, ref in enumerate(left):
                turn(ref[0:main, :], i * main)
                tail[i * spare : (i + 1) * spare, 0:width] = ref[main:, :].astype(F32)
            turn(tail[:, 0:width], images * main)

        @pl.when((step >= begin) & (step < begin + steps))
        def _(right=right, images=images):
            tail[...] = jnp.zeros_like(tail)
            for i, ref in enumerate(right):
                stacked[i * main : (i + 1) * main, :] = ref[0:main, :].astype(BF16)
                tail[i * spare : (i + 1) * spare, 0:chunk] = ref[main:, :].astype(F32)
            stacked[images * main :, :] = tail[:, 0:chunk].astype(BF16)

        begin += steps
    total = mm(turned[...], stacked[...])
    keep[0:half, :] = total[0:half, :]
    send[0:half, :] = total[half:, :]
    if smalls:
        keep[half:, :] = jnp.zeros_like(keep[half:, :])
        send[half:, :] = jnp.zeros_like(send[half:, :])
        for place in range(width // chunk):
            @pl.when(step == place)
            def _(place=place):
                cols = slice(place * chunk, (place + 1) * chunk)
                small = small_refs[0][:, cols]
                for ref in small_refs[1:]:
                    small = small + ref[:, cols]
                keep[half:, :] = small
                send[half:, :] = small


def sum_body(count, smalls, ids, *refs):
    blocks, small_refs, outs = refs[:count], refs[count : count + smalls], refs[count + smalls :]
    size = blocks[0].shape[0]
    total = blocks[0][...] + blocks[1][...]
    for ref in blocks[2:]:
        total = total + ref[...]
    outs[0][0:size, :] = total
    if smalls:
        kept, got, near, far_one, *rest = (ref[...] for ref in small_refs)
        small = (kept + got) + (near + far_one)
        for one in rest:
            small = small + one
        if len(outs) == 1:
            outs[0][size:, :] = small
        else:
            outs[1][...] = small


class Part:
    def __init__(self, chain, ids, dp, name, order, arrays, columns, at, cross):
        self.chain, self.ids, self.dp, self.name, self.order = chain, ids, dp, name, order
        self.columns, self.at, self.cross = columns, at, cross
        self.arrays = [(array, 0) for array in arrays]
        self.half = arrays[0].shape[0] // 8 * 8 if cross is None else arrays[0].shape[0] - 8
        self.steps = 0

    def add(self, digits, flip, outs, name):
        size = self.half >> digits
        args, specs = [self.ids], []

        def rows_of(level):
            def index(j, ids):
                at = 0
                for digit in range(level, digits):
                    bit = ids[self.order[digit]]
                    at = 2 * at + ((1 - bit) if flip and digit == digits - 1 else bit)
                return (at, self.at if level == 0 else 0)
            return index

        for array, level in self.arrays:
            args.append(array)
            specs.append(pl.BlockSpec((size, self.columns), rows_of(level)))
        smalls = 0
        if self.cross is not None:
            small = [(array, (self.half >> level) // 8) for array, level in self.arrays]
            small[2:2] = [(array, 0) for array in self.cross]
            for array, row in small:
                args.append(array)
                specs.append(pl.BlockSpec((8, self.columns), lambda j, ids, row=row: (row, 0)))
            smalls = len(small)
        return self.chain.call(
            partial(sum_body, len(self.arrays), smalls), args, specs, outs, 16, f"{self.name}_{name}",
            scalar=1, deep=(1, 2) if digits == 1 else (1,),
        )

    def step(self):
        if self.arrays is None:
            return
        bit = self.order[self.steps]
        self.steps += 1
        extra = 0 if self.cross is None else 8
        out = shape(((self.half >> self.steps) + extra, self.columns))
        (send,) = self.add(self.steps, True, [out], f"step{bit}")
        self.arrays.append((lax.ppermute(send, "dp", flips(self.dp, bit)), self.steps))

    def finish(self):
        outs = [shape((self.half >> self.steps, self.columns))]
        if self.cross is not None:
            outs.append(shape((8, self.columns)))
        return self.add(self.steps, False, outs, "last")


class Plain:
    def __init__(self, full, small):
        self.full, self.small = full, small

    def step(self):
        pass

    def finish(self):
        total = lax.psum_scatter(self.full, "dp", scatter_dimension=0, tiled=True)
        return [total] if self.small is None else [total, lax.psum(self.small, "dp")]


def weight_sum(chain, ids, dp, name, chunk, sets, smalls=(), cross=None, beside=None, parts=1, order=(1, 2, 3)):
    width = sets[0][0].shape[-1] if not isinstance(sets[0][0], list) else sets[0][0][0].shape[1]
    columns = sum(rights[0].shape[1] for _, rights in sets)
    size = columns // parts
    if not folded(dp):
        products = [sum(mm_tn(left, right.astype(BF16)) for left, right in zip(*pair)) for pair in sets]
        full = jnp.concatenate(products, 1)
        small = sum(smalls) + lax.ppermute(cross[:, :width], "mp", SWAP) if smalls else None
        pieces = [
            Plain(full[:, i * size : (i + 1) * size], small if i == 0 else None) for i in range(parts)
        ]
        return pieces, beside() if beside else None
    args, specs, layout, begin = [], [], [], 0
    for lefts, rights in sets:
        steps = rights[0].shape[1] // chunk
        if isinstance(lefts, list):
            args += lefts
            specs += [whole(v) for v in lefts]
        else:
            args += [lefts] * lefts.shape[0]
            specs += [one_of(lefts, b) for b in range(lefts.shape[0])]
        args += rights
        for v in rights:
            block = lambda j, begin=begin, steps=steps: (0, jnp.clip(j - begin, 0, steps - 1))
            specs.append(pl.BlockSpec((v.shape[0], chunk), block))
        layout.append((len(rights), steps))
        begin += steps
    images, rows = len(sets[0][1]), sets[0][1][0].shape[0]
    spare = 8 * pl.cdiv(images * (rows % 8), 8)
    depth = images * (rows // 8 * 8) + spare
    dims = (width // 2 + (8 if smalls else 0), columns)
    block = pl.BlockSpec((dims[0], chunk), lambda j: (0, j))
    keep, send = chain.call(
        partial(grads_body, layout, order, chunk, len(smalls)), [ids, *args, *smalls],
        [scalars(), *specs] + [whole(v) for v in smalls], [far(dims), far(dims)], 32,
        f"{name}_grads", grid=begin, out_specs=[block, block],
        scratch=[
            pltpu.VMEM((width, depth), BF16),
            pltpu.VMEM((depth, chunk), BF16),
            pltpu.VMEM((spare, max(width, chunk)), F32),
        ],
        deep=range(1, 1 + len(args)),
    )
    swap = lambda v: lax.ppermute(v, "dp", flips(dp, 0))
    if cross is not None:
        pairs = [((d, m), (d ^ 1, m ^ 1)) for d in range(dp) for m in range(2)]
        corners = [(2 * p[0] + p[1], 2 * q[0] + q[1]) for p, q in pairs]
        moves = lambda v, c: (swap(v), lax.ppermute(c, "mp", SWAP), lax.ppermute(c, ("dp", "mp"), corners))
        got, *crosses = chain.at_once(ids, moves, send, cross)
        done = None
    elif beside:
        got, done = chain.at_once(ids, lambda v: (swap(v), beside()), send)
        crosses = None
    else:
        (got,) = chain.at_once(ids, lambda v: (swap(v),), send)
        crosses, done = None, None
    pieces = [
        Part(chain, ids, dp, f"{name}{i}", order, [keep, got], size, i, crosses if i == 0 else None)
        for i in range(parts)
    ]
    for piece in pieces:
        piece.half = width // 2
    return pieces, done


def folded(dp):
    return dp == 16


def flips(dp, bit):
    return [(i, i ^ (1 << bit)) for i in range(dp)]


def per_device(
    dp,
    patches,
    extra_tokens,
    visible,
    qkv_weight,
    out_weight,
    out_bias,
    up_weight,
    up_bias,
    down_weight,
    down_bias,
    first_gain,
    first_shift,
    second_gain,
    second_shift,
    cotangent,
):
    images, _, width = patches.shape
    rows = visible.shape[1] + extra_tokens.shape[1]
    inner = qkv_weight.shape[2]
    hidden_width = up_weight.shape[1]
    place = lax.axis_index("dp")
    core = place % 2
    ids = jnp.stack([core] + [(place >> bit) & 1 for bit in (1, 2, 3)] + [lax.axis_index("mp")])
    ids = lax.optimization_barrier(ids.astype(jnp.int32))
    across = lambda v: lax.ppermute(v, "mp", SWAP)

    core_swap = lambda v: (lax.ppermute(v, "dp", flips(dp, 0)),)
    chain = Chain()

    quarter = inner // 2
    piece = lax.dynamic_slice_in_dim(out_weight, core * quarter, quarter, 0).astype(F32)
    near = across(piece)

    every = range(images)
    args = [visible, patches, extra_tokens, qkv_weight, first_gain, first_shift]
    each = lambda dims: pl.BlockSpec((None, *dims[1:]), lambda j: (j,) + (0,) * (len(dims) - 1))
    stacks = [
        far((images, rows, width)), far((images, rows, width), BF16), far((images, rows, 3 * inner), BF16),
        far((images, rows, PAIR)),
    ]
    flat = [shape((rows, inner))] * images
    seqs, firsts, qkvs, logs, *mixeds = chain.call(
        partial(attend_body, images), args,
        [whole(visible), each(patches.shape)] + [whole(a) for a in args[2:]],
        stacks + flat, 40, "attend", grid=images,
        out_specs=[each(o.shape) for o in stacks] + [whole(o) for o in flat], deep=range(6),
    )
    mixed_others = [across(mixeds[0])]
    (distant,) = chain.at_once(ids, core_swap, near)
    (full,) = chain.call(
        join_body, [ids, out_weight, near, distant],
        [scalars(), whole(out_weight), whole(near), whole(distant)],
        [shape((2 * inner, width), BF16)], 16, "join",
    )

    for b in range(1, images):
        mixeds[b] = chain.hold(mixeds[b])
        mixed_others.append(across(mixeds[b]))

    middles, seconds, hiddens, uppers, norms, smalls, norm_others = [], [], [], [], [], [], []
    for b in every:
        args = [ids, seqs, cotangent, out_bias, second_gain, second_shift, up_bias,
                mixeds[b], mixed_others[b], full, up_weight, down_weight]
        got = chain.call(
            forward_body, args,
            [scalars(), one_of(seqs, b), one_of(cotangent, b)] + [whole(a) for a in args[3:]],
            [far((rows, width)), far((rows, width), BF16), far((rows, hidden_width), BF16),
             far((rows, hidden_width), BF16), shape((rows, width)), far((8, width))],
            44, f"forward{b}", deep=(1, 3, 4, 5, 6),
        )
        for kept, one in zip((middles, seconds, hiddens, uppers, norms, smalls), got):
            kept.append(one)
        norm_others.append(across(norms[b]))

    padded = images * 8 * pl.cdiv(rows, 8)

    def branch():
        return kernel(
            branch_body, [*hiddens, down_weight], [whole(a) for a in (*hiddens, down_weight)],
            [shape((padded, width))], 32, "branch",
        )[0]

    (down_sum,), down_part = weight_sum(chain, ids, dp, "down", 512, [(cotangent, hiddens)], beside=branch)
    down_sum.step()

    grads, attns, backs, firsts_part, crosses, part_others = [], [], [], [], [], []
    for b in every:
        args = [norms[b], norm_others[b], middles[b], qkvs, logs, seqs, cotangent, second_gain,
                out_weight, qkv_weight, *crosses[-1:]]
        specs = [whole(a) for a in args]
        for i in (3, 4, 5, 6):
            specs[i] = one_of(args[i], b)
        got = chain.call(
            backward_body, args, specs,
            [far((rows, width)), far((rows, width), BF16), far((rows, 3 * inner), BF16),
             shape((rows, width)), far((8, width)), shape((8, hidden_width))],
            44, f"backward{b}", deep=(2, 3, 4, 5, 7), cost=33,
        )
        for kept, one in zip((grads, attns, backs, firsts_part, smalls, crosses), got):
            kept.append(one)
        part_others.append(across(firsts_part[b]))
        if b == 0:
            (up_sum,), _ = weight_sum(chain, ids, dp, "up", 512, [(seconds, uppers)])
            up_sum.step()
    part_others[0] = chain.hold(part_others[0])
    down_sum.step()
    sets = [(attns, mixeds), (firsts, backs)]
    (out_sum, qkv_sum), _ = weight_sum(
        chain, ids, dp, "last", 384, sets, [*smalls, crosses[-1][:, :width]], crosses[-1], parts=2,
    )

    def input_of(b):
        args = [first_gain, seqs, firsts_part[b], part_others[b], grads[b]]
        specs = [whole(a) for a in args]
        specs[1] = one_of(seqs, b)
        return chain.call(
            input_body, args, specs, [shape((rows, width))], 32, f"input{b}", deep=(0, 1, 4)
        )[0]

    out_sum.step()
    down_sum.step()
    up_sum.step()
    qkv_sum.step()
    input_grads = [input_of(b) for b in range(images - 1)]
    out_sum.step()
    input_grads.append(input_of(images - 1))
    down_part = chain.hold(down_part)
    down_other = across(down_part)
    (down_total,) = down_sum.finish()
    up_sum.step()
    qkv_sum.step()
    out_sum.step()
    (up_total,) = up_sum.finish()
    qkv_sum.step()
    out_total, small = out_sum.finish()
    args = [down_part, down_other, down_bias, *middles]
    (output,) = chain.call(
        partial(output_body, images), args, [whole(a) for a in args],
        [shape((images, rows, width), BF16)], 32, "output", deep=(2,),
    )
    (qkv_total,) = qkv_sum.finish()
    small = small[:, :width]
    return (
        output,
        jnp.stack(input_grads),
        jnp.stack([out_total[:, inner:], qkv_total[:, :inner], qkv_total[:, inner:]]),
        out_total[:, :inner].T,
        small[5],
        up_total,
        small[0:2].reshape(-1),
        down_total.T,
        small[4],
        small[6],
        small[7],
        small[2],
        small[3],
    )


def solution(mesh):
    return jax.shard_map(
        partial(per_device, mesh.shape["dp"]),
        mesh=mesh,
        in_specs=(
            P("dp", None, None),
            P("dp", None, None),
            P("dp", None),
            P(None, None, "mp"),
            P("mp", None),
            P(),
            P(None, "mp"),
            P("mp"),
            P("mp", None),
            P(),
            P(),
            P(),
            P(),
            P(),
            P("dp", None, None),
        ),
        out_specs=(
            P("dp", None, None),
            P("dp", None, None),
            P(None, "dp", "mp"),
            P("mp", "dp"),
            P(),
            P("dp", "mp"),
            P("mp"),
            P("mp", "dp"),
            P(),
            P(),
            P(),
            P(),
            P(),
        ),
        check_vma=False,
    )
```

```python
from functools import partial

import jax
import jax.numpy as jnp
from jax import lax
from jax.experimental import pallas as pl
from jax.experimental.pallas import tpu as pltpu
from jax.sharding import PartitionSpec as P

HEAD_DIM = 64
PAIR = 2 * HEAD_DIM
F32 = jnp.float32
BF16 = jnp.bfloat16
MIB = 1 << 20
SWAP = ((0, 1), (1, 0))


def mm(a, b):
    return lax.dot_general(a, b, (((1,), (0,)), ((), ())), preferred_element_type=F32)


def mm_nt(a, b):
    return lax.dot_general(a, b, (((1,), (1,)), ((), ())), preferred_element_type=F32)


def mm_tn(a, b):
    return lax.dot_general(a, b, (((0,), (0,)), ((), ())), preferred_element_type=F32)


def normed(values):
    center = values - jnp.mean(values, -1, keepdims=True)
    rate = lax.rsqrt(jnp.mean(center * center, -1, keepdims=True) + 1e-06)
    return center * rate, rate


def norm_back(grad, hat, rate, gain):
    scaled = grad * gain
    return rate * (
        scaled
        - jnp.mean(scaled, -1, keepdims=True)
        - hat * jnp.mean(scaled * hat, -1, keepdims=True)
    )


def shape(dims, dtype=F32):
    return jax.ShapeDtypeStruct(tuple(dims), dtype)


def far(dims, dtype=F32):
    return pltpu.HBM(tuple(dims), dtype)


def whole(x):
    return pl.BlockSpec(x.shape, lambda i, *_: (0,) * len(x.shape))


def one_of(x, image):
    return pl.BlockSpec((None,) + x.shape[1:], lambda i, *_: (image,) + (0,) * (x.ndim - 1))


def scalars():
    return pl.BlockSpec(memory_space=pltpu.SMEM)


ANYWHERE = pl.BlockSpec(memory_space=pl.ANY)


def kernel(body, args, specs, outs, vmem, name, grid=1, out_specs=None, scratch=(), deep=(), scalar=0, cost=31):
    args = [pltpu.with_memory_space_constraint(a, pltpu.HBM) if i in deep else a for i, a in enumerate(args)]
    return pl.pallas_call(
        body,
        out_shape=tuple(outs),
        grid_spec=pltpu.PrefetchScalarGridSpec(
            num_scalar_prefetch=scalar,
            grid=(grid,),
            in_specs=specs,
            out_specs=tuple(out_specs or [whole(o) for o in outs]),
            scratch_shapes=list(scratch),
        ),
        compiler_params=pltpu.CompilerParams(vmem_limit_bytes=vmem * MIB),
        cost_estimate=pl.CostEstimate(flops=1 << cost, bytes_accessed=1, transcendentals=0),
        name=name,
    )(*args)


class Chain:
    def __init__(self):
        self.token = jnp.zeros((8, 128), F32)

    def call(self, body, args, specs, outs, vmem, name, out_specs=None, **more):
        taken, given = len(args), len(outs)

        def without_tokens(*refs):
            return body(*refs[:taken], *refs[taken + 1 : taken + 1 + given], *refs[taken + 2 + given :])

        *got, self.token = kernel(
            without_tokens, [*args, self.token], [*specs, ANYWHERE], [*outs, shape((8, 128))], vmem, name,
            out_specs=[*(out_specs or [whole(o) for o in outs]), ANYWHERE], **more,
        )
        return got

    def hold(self, value):
        value, self.token = lax.optimization_barrier((value, self.token))
        return value

    def at_once(self, ids, moves, *values):
        outs = jax.eval_shape(moves, *values)
        moved = lambda token, *vs: (token, *moves(*vs))
        never = lambda token, *vs: (token, *(jnp.zeros(o.shape, o.dtype) for o in outs))
        self.token, *got = lax.cond(ids[0] >= 0, moved, never, self.token, *values)
        return got


def line(vector):
    return vector[...].reshape(1, -1)


def side_masks(value=1.0):
    lane = lax.broadcasted_iota(jnp.int32, (1, PAIR), 1)
    low = jnp.where(lane < HEAD_DIM, value, 0.0)
    return low.astype(BF16), (value - low).astype(BF16)


def attend_body(image, pick, patch, extra, weight, gain, shift, seq_out, first_out, qkv_out, log_out, mixed_out):
    rows, width = seq_out.shape
    inner = mixed_out.shape[1]
    extras, picks = extra.shape[1], pick.shape[1]
    spread = jnp.broadcast_to(pick[image : image + 1, :].astype(F32), (128, picks))
    column = spread.T[:, 0:1].astype(jnp.int32)
    hot = lax.broadcasted_iota(jnp.int32, (picks, patch.shape[0]), 1) == column
    seq_out[extras:, :] = mm(jnp.where(hot, 1.0, 0.0).astype(BF16), patch[...])
    seq_out[0:extras, :] = extra[image].astype(F32)
    hat, _ = normed(seq_out[...])
    first = (hat * line(gain) + line(shift)).astype(BF16)
    first_out[...] = first
    for j in range(3):
        qkv_out[:, j * inner : (j + 1) * inner] = mm(first, weight[j]).astype(BF16)
    masks = side_masks(HEAD_DIM**-0.5)
    lane = lax.broadcasted_iota(jnp.int32, (rows, PAIR), 1)
    logs = jnp.zeros((rows, PAIR), F32)
    for pair in range(inner // PAIR):
        q = qkv_out[:, pair * PAIR : (pair + 1) * PAIR]
        k = qkv_out[:, inner + pair * PAIR : inner + (pair + 1) * PAIR]
        v = qkv_out[:, 2 * inner + pair * PAIR : 2 * inner + (pair + 1) * PAIR]
        sides = []
        for side in range(2):
            scores = mm_nt(q * masks[side], k)
            top = jnp.max(scores, -1, keepdims=True)
            expo = jnp.exp(scores - top)
            total = jnp.sum(expo, -1, keepdims=True)
            sides.append(mm((expo * (1.0 / total)).astype(BF16), v))
            logs = jnp.where(lane == 2 * pair + side, top + jnp.log(total), logs)
        mixed = jnp.where(lane < HEAD_DIM, sides[0], sides[1]).astype(BF16).astype(F32)
        mixed_out[:, pair * PAIR : (pair + 1) * PAIR] = mixed
    log_out[...] = logs


def join_body(ids, mine, *refs):
    *quarters, full_out = refs
    half = mine.shape[0]
    part = quarters[0].shape[0]
    other = (1 - ids[4]) * half
    full_out[pl.ds(pl.multiple_of(ids[4] * half, part), half), :] = mine[...]
    for i, quarter in enumerate(quarters):
        place = ((ids[1] ^ (i & 1)) * 2 + (ids[0] ^ (i >> 1))) * part
        full_out[pl.ds(pl.multiple_of(other + place, part), part), :] = quarter[...].astype(BF16)


def forward_body(
    ids, seq, dy, out_bias, gain, shift, up_bias, mine, other, full, up, down,
    middle_out, second_out, hidden_out, upper_out, norm_out, small_out,
):
    rows, width = seq.shape
    inner = mine.shape[1]
    first_half = ids[4] == 0
    left = jnp.where(first_half, mine[...], other[...]).astype(BF16)
    right = jnp.where(first_half, other[...], mine[...]).astype(BF16)
    attn = mm(left, full[0:inner, :]) + mm(right, full[inner:, :]) + line(out_bias)
    middle = seq[...] + attn
    middle_out[...] = middle
    hat, _ = normed(middle)
    second = (hat * line(gain) + line(shift)).astype(BF16)
    second_out[...] = second
    grad = dy[...].astype(BF16)
    small_out[...] = jnp.zeros_like(small_out)
    chunk = 512
    biases = line(up_bias)
    norm = jnp.zeros((rows, width), F32)
    for start in range(0, up.shape[1], chunk):
        cols = slice(start, start + chunk)
        upper = mm(second, up[:, cols]) + biases[:, cols]
        phi = 0.5 + 0.5 * lax.erf(upper * (0.5**0.5))
        hidden_out[:, cols] = (upper * phi).astype(BF16)
        slope = phi + upper * (jnp.exp(-0.5 * upper * upper) * 0.3989422804014327)
        back = (mm_nt(grad, down[cols, :]) * slope).astype(BF16)
        upper_out[:, cols] = back
        total = jnp.sum(back.astype(F32), 0, keepdims=True)
        for at in range(start, start + chunk, 256):
            row, place = divmod(at, width)
            small_out[row : row + 1, place : place + 256] = total[:, at - start : at - start + 256]
        norm = norm + mm_nt(back, up[:, cols])
    norm_out[...] = norm
    small_out[4:5, :] = jnp.sum(grad.astype(F32), 0, keepdims=True)


def backward_body(mine, other, middle, qkv, logs, seq, dy, gain, out_weight, weight, *refs):
    (*before, grad_out, attn_out, back, part_out, small_out, cross_out) = refs
    before = before[0] if before else None
    rows, width = middle.shape
    inner = out_weight.shape[0]
    hat, rate = normed(middle[...])
    total = mine[...] + other[...]
    grad = dy[...].astype(F32) + norm_back(total, hat, rate, line(gain))
    grad_out[...] = grad
    attn = grad.astype(BF16)
    attn_out[...] = attn
    small_out[...] = jnp.zeros_like(small_out)
    small_out[2:3, :] = jnp.sum(total * hat, 0, keepdims=True)
    small_out[3:4, :] = jnp.sum(total, 0, keepdims=True)
    small_out[5:6, :] = jnp.sum(attn.astype(F32), 0, keepdims=True)
    mixed = mm_nt(attn, out_weight[...]).astype(BF16)
    masks = side_masks()
    scaled = side_masks(HEAD_DIM**-0.5)
    lane = lax.broadcasted_iota(jnp.int32, (rows, PAIR), 1)
    scale = HEAD_DIM**-0.5
    for pair in range(inner // PAIR):
        cols = slice(pair * PAIR, (pair + 1) * PAIR)
        q = qkv[:, cols]
        k = qkv[:, inner + pair * PAIR : inner + (pair + 1) * PAIR]
        v = qkv[:, 2 * inner + pair * PAIR : 2 * inner + (pair + 1) * PAIR]
        dm = mixed[:, cols]
        q_t = q.astype(F32).T.astype(BF16)
        dm_t = dm.astype(F32).T.astype(BF16)
        dq, dk, dv = [], [], []
        for side in range(2):
            half = slice(side * HEAD_DIM, (side + 1) * HEAD_DIM)
            head = 2 * pair + side
            scores = mm_nt(q * scaled[side], k)
            probs = jnp.exp(scores - logs[:, head : head + 1])
            dv.append(mm(dm_t[half, :], probs.astype(BF16)))
            prob_grad = mm_nt(dm * masks[side], v)
            score = probs * (prob_grad - jnp.sum(prob_grad * probs, -1, keepdims=True))
            score = score.astype(BF16)
            dq.append(mm(score, k))
            dk.append(mm(q_t[half, :], score))
        parts = (
            jnp.where(lane < HEAD_DIM, dq[0], dq[1]) * scale,
            (jnp.concatenate(dk, 0) * scale).T,
            jnp.concatenate(dv, 0).T,
        )
        for j, value in enumerate(parts):
            start = j * inner + pair * PAIR
            back[:, start : start + PAIR] = value.astype(BF16)
    part = mm_nt(back[:, 0:inner], weight[0])
    for j in range(1, 3):
        part = part + mm_nt(back[:, j * inner : (j + 1) * inner], weight[j])
    part_out[...] = part
    first_hat, _ = normed(seq[...])
    cross_out[...] = jnp.zeros_like(cross_out) if before is None else before[...]
    cross_out[6:7, 0:width] += jnp.sum(part * first_hat, 0, keepdims=True)
    cross_out[7:8, 0:width] += jnp.sum(part, 0, keepdims=True)


def branch_body(*refs):
    (*hiddens, down, part_out) = refs
    rows, size = hiddens[0].shape[0], part_out.shape[0] // len(hiddens)
    for image, hidden in enumerate(hiddens):
        part_out[(image + 1) * size - 8 : (image + 1) * size, :] = jnp.zeros((8, part_out.shape[1]), F32)
        part_out[image * size : image * size + rows, :] = mm(hidden[...], down[...])


def output_body(images, down_mine, down_other, bias, *refs):
    middles, out = refs[:images], refs[images]
    rows, size = middles[0].shape[0], down_mine.shape[0] // images
    for image in range(images):
        own = slice(image * size, image * size + rows)
        branch = down_mine[own, :] + down_other[own, :] + line(bias)
        out[image] = (middles[image][...] + branch).astype(BF16)


def input_body(gain, seq, mine, other, grad, out):
    hat, rate = normed(seq[...])
    out[...] = grad[...] + norm_back(mine[...] + other[...], hat, rate, line(gain))


def grads_body(layout, order, chunk, smalls, ids, *refs):
    lefts, rights, at = [], [], 0
    for images, _ in layout:
        lefts.append(refs[at : at + images])
        rights.append(refs[at + images : at + 2 * images])
        at += 2 * images
    small_refs = refs[at : at + smalls]
    keep, send, turned, stacked, tail = refs[at + smalls :]
    width = lefts[0][0].shape[1]
    size, half = width // 16, width // 2
    main = lefts[0][0].shape[0] // 8 * 8
    spare = lefts[0][0].shape[0] - main
    step = pl.program_id(0)
    even = ids[0] == 0

    def turn(value, start):
        columns = value.astype(F32).T
        stop = start + value.shape[0]
        for place in range(8):
            source = 0
            for digit, bit in enumerate(order):
                source |= ((place >> (2 - digit)) & 1) << bit
            zero = columns[source * size : (source + 1) * size, :]
            one = columns[(source + 1) * size : (source + 2) * size, :]
            rows = slice(place * size, (place + 1) * size)
            turned[rows, start:stop] = jnp.where(even, zero, one).astype(BF16)
            rows = slice(half + place * size, half + (place + 1) * size)
            turned[rows, start:stop] = jnp.where(even, one, zero).astype(BF16)

    begin = 0
    for (images, steps), left, right in zip(layout, lefts, rights):
        @pl.when(step == begin)
        def _(left=left, images=images):
            tail[...] = jnp.zeros_like(tail)
            for i, ref in enumerate(left):
                turn(ref[0:main, :], i * main)
                tail[i * spare : (i + 1) * spare, 0:width] = ref[main:, :].astype(F32)
            turn(tail[:, 0:width], images * main)

        @pl.when((step >= begin) & (step < begin + steps))
        def _(right=right, images=images):
            tail[...] = jnp.zeros_like(tail)
            for i, ref in enumerate(right):
                stacked[i * main : (i + 1) * main, :] = ref[0:main, :].astype(BF16)
                tail[i * spare : (i + 1) * spare, 0:chunk] = ref[main:, :].astype(F32)
            stacked[images * main :, :] = tail[:, 0:chunk].astype(BF16)

        begin += steps
    total = mm(turned[...], stacked[...])
    keep[0:half, :] = total[0:half, :]
    send[0:half, :] = total[half:, :]
    if smalls:
        keep[half:, :] = jnp.zeros_like(keep[half:, :])
        send[half:, :] = jnp.zeros_like(send[half:, :])
        for place in range(width // chunk):
            @pl.when(step == place)
            def _(place=place):
                cols = slice(place * chunk, (place + 1) * chunk)
                small = small_refs[0][:, cols]
                for ref in small_refs[1:]:
                    small = small + ref[:, cols]
                keep[half:, :] = small
                send[half:, :] = small


def sum_body(count, smalls, ids, *refs):
    blocks, small_refs, outs = refs[:count], refs[count : count + smalls], refs[count + smalls :]
    size = blocks[0].shape[0]
    total = blocks[0][...] + blocks[1][...]
    for ref in blocks[2:]:
        total = total + ref[...]
    outs[0][0:size, :] = total
    if smalls:
        kept, got, near, far_one, *rest = (ref[...] for ref in small_refs)
        small = (kept + got) + (near + far_one)
        for one in rest:
            small = small + one
        if len(outs) == 1:
            outs[0][size:, :] = small
        else:
            outs[1][...] = small


class Part:
    def __init__(self, chain, ids, dp, name, order, arrays, columns, at, cross):
        self.chain, self.ids, self.dp, self.name, self.order = chain, ids, dp, name, order
        self.columns, self.at, self.cross = columns, at, cross
        self.arrays = [(array, 0) for array in arrays]
        self.half = arrays[0].shape[0] // 8 * 8 if cross is None else arrays[0].shape[0] - 8
        self.steps = 0

    def add(self, digits, flip, outs, name):
        size = self.half >> digits
        args, specs = [self.ids], []

        def rows_of(level):
            def index(j, ids):
                at = 0
                for digit in range(level, digits):
                    bit = ids[self.order[digit]]
                    at = 2 * at + ((1 - bit) if flip and digit == digits - 1 else bit)
                return (at, self.at if level == 0 else 0)
            return index

        for array, level in self.arrays:
            args.append(array)
            specs.append(pl.BlockSpec((size, self.columns), rows_of(level)))
        smalls = 0
        if self.cross is not None:
            small = [(array, (self.half >> level) // 8) for array, level in self.arrays]
            small[2:2] = [(array, 0) for array in self.cross]
            for array, row in small:
                args.append(array)
                specs.append(pl.BlockSpec((8, self.columns), lambda j, ids, row=row: (row, 0)))
            smalls = len(small)
        return self.chain.call(
            partial(sum_body, len(self.arrays), smalls), args, specs, outs, 16, f"{self.name}_{name}",
            scalar=1, deep=(1, 2) if digits == 1 else (1,),
        )

    def step(self):
        if self.arrays is None:
            return
        bit = self.order[self.steps]
        self.steps += 1
        extra = 0 if self.cross is None else 8
        out = shape(((self.half >> self.steps) + extra, self.columns))
        (send,) = self.add(self.steps, True, [out], f"step{bit}")
        self.arrays.append((lax.ppermute(send, "dp", flips(self.dp, bit)), self.steps))

    def finish(self):
        outs = [shape((self.half >> self.steps, self.columns))]
        if self.cross is not None:
            outs.append(shape((8, self.columns)))
        return self.add(self.steps, False, outs, "last")


class Plain:
    def __init__(self, full, small):
        self.full, self.small = full, small

    def step(self):
        pass

    def finish(self):
        total = lax.psum_scatter(self.full, "dp", scatter_dimension=0, tiled=True)
        return [total] if self.small is None else [total, lax.psum(self.small, "dp")]


def weight_sum(chain, ids, dp, name, chunk, sets, smalls=(), cross=None, beside=None, parts=1, order=(1, 2, 3)):
    width = sets[0][0].shape[-1] if not isinstance(sets[0][0], list) else sets[0][0][0].shape[1]
    columns = sum(rights[0].shape[1] for _, rights in sets)
    size = columns // parts
    if not folded(dp):
        products = [sum(mm_tn(left, right.astype(BF16)) for left, right in zip(*pair)) for pair in sets]
        full = jnp.concatenate(products, 1)
        small = sum(smalls) + lax.ppermute(cross[:, :width], "mp", SWAP) if smalls else None
        pieces = [
            Plain(full[:, i * size : (i + 1) * size], small if i == 0 else None) for i in range(parts)
        ]
        return pieces, beside() if beside else None
    args, specs, layout, begin = [], [], [], 0
    for lefts, rights in sets:
        steps = rights[0].shape[1] // chunk
        if isinstance(lefts, list):
            args += lefts
            specs += [whole(v) for v in lefts]
        else:
            args += [lefts] * lefts.shape[0]
            specs += [one_of(lefts, b) for b in range(lefts.shape[0])]
        args += rights
        for v in rights:
            block = lambda j, begin=begin, steps=steps: (0, jnp.clip(j - begin, 0, steps - 1))
            specs.append(pl.BlockSpec((v.shape[0], chunk), block))
        layout.append((len(rights), steps))
        begin += steps
    images, rows = len(sets[0][1]), sets[0][1][0].shape[0]
    spare = 8 * pl.cdiv(images * (rows % 8), 8)
    depth = images * (rows // 8 * 8) + spare
    dims = (width // 2 + (8 if smalls else 0), columns)
    block = pl.BlockSpec((dims[0], chunk), lambda j: (0, j))
    keep, send = chain.call(
        partial(grads_body, layout, order, chunk, len(smalls)), [ids, *args, *smalls],
        [scalars(), *specs] + [whole(v) for v in smalls], [far(dims), far(dims)], 32,
        f"{name}_grads", grid=begin, out_specs=[block, block],
        scratch=[
            pltpu.VMEM((width, depth), BF16),
            pltpu.VMEM((depth, chunk), BF16),
            pltpu.VMEM((spare, max(width, chunk)), F32),
        ],
        deep=range(1, 1 + len(args)),
    )
    swap = lambda v: lax.ppermute(v, "dp", flips(dp, 0))
    if cross is not None:
        pairs = [((d, m), (d ^ 1, m ^ 1)) for d in range(dp) for m in range(2)]
        corners = [(2 * p[0] + p[1], 2 * q[0] + q[1]) for p, q in pairs]
        moves = lambda v, c: (swap(v), lax.ppermute(c, "mp", SWAP), lax.ppermute(c, ("dp", "mp"), corners))
        got, *crosses = chain.at_once(ids, moves, send, cross)
        done = None
    elif beside:
        got, done = chain.at_once(ids, lambda v: (swap(v), beside()), send)
        crosses = None
    else:
        (got,) = chain.at_once(ids, lambda v: (swap(v),), send)
        crosses, done = None, None
    pieces = [
        Part(chain, ids, dp, f"{name}{i}", order, [keep, got], size, i, crosses if i == 0 else None)
        for i in range(parts)
    ]
    for piece in pieces:
        piece.half = width // 2
    return pieces, done


def folded(dp):
    return dp == 16


def flips(dp, bit):
    return [(i, i ^ (1 << bit)) for i in range(dp)]


def per_device(
    dp,
    patches,
    extra_tokens,
    visible,
    qkv_weight,
    out_weight,
    out_bias,
    up_weight,
    up_bias,
    down_weight,
    down_bias,
    first_gain,
    first_shift,
    second_gain,
    second_shift,
    cotangent,
):
    images, _, width = patches.shape
    rows = visible.shape[1] + extra_tokens.shape[1]
    inner = qkv_weight.shape[2]
    hidden_width = up_weight.shape[1]
    place = lax.axis_index("dp")
    core = place % 2
    ids = jnp.stack([core] + [(place >> bit) & 1 for bit in (1, 2, 3)] + [lax.axis_index("mp")])
    ids = lax.optimization_barrier(ids.astype(jnp.int32))
    across = lambda v: lax.ppermute(v, "mp", SWAP)

    chain = Chain()
    every = range(images)

    quarter = inner // 4
    piece = lax.dynamic_slice_in_dim(out_weight, place % 4 * quarter, quarter, 0).astype(F32)
    near = across(piece)

    seqs, firsts, qkvs, logs, mixeds, mixed_others = [], [], [], [], [], []
    for b in every:
        args = [visible, patches, extra_tokens, qkv_weight, first_gain, first_shift]
        got = chain.call(
            partial(attend_body, b), args,
            [whole(visible), one_of(patches, b)] + [whole(a) for a in args[2:]],
            [far((rows, width)), far((rows, width), BF16), far((rows, 3 * inner), BF16),
             far((rows, PAIR)), shape((rows, inner))],
            40, f"attend{b}", deep=range(6),
        )
        for kept, one in zip((seqs, firsts, qkvs, logs, mixeds), got):
            kept.append(one)
        mixed_others.append(across(mixeds[b]))
        if b == 0:
            near = chain.hold(near)
            beyond = lax.ppermute(near, "dp", flips(dp, 1))
    swaps = lambda *vs: tuple(lax.ppermute(v, "dp", flips(dp, 0)) for v in vs)
    quarters = [near, beyond, *chain.at_once(ids, swaps, near, beyond)]
    (full,) = chain.call(
        join_body, [ids, out_weight, *quarters],
        [scalars(), whole(out_weight)] + [whole(q) for q in quarters],
        [shape((2 * inner, width), BF16)], 16, "join",
    )

    middles, seconds, hiddens, uppers, norms, smalls, norm_others = [], [], [], [], [], [], []
    for b in every:
        args = [ids, seqs[b], cotangent, out_bias, second_gain, second_shift, up_bias,
                mixeds[b], mixed_others[b], full, up_weight, down_weight]
        got = chain.call(
            forward_body, args,
            [scalars(), whole(seqs[b]), one_of(cotangent, b)] + [whole(a) for a in args[3:]],
            [far((rows, width)), far((rows, width), BF16), far((rows, hidden_width), BF16),
             far((rows, hidden_width), BF16), shape((rows, width)), far((8, width))],
            44, f"forward{b}", deep=(1, 3, 4, 5, 6),
        )
        for kept, one in zip((middles, seconds, hiddens, uppers, norms, smalls), got):
            kept.append(one)
        norm_others.append(across(norms[b]))

    padded = images * 8 * pl.cdiv(rows, 8)

    def branch():
        return kernel(
            branch_body, [*hiddens, down_weight], [whole(a) for a in (*hiddens, down_weight)],
            [shape((padded, width))], 32, "branch",
        )[0]

    (down_sum,), down_part = weight_sum(chain, ids, dp, "down", 768, [(cotangent, hiddens)], beside=branch)
    down_sum.step()

    grads, attns, backs, firsts_part, crosses, part_others = [], [], [], [], [], []
    for b in every:
        args = [norms[b], norm_others[b], middles[b], qkvs[b], logs[b], seqs[b], cotangent, second_gain,
                out_weight, qkv_weight, *crosses[-1:]]
        specs = [whole(a) for a in args]
        specs[6] = one_of(cotangent, b)
        got = chain.call(
            backward_body, args, specs,
            [far((rows, width)), far((rows, width), BF16), far((rows, 3 * inner), BF16),
             shape((rows, width)), far((8, width)), shape((8, hidden_width))],
            44, f"backward{b}", deep=(2, 3, 4, 5, 7), cost=33,
        )
        for kept, one in zip((grads, attns, backs, firsts_part, smalls, crosses), got):
            kept.append(one)
        part_others.append(across(firsts_part[b]))
        if b == 0:
            (up_sum,), _ = weight_sum(chain, ids, dp, "up", 768, [(seconds, uppers)])
            up_sum.step()
    part_others[0] = chain.hold(part_others[0])
    down_sum.step()
    sets = [(attns, mixeds), (firsts, backs)]
    (out_sum, qkv_sum), _ = weight_sum(
        chain, ids, dp, "last", 384, sets, [*smalls, crosses[-1][:, :width]], crosses[-1], parts=2,
    )

    def input_of(b):
        args = [first_gain, seqs[b], firsts_part[b], part_others[b], grads[b]]
        return chain.call(
            input_body, args, [whole(a) for a in args], [shape((rows, width))], 32, f"input{b}", deep=(0, 1, 4)
        )[0]

    out_sum.step()
    down_sum.step()
    up_sum.step()
    qkv_sum.step()
    input_grads = [input_of(b) for b in range(images - 1)]
    out_sum.step()
    input_grads.append(input_of(images - 1))
    down_part = chain.hold(down_part)
    down_other = across(down_part)
    (down_total,) = down_sum.finish()
    up_sum.step()
    qkv_sum.step()
    out_sum.step()
    (up_total,) = up_sum.finish()
    qkv_sum.step()
    out_total, small = out_sum.finish()
    args = [down_part, down_other, down_bias, *middles]
    (output,) = chain.call(
        partial(output_body, images), args, [whole(a) for a in args],
        [shape((images, rows, width), BF16)], 32, "output", deep=(2,),
    )
    (qkv_total,) = qkv_sum.finish()
    small = small[:, :width]
    return (
        output,
        jnp.stack(input_grads),
        jnp.stack([out_total[:, inner:], qkv_total[:, :inner], qkv_total[:, inner:]]),
        out_total[:, :inner].T,
        small[5],
        up_total,
        small[0:2].reshape(-1),
        down_total.T,
        small[4],
        small[6],
        small[7],
        small[2],
        small[3],
    )


def solution(mesh):
    return jax.shard_map(
        partial(per_device, mesh.shape["dp"]),
        mesh=mesh,
        in_specs=(
            P("dp", None, None),
            P("dp", None, None),
            P("dp", None),
            P(None, None, "mp"),
            P("mp", None),
            P(),
            P(None, "mp"),
            P("mp"),
            P("mp", None),
            P(),
            P(),
            P(),
            P(),
            P(),
            P("dp", None, None),
        ),
        out_specs=(
            P("dp", None, None),
            P("dp", None, None),
            P(None, "dp", "mp"),
            P("mp", "dp"),
            P(),
            P("dp", "mp"),
            P("mp"),
            P("mp", "dp"),
            P(),
            P(),
            P(),
            P(),
            P(),
        ),
        check_vma=False,
    )
```

```python
from functools import partial

import jax
import jax.numpy as jnp
from jax import lax
from jax.experimental import pallas as pl
from jax.experimental.pallas import tpu as pltpu
from jax.sharding import PartitionSpec as P

HEAD_DIM = 64
PAIR = 2 * HEAD_DIM
F32 = jnp.float32
BF16 = jnp.bfloat16
MIB = 1 << 20
SWAP = ((0, 1), (1, 0))


def mm(a, b):
    return lax.dot_general(a, b, (((1,), (0,)), ((), ())), preferred_element_type=F32)


def mm_nt(a, b):
    return lax.dot_general(a, b, (((1,), (1,)), ((), ())), preferred_element_type=F32)


def mm_tn(a, b):
    return lax.dot_general(a, b, (((0,), (0,)), ((), ())), preferred_element_type=F32)


def normed(values):
    center = values - jnp.mean(values, -1, keepdims=True)
    rate = lax.rsqrt(jnp.mean(center * center, -1, keepdims=True) + 1e-06)
    return center * rate, rate


def norm_back(grad, hat, rate, gain):
    scaled = grad * gain
    return rate * (
        scaled
        - jnp.mean(scaled, -1, keepdims=True)
        - hat * jnp.mean(scaled * hat, -1, keepdims=True)
    )


def shape(dims, dtype=F32):
    return jax.ShapeDtypeStruct(tuple(dims), dtype)


def far(dims, dtype=F32):
    return pltpu.HBM(tuple(dims), dtype)


def whole(x):
    return pl.BlockSpec(x.shape, lambda i, *_: (0,) * len(x.shape))


def one_of(x, image):
    return pl.BlockSpec((None,) + x.shape[1:], lambda i, *_: (image,) + (0,) * (x.ndim - 1))


def scalars():
    return pl.BlockSpec(memory_space=pltpu.SMEM)


ANYWHERE = pl.BlockSpec(memory_space=pl.ANY)


def kernel(body, args, specs, outs, vmem, name, grid=1, out_specs=None, scratch=(), deep=(), scalar=0, cost=31):
    args = [pltpu.with_memory_space_constraint(a, pltpu.HBM) if i in deep else a for i, a in enumerate(args)]
    return pl.pallas_call(
        body,
        out_shape=tuple(outs),
        grid_spec=pltpu.PrefetchScalarGridSpec(
            num_scalar_prefetch=scalar,
            grid=(grid,),
            in_specs=specs,
            out_specs=tuple(out_specs or [whole(o) for o in outs]),
            scratch_shapes=list(scratch),
        ),
        compiler_params=pltpu.CompilerParams(vmem_limit_bytes=vmem * MIB),
        cost_estimate=pl.CostEstimate(flops=1 << cost, bytes_accessed=1, transcendentals=0),
        name=name,
    )(*args)


class Chain:
    def __init__(self):
        self.token = jnp.zeros((8, 128), F32)

    def call(self, body, args, specs, outs, vmem, name, out_specs=None, **more):
        taken, given = len(args), len(outs)

        def without_tokens(*refs):
            return body(*refs[:taken], *refs[taken + 1 : taken + 1 + given], *refs[taken + 2 + given :])

        *got, self.token = kernel(
            without_tokens, [*args, self.token], [*specs, ANYWHERE], [*outs, shape((8, 128))], vmem, name,
            out_specs=[*(out_specs or [whole(o) for o in outs]), ANYWHERE], **more,
        )
        return got

    def hold(self, value):
        value, self.token = lax.optimization_barrier((value, self.token))
        return value

    def at_once(self, ids, moves, *values):
        outs = jax.eval_shape(moves, *values)
        moved = lambda token, *vs: (token, *moves(*vs))
        never = lambda token, *vs: (token, *(jnp.zeros(o.shape, o.dtype) for o in outs))
        self.token, *got = lax.cond(ids[0] >= 0, moved, never, self.token, *values)
        return got


def line(vector):
    return vector[...].reshape(1, -1)


def side_masks(value=1.0):
    lane = lax.broadcasted_iota(jnp.int32, (1, PAIR), 1)
    low = jnp.where(lane < HEAD_DIM, value, 0.0)
    return low.astype(BF16), (value - low).astype(BF16)


def attend_body(image, pick, patch, extra, weight, gain, shift, seq_out, first_out, qkv_out, log_out, mixed_out):
    rows, width = seq_out.shape
    inner = mixed_out.shape[1]
    extras, picks = extra.shape[1], pick.shape[1]
    spread = jnp.broadcast_to(pick[image : image + 1, :].astype(F32), (128, picks))
    column = spread.T[:, 0:1].astype(jnp.int32)
    hot = lax.broadcasted_iota(jnp.int32, (picks, patch.shape[0]), 1) == column
    seq_out[extras:, :] = mm(jnp.where(hot, 1.0, 0.0).astype(BF16), patch[...])
    seq_out[0:extras, :] = extra[image].astype(F32)
    hat, _ = normed(seq_out[...])
    first = (hat * line(gain) + line(shift)).astype(BF16)
    first_out[...] = first
    for j in range(3):
        qkv_out[:, j * inner : (j + 1) * inner] = mm(first, weight[j]).astype(BF16)
    masks = side_masks(HEAD_DIM**-0.5)
    lane = lax.broadcasted_iota(jnp.int32, (rows, PAIR), 1)
    logs = jnp.zeros((rows, PAIR), F32)
    for pair in range(inner // PAIR):
        q = qkv_out[:, pair * PAIR : (pair + 1) * PAIR]
        k = qkv_out[:, inner + pair * PAIR : inner + (pair + 1) * PAIR]
        v = qkv_out[:, 2 * inner + pair * PAIR : 2 * inner + (pair + 1) * PAIR]
        sides = []
        for side in range(2):
            scores = mm_nt(q * masks[side], k)
            top = jnp.max(scores, -1, keepdims=True)
            expo = jnp.exp(scores - top)
            total = jnp.sum(expo, -1, keepdims=True)
            sides.append(mm((expo * (1.0 / total)).astype(BF16), v))
            logs = jnp.where(lane == 2 * pair + side, top + jnp.log(total), logs)
        mixed = jnp.where(lane < HEAD_DIM, sides[0], sides[1]).astype(BF16).astype(F32)
        mixed_out[:, pair * PAIR : (pair + 1) * PAIR] = mixed
    log_out[...] = logs


def join_body(ids, mine, *refs):
    *quarters, full_out = refs
    half = mine.shape[0]
    part = quarters[0].shape[0]
    other = (1 - ids[4]) * half
    full_out[pl.ds(pl.multiple_of(ids[4] * half, part), half), :] = mine[...]
    for i, quarter in enumerate(quarters):
        place = ((ids[1] ^ (i & 1)) * 2 + (ids[0] ^ (i >> 1))) * part
        full_out[pl.ds(pl.multiple_of(other + place, part), part), :] = quarter[...].astype(BF16)


def forward_body(
    ids, seq, dy, out_bias, gain, shift, up_bias, mine, other, full, up, down,
    middle_out, second_out, hidden_out, upper_out, norm_out, small_out,
):
    rows, width = seq.shape
    inner = mine.shape[1]
    first_half = ids[4] == 0
    left = jnp.where(first_half, mine[...], other[...]).astype(BF16)
    right = jnp.where(first_half, other[...], mine[...]).astype(BF16)
    attn = mm(left, full[0:inner, :]) + mm(right, full[inner:, :]) + line(out_bias)
    middle = seq[...] + attn
    middle_out[...] = middle
    hat, _ = normed(middle)
    second = (hat * line(gain) + line(shift)).astype(BF16)
    second_out[...] = second
    grad = dy[...].astype(BF16)
    small_out[...] = jnp.zeros_like(small_out)
    chunk = 768
    biases = line(up_bias)
    norm = jnp.zeros((rows, width), F32)
    for start in range(0, up.shape[1], chunk):
        cols = slice(start, start + chunk)
        upper = mm(second, up[:, cols]) + biases[:, cols]
        phi = 0.5 + 0.5 * lax.erf(upper * (0.5**0.5))
        hidden_out[:, cols] = (upper * phi).astype(BF16)
        slope = phi + upper * (jnp.exp(-0.5 * upper * upper) * 0.3989422804014327)
        back = (mm_nt(grad, down[cols, :]) * slope).astype(BF16)
        upper_out[:, cols] = back
        total = jnp.sum(back.astype(F32), 0, keepdims=True)
        for at in range(start, start + chunk, 256):
            row, place = divmod(at, width)
            small_out[row : row + 1, place : place + 256] = total[:, at - start : at - start + 256]
        norm = norm + mm_nt(back, up[:, cols])
    norm_out[...] = norm
    small_out[4:5, :] = jnp.sum(grad.astype(F32), 0, keepdims=True)


def backward_body(mine, other, middle, qkv, logs, seq, dy, gain, out_weight, weight, *refs):
    (*before, grad_out, attn_out, back, part_out, small_out, cross_out) = refs
    before = before[0] if before else None
    rows, width = middle.shape
    inner = out_weight.shape[0]
    hat, rate = normed(middle[...])
    total = mine[...] + other[...]
    grad = dy[...].astype(F32) + norm_back(total, hat, rate, line(gain))
    grad_out[...] = grad
    attn = grad.astype(BF16)
    attn_out[...] = attn
    small_out[...] = jnp.zeros_like(small_out)
    small_out[2:3, :] = jnp.sum(total * hat, 0, keepdims=True)
    small_out[3:4, :] = jnp.sum(total, 0, keepdims=True)
    small_out[5:6, :] = jnp.sum(attn.astype(F32), 0, keepdims=True)
    mixed = mm_nt(attn, out_weight[...]).astype(BF16)
    masks = side_masks()
    scaled = side_masks(HEAD_DIM**-0.5)
    lane = lax.broadcasted_iota(jnp.int32, (rows, PAIR), 1)
    scale = HEAD_DIM**-0.5
    for pair in range(inner // PAIR):
        cols = slice(pair * PAIR, (pair + 1) * PAIR)
        q = qkv[:, cols]
        k = qkv[:, inner + pair * PAIR : inner + (pair + 1) * PAIR]
        v = qkv[:, 2 * inner + pair * PAIR : 2 * inner + (pair + 1) * PAIR]
        dm = mixed[:, cols]
        q_t = q.astype(F32).T.astype(BF16)
        dm_t = dm.astype(F32).T.astype(BF16)
        dq, dk, dv = [], [], []
        for side in range(2):
            half = slice(side * HEAD_DIM, (side + 1) * HEAD_DIM)
            head = 2 * pair + side
            scores = mm_nt(q * scaled[side], k)
            probs = jnp.exp(scores - logs[:, head : head + 1])
            dv.append(mm(dm_t[half, :], probs.astype(BF16)))
            prob_grad = mm_nt(dm * masks[side], v)
            score = probs * (prob_grad - jnp.sum(prob_grad * probs, -1, keepdims=True))
            score = score.astype(BF16)
            dq.append(mm(score, k))
            dk.append(mm(q_t[half, :], score))
        parts = (
            jnp.where(lane < HEAD_DIM, dq[0], dq[1]) * scale,
            (jnp.concatenate(dk, 0) * scale).T,
            jnp.concatenate(dv, 0).T,
        )
        for j, value in enumerate(parts):
            start = j * inner + pair * PAIR
            back[:, start : start + PAIR] = value.astype(BF16)
    part = mm_nt(back[:, 0:inner], weight[0])
    for j in range(1, 3):
        part = part + mm_nt(back[:, j * inner : (j + 1) * inner], weight[j])
    part_out[...] = part
    first_hat, _ = normed(seq[...])
    cross_out[...] = jnp.zeros_like(cross_out) if before is None else before[...]
    cross_out[6:7, 0:width] += jnp.sum(part * first_hat, 0, keepdims=True)
    cross_out[7:8, 0:width] += jnp.sum(part, 0, keepdims=True)


def branch_body(*refs):
    (*hiddens, down, part_out) = refs
    rows, size = hiddens[0].shape[0], part_out.shape[0] // len(hiddens)
    for image, hidden in enumerate(hiddens):
        part_out[(image + 1) * size - 8 : (image + 1) * size, :] = jnp.zeros((8, part_out.shape[1]), F32)
        part_out[image * size : image * size + rows, :] = mm(hidden[...], down[...])


def output_body(images, down_mine, down_other, bias, *refs):
    middles, out = refs[:images], refs[images]
    rows, size = middles[0].shape[0], down_mine.shape[0] // images
    for image in range(images):
        own = slice(image * size, image * size + rows)
        branch = down_mine[own, :] + down_other[own, :] + line(bias)
        out[image] = (middles[image][...] + branch).astype(BF16)


def input_body(gain, seq, mine, other, grad, out):
    hat, rate = normed(seq[...])
    out[...] = grad[...] + norm_back(mine[...] + other[...], hat, rate, line(gain))


def grads_body(layout, order, chunk, smalls, ids, *refs):
    lefts, rights, at = [], [], 0
    for images, _ in layout:
        lefts.append(refs[at : at + images])
        rights.append(refs[at + images : at + 2 * images])
        at += 2 * images
    small_refs = refs[at : at + smalls]
    keep, send, turned, stacked, tail = refs[at + smalls :]
    width = lefts[0][0].shape[1]
    size, half = width // 16, width // 2
    main = lefts[0][0].shape[0] // 8 * 8
    spare = lefts[0][0].shape[0] - main
    step = pl.program_id(0)
    even = ids[0] == 0

    def turn(value, start):
        columns = value.T
        stop = start + value.shape[0]
        for place in range(8):
            source = 0
            for digit, bit in enumerate(order):
                source |= ((place >> (2 - digit)) & 1) << bit
            zero = columns[source * size : (source + 1) * size, :]
            one = columns[(source + 1) * size : (source + 2) * size, :]
            rows = slice(place * size, (place + 1) * size)
            turned[rows, start:stop] = jnp.where(even, zero, one).astype(BF16)
            rows = slice(half + place * size, half + (place + 1) * size)
            turned[rows, start:stop] = jnp.where(even, one, zero).astype(BF16)

    begin = 0
    for (images, steps), left, right in zip(layout, lefts, rights):
        @pl.when(step == begin)
        def _(left=left, images=images):
            tail[...] = jnp.zeros_like(tail)
            for i, ref in enumerate(left):
                turn(ref[0:main, :], i * main)
                tail[i * spare : (i + 1) * spare, 0:width] = ref[main:, :].astype(F32)
            turn(tail[:, 0:width], images * main)

        @pl.when((step >= begin) & (step < begin + steps))
        def _(right=right, images=images):
            tail[...] = jnp.zeros_like(tail)
            for i, ref in enumerate(right):
                stacked[i * main : (i + 1) * main, :] = ref[0:main, :].astype(BF16)
                tail[i * spare : (i + 1) * spare, 0:chunk] = ref[main:, :].astype(F32)
            stacked[images * main :, :] = tail[:, 0:chunk].astype(BF16)

        begin += steps
    total = mm(turned[...], stacked[...])
    keep[0:half, :] = total[0:half, :]
    send[0:half, :] = total[half:, :]
    if smalls:
        keep[half:, :] = jnp.zeros_like(keep[half:, :])
        send[half:, :] = jnp.zeros_like(send[half:, :])
        for place in range(width // chunk):
            @pl.when(step == place)
            def _(place=place):
                cols = slice(place * chunk, (place + 1) * chunk)
                small = small_refs[0][:, cols]
                for ref in small_refs[1:]:
                    small = small + ref[:, cols]
                keep[half:, :] = small
                send[half:, :] = small


def sum_body(count, smalls, ids, *refs):
    blocks, small_refs, outs = refs[:count], refs[count : count + smalls], refs[count + smalls :]
    size = blocks[0].shape[0]
    total = blocks[0][...] + blocks[1][...]
    for ref in blocks[2:]:
        total = total + ref[...]
    outs[0][0:size, :] = total
    if smalls:
        kept, got, near, far_one, *rest = (ref[...] for ref in small_refs)
        small = (kept + got) + (near + far_one)
        for one in rest:
            small = small + one
        if len(outs) == 1:
            outs[0][size:, :] = small
        else:
            outs[1][...] = small


class Part:
    def __init__(self, chain, ids, dp, name, order, arrays, columns, at, cross):
        self.chain, self.ids, self.dp, self.name, self.order = chain, ids, dp, name, order
        self.columns, self.at, self.cross = columns, at, cross
        self.arrays = [(array, 0) for array in arrays]
        self.half = arrays[0].shape[0] // 8 * 8 if cross is None else arrays[0].shape[0] - 8
        self.steps = 0

    def add(self, digits, flip, outs, name):
        size = self.half >> digits
        args, specs = [self.ids], []

        def rows_of(level):
            def index(j, ids):
                at = 0
                for digit in range(level, digits):
                    bit = ids[self.order[digit]]
                    at = 2 * at + ((1 - bit) if flip and digit == digits - 1 else bit)
                return (at, self.at if level == 0 else 0)
            return index

        for array, level in self.arrays:
            args.append(array)
            specs.append(pl.BlockSpec((size, self.columns), rows_of(level)))
        smalls = 0
        if self.cross is not None:
            small = [(array, (self.half >> level) // 8) for array, level in self.arrays]
            small[2:2] = [(array, 0) for array in self.cross]
            for array, row in small:
                args.append(array)
                specs.append(pl.BlockSpec((8, self.columns), lambda j, ids, row=row: (row, 0)))
            smalls = len(small)
        return self.chain.call(
            partial(sum_body, len(self.arrays), smalls), args, specs, outs, 16, f"{self.name}_{name}",
            scalar=1, deep=(1, 2) if digits == 1 else (1,),
        )

    def step(self):
        if self.arrays is None:
            return
        bit = self.order[self.steps]
        self.steps += 1
        extra = 0 if self.cross is None else 8
        out = shape(((self.half >> self.steps) + extra, self.columns))
        (send,) = self.add(self.steps, True, [out], f"step{bit}")
        self.arrays.append((lax.ppermute(send, "dp", flips(self.dp, bit)), self.steps))

    def finish(self):
        outs = [shape((self.half >> self.steps, self.columns))]
        if self.cross is not None:
            outs.append(shape((8, self.columns)))
        return self.add(self.steps, False, outs, "last")


class Plain:
    def __init__(self, full, small):
        self.full, self.small = full, small

    def step(self):
        pass

    def finish(self):
        total = lax.psum_scatter(self.full, "dp", scatter_dimension=0, tiled=True)
        return [total] if self.small is None else [total, lax.psum(self.small, "dp")]


def weight_sum(chain, ids, dp, name, chunk, sets, smalls=(), cross=None, beside=None, parts=1, order=(1, 2, 3)):
    width = sets[0][0].shape[-1] if not isinstance(sets[0][0], list) else sets[0][0][0].shape[1]
    columns = sum(rights[0].shape[1] for _, rights in sets)
    size = columns // parts
    if not folded(dp):
        products = [sum(mm_tn(left, right.astype(BF16)) for left, right in zip(*pair)) for pair in sets]
        full = jnp.concatenate(products, 1)
        small = sum(smalls) + lax.ppermute(cross[:, :width], "mp", SWAP) if smalls else None
        pieces = [
            Plain(full[:, i * size : (i + 1) * size], small if i == 0 else None) for i in range(parts)
        ]
        return pieces, beside() if beside else None
    args, specs, layout, begin = [], [], [], 0
    for lefts, rights in sets:
        steps = rights[0].shape[1] // chunk
        if isinstance(lefts, list):
            args += lefts
            specs += [whole(v) for v in lefts]
        else:
            args += [lefts] * lefts.shape[0]
            specs += [one_of(lefts, b) for b in range(lefts.shape[0])]
        args += rights
        for v in rights:
            block = lambda j, begin=begin, steps=steps: (0, jnp.clip(j - begin, 0, steps - 1))
            specs.append(pl.BlockSpec((v.shape[0], chunk), block))
        layout.append((len(rights), steps))
        begin += steps
    images, rows = len(sets[0][1]), sets[0][1][0].shape[0]
    spare = 8 * pl.cdiv(images * (rows % 8), 8)
    depth = images * (rows // 8 * 8) + spare
    dims = (width // 2 + (8 if smalls else 0), columns)
    block = pl.BlockSpec((dims[0], chunk), lambda j: (0, j))
    keep, send = chain.call(
        partial(grads_body, layout, order, chunk, len(smalls)), [ids, *args, *smalls],
        [scalars(), *specs] + [whole(v) for v in smalls], [far(dims), far(dims)], 32,
        f"{name}_grads", grid=begin, out_specs=[block, block],
        scratch=[
            pltpu.VMEM((width, depth), BF16),
            pltpu.VMEM((depth, chunk), BF16),
            pltpu.VMEM((spare, max(width, chunk)), F32),
        ],
        deep=range(1, 1 + len(args)),
    )
    swap = lambda v: lax.ppermute(v, "dp", flips(dp, 0))
    if cross is not None:
        pairs = [((d, m), (d ^ 1, m ^ 1)) for d in range(dp) for m in range(2)]
        corners = [(2 * p[0] + p[1], 2 * q[0] + q[1]) for p, q in pairs]
        moves = lambda v, c: (swap(v), lax.ppermute(c, "mp", SWAP), lax.ppermute(c, ("dp", "mp"), corners))
        got, *crosses = chain.at_once(ids, moves, send, cross)
        done = None
    elif beside:
        got, done = chain.at_once(ids, lambda v: (swap(v), beside()), send)
        crosses = None
    else:
        (got,) = chain.at_once(ids, lambda v: (swap(v),), send)
        crosses, done = None, None
    pieces = [
        Part(chain, ids, dp, f"{name}{i}", order, [keep, got], size, i, crosses if i == 0 else None)
        for i in range(parts)
    ]
    for piece in pieces:
        piece.half = width // 2
    return pieces, done


def folded(dp):
    return dp == 16


def flips(dp, bit):
    return [(i, i ^ (1 << bit)) for i in range(dp)]


def per_device(
    dp,
    patches,
    extra_tokens,
    visible,
    qkv_weight,
    out_weight,
    out_bias,
    up_weight,
    up_bias,
    down_weight,
    down_bias,
    first_gain,
    first_shift,
    second_gain,
    second_shift,
    cotangent,
):
    images, _, width = patches.shape
    rows = visible.shape[1] + extra_tokens.shape[1]
    inner = qkv_weight.shape[2]
    hidden_width = up_weight.shape[1]
    place = lax.axis_index("dp")
    core = place % 2
    ids = jnp.stack([core] + [(place >> bit) & 1 for bit in (1, 2, 3)] + [lax.axis_index("mp")])
    ids = lax.optimization_barrier(ids.astype(jnp.int32))
    across = lambda v: lax.ppermute(v, "mp", SWAP)

    chain = Chain()
    every = range(images)

    quarter = inner // 4
    piece = lax.dynamic_slice_in_dim(out_weight, place % 4 * quarter, quarter, 0).astype(F32)
    near = across(piece)

    seqs, firsts, qkvs, logs, mixeds, mixed_others = [], [], [], [], [], []
    for b in every:
        args = [visible, patches, extra_tokens, qkv_weight, first_gain, first_shift]
        got = chain.call(
            partial(attend_body, b), args,
            [whole(visible), one_of(patches, b)] + [whole(a) for a in args[2:]],
            [far((rows, width)), far((rows, width), BF16), far((rows, 3 * inner), BF16),
             far((rows, PAIR)), shape((rows, inner))],
            40, f"attend{b}", deep=range(6),
        )
        for kept, one in zip((seqs, firsts, qkvs, logs, mixeds), got):
            kept.append(one)
        mixed_others.append(across(mixeds[b]))
        if b == 0:
            near = chain.hold(near)
            beyond = lax.ppermute(near, "dp", flips(dp, 1))
    swaps = lambda *vs: tuple(lax.ppermute(v, "dp", flips(dp, 0)) for v in vs)
    quarters = [near, beyond, *chain.at_once(ids, swaps, near, beyond)]
    (full,) = chain.call(
        join_body, [ids, out_weight, *quarters],
        [scalars(), whole(out_weight)] + [whole(q) for q in quarters],
        [shape((2 * inner, width), BF16)], 16, "join",
    )

    middles, seconds, hiddens, uppers, norms, smalls, norm_others = [], [], [], [], [], [], []
    for b in every:
        args = [ids, seqs[b], cotangent, out_bias, second_gain, second_shift, up_bias,
                mixeds[b], mixed_others[b], full, up_weight, down_weight]
        got = chain.call(
            forward_body, args,
            [scalars(), whole(seqs[b]), one_of(cotangent, b)] + [whole(a) for a in args[3:]],
            [far((rows, width)), far((rows, width), BF16), far((rows, hidden_width), BF16),
             far((rows, hidden_width), BF16), shape((rows, width)), far((8, width))],
            44, f"forward{b}", deep=(1, 3, 4, 5, 6),
        )
        for kept, one in zip((middles, seconds, hiddens, uppers, norms, smalls), got):
            kept.append(one)
        norm_others.append(across(norms[b]))

    padded = images * 8 * pl.cdiv(rows, 8)

    def branch():
        return kernel(
            branch_body, [*hiddens, down_weight], [whole(a) for a in (*hiddens, down_weight)],
            [shape((padded, width))], 32, "branch",
        )[0]

    (down_sum,), down_part = weight_sum(chain, ids, dp, "down", 768, [(cotangent, hiddens)], beside=branch)
    down_sum.step()

    grads, attns, backs, firsts_part, crosses, part_others = [], [], [], [], [], []
    for b in every:
        args = [norms[b], norm_others[b], middles[b], qkvs[b], logs[b], seqs[b], cotangent, second_gain,
                out_weight, qkv_weight, *crosses[-1:]]
        specs = [whole(a) for a in args]
        specs[6] = one_of(cotangent, b)
        got = chain.call(
            backward_body, args, specs,
            [far((rows, width)), far((rows, width), BF16), far((rows, 3 * inner), BF16),
             shape((rows, width)), far((8, width)), shape((8, hidden_width))],
            44, f"backward{b}", deep=(2, 3, 4, 5, 7), cost=33,
        )
        for kept, one in zip((grads, attns, backs, firsts_part, smalls, crosses), got):
            kept.append(one)
        part_others.append(across(firsts_part[b]))
        if b == 0:
            (up_sum,), _ = weight_sum(chain, ids, dp, "up", 768, [(seconds, uppers)])
            up_sum.step()
    part_others[0] = chain.hold(part_others[0])
    down_sum.step()
    sets = [(attns, mixeds), (firsts, backs)]
    (out_sum, qkv_sum), _ = weight_sum(
        chain, ids, dp, "last", 384, sets, [*smalls, crosses[-1][:, :width]], crosses[-1], parts=2,
    )

    def input_of(b):
        args = [first_gain, seqs[b], firsts_part[b], part_others[b], grads[b]]
        return chain.call(
            input_body, args, [whole(a) for a in args], [shape((rows, width))], 32, f"input{b}", deep=(0, 1, 4)
        )[0]

    out_sum.step()
    up_sum.step()
    down_sum.step()
    qkv_sum.step()
    input_grads = [input_of(b) for b in range(images - 1)]
    out_sum.step()
    input_grads.append(input_of(images - 1))
    down_part = chain.hold(down_part)
    down_other = across(down_part)
    (down_total,) = down_sum.finish()
    up_sum.step()
    qkv_sum.step()
    out_sum.step()
    (up_total,) = up_sum.finish()
    qkv_sum.step()
    out_total, small = out_sum.finish()
    args = [down_part, down_other, down_bias, *middles]
    (output,) = chain.call(
        partial(output_body, images), args, [whole(a) for a in args],
        [shape((images, rows, width), BF16)], 32, "output", deep=(2, 3, 4),
    )
    (qkv_total,) = qkv_sum.finish()
    small = small[:, :width]
    return (
        output,
        jnp.stack(input_grads),
        jnp.stack([out_total[:, inner:], qkv_total[:, :inner], qkv_total[:, inner:]]),
        out_total[:, :inner].T,
        small[5],
        up_total,
        small[0:2].reshape(-1),
        down_total.T,
        small[4],
        small[6],
        small[7],
        small[2],
        small[3],
    )


def solution(mesh):
    return jax.shard_map(
        partial(per_device, mesh.shape["dp"]),
        mesh=mesh,
        in_specs=(
            P("dp", None, None),
            P("dp", None, None),
            P("dp", None),
            P(None, None, "mp"),
            P("mp", None),
            P(),
            P(None, "mp"),
            P("mp"),
            P("mp", None),
            P(),
            P(),
            P(),
            P(),
            P(),
            P("dp", None, None),
        ),
        out_specs=(
            P("dp", None, None),
            P("dp", None, None),
            P(None, "dp", "mp"),
            P("mp", "dp"),
            P(),
            P("dp", "mp"),
            P("mp"),
            P("mp", "dp"),
            P(),
            P(),
            P(),
            P(),
            P(),
        ),
        check_vma=False,
    )
```

```python
from functools import partial

import jax
import jax.numpy as jnp
from jax import lax
from jax.experimental import pallas as pl
from jax.experimental.pallas import tpu as pltpu
from jax.sharding import PartitionSpec as P

HEAD_DIM = 64
PAIR = 2 * HEAD_DIM
F32 = jnp.float32
BF16 = jnp.bfloat16
MIB = 1 << 20
SWAP = ((0, 1), (1, 0))


def mm(a, b):
    return lax.dot_general(a, b, (((1,), (0,)), ((), ())), preferred_element_type=F32)


def mm_nt(a, b):
    return lax.dot_general(a, b, (((1,), (1,)), ((), ())), preferred_element_type=F32)


def mm_tn(a, b):
    return lax.dot_general(a, b, (((0,), (0,)), ((), ())), preferred_element_type=F32)


def normed(values):
    center = values - jnp.mean(values, -1, keepdims=True)
    rate = lax.rsqrt(jnp.mean(center * center, -1, keepdims=True) + 1e-06)
    return center * rate, rate


def norm_back(grad, hat, rate, gain):
    scaled = grad * gain
    return rate * (
        scaled
        - jnp.mean(scaled, -1, keepdims=True)
        - hat * jnp.mean(scaled * hat, -1, keepdims=True)
    )


def shape(dims, dtype=F32):
    return jax.ShapeDtypeStruct(tuple(dims), dtype)


def far(dims, dtype=F32):
    return pltpu.HBM(tuple(dims), dtype)


def whole(x):
    return pl.BlockSpec(x.shape, lambda i, *_: (0,) * len(x.shape))


def one_of(x, image):
    return pl.BlockSpec((None,) + x.shape[1:], lambda i, *_: (image,) + (0,) * (x.ndim - 1))


def scalars():
    return pl.BlockSpec(memory_space=pltpu.SMEM)


ANYWHERE = pl.BlockSpec(memory_space=pl.ANY)


def kernel(body, args, specs, outs, vmem, name, grid=1, out_specs=None, scratch=(), deep=(), scalar=0, cost=31):
    args = [pltpu.with_memory_space_constraint(a, pltpu.HBM) if i in deep else a for i, a in enumerate(args)]
    return pl.pallas_call(
        body,
        out_shape=tuple(outs),
        grid_spec=pltpu.PrefetchScalarGridSpec(
            num_scalar_prefetch=scalar,
            grid=(grid,),
            in_specs=specs,
            out_specs=tuple(out_specs or [whole(o) for o in outs]),
            scratch_shapes=list(scratch),
        ),
        compiler_params=pltpu.CompilerParams(vmem_limit_bytes=vmem * MIB),
        cost_estimate=pl.CostEstimate(flops=1 << cost, bytes_accessed=1, transcendentals=0),
        name=name,
    )(*args)


class Chain:
    def __init__(self):
        self.token = jnp.zeros((8, 128), F32)

    def call(self, body, args, specs, outs, vmem, name, out_specs=None, **more):
        taken, given = len(args), len(outs)

        def without_tokens(*refs):
            return body(*refs[:taken], *refs[taken + 1 : taken + 1 + given], *refs[taken + 2 + given :])

        *got, self.token = kernel(
            without_tokens, [*args, self.token], [*specs, ANYWHERE], [*outs, shape((8, 128))], vmem, name,
            out_specs=[*(out_specs or [whole(o) for o in outs]), ANYWHERE], **more,
        )
        return got

    def hold(self, value):
        value, self.token = lax.optimization_barrier((value, self.token))
        return value

    def at_once(self, ids, moves, *values):
        outs = jax.eval_shape(moves, *values)
        moved = lambda token, *vs: (token, *moves(*vs))
        never = lambda token, *vs: (token, *(jnp.zeros(o.shape, o.dtype) for o in outs))
        self.token, *got = lax.cond(ids[0] >= 0, moved, never, self.token, *values)
        return got


def line(vector):
    return vector[...].reshape(1, -1)


def side_masks(value=1.0):
    lane = lax.broadcasted_iota(jnp.int32, (1, PAIR), 1)
    low = jnp.where(lane < HEAD_DIM, value, 0.0)
    return low.astype(BF16), (value - low).astype(BF16)


def attend_body(image, pick, patch, extra, weight, gain, shift, seq_out, first_out, qkv_out, log_out, mixed_out):
    rows, width = seq_out.shape
    inner = mixed_out.shape[1]
    extras, picks = extra.shape[1], pick.shape[1]
    spread = jnp.broadcast_to(pick[image : image + 1, :].astype(F32), (128, picks))
    column = spread.T[:, 0:1].astype(jnp.int32)
    hot = lax.broadcasted_iota(jnp.int32, (picks, patch.shape[0]), 1) == column
    seq_out[extras:, :] = mm(jnp.where(hot, 1.0, 0.0).astype(BF16), patch[...])
    seq_out[0:extras, :] = extra[image].astype(F32)
    hat, _ = normed(seq_out[...])
    first = (hat * line(gain) + line(shift)).astype(BF16)
    first_out[...] = first
    for j in range(3):
        qkv_out[:, j * inner : (j + 1) * inner] = mm(first, weight[j]).astype(BF16)
    masks = side_masks(HEAD_DIM**-0.5)
    lane = lax.broadcasted_iota(jnp.int32, (rows, PAIR), 1)
    logs = jnp.zeros((rows, PAIR), F32)
    for pair in range(inner // PAIR):
        q = qkv_out[:, pair * PAIR : (pair + 1) * PAIR]
        k = qkv_out[:, inner + pair * PAIR : inner + (pair + 1) * PAIR]
        v = qkv_out[:, 2 * inner + pair * PAIR : 2 * inner + (pair + 1) * PAIR]
        sides = []
        for side in range(2):
            scores = mm_nt(q * masks[side], k)
            top = jnp.max(scores, -1, keepdims=True)
            expo = jnp.exp(scores - top)
            total = jnp.sum(expo, -1, keepdims=True)
            sides.append(mm((expo * (1.0 / total)).astype(BF16), v))
            logs = jnp.where(lane == 2 * pair + side, top + jnp.log(total), logs)
        mixed = jnp.where(lane < HEAD_DIM, sides[0], sides[1]).astype(BF16).astype(F32)
        mixed_out[:, pair * PAIR : (pair + 1) * PAIR] = mixed
    log_out[...] = logs


def join_body(ids, mine, *refs):
    *quarters, full_out = refs
    half = mine.shape[0]
    part = quarters[0].shape[0]
    other = (1 - ids[4]) * half
    full_out[pl.ds(pl.multiple_of(ids[4] * half, part), half), :] = mine[...]
    for i, quarter in enumerate(quarters):
        place = ((ids[1] ^ (i & 1)) * 2 + (ids[0] ^ (i >> 1))) * part
        full_out[pl.ds(pl.multiple_of(other + place, part), part), :] = quarter[...].astype(BF16)


def forward_body(
    ids, seq, dy, out_bias, gain, shift, up_bias, mine, other, full, up, down,
    middle_out, second_out, hidden_out, upper_out, norm_out, small_out,
):
    rows, width = seq.shape
    inner = mine.shape[1]
    first_half = ids[4] == 0
    left = jnp.where(first_half, mine[...], other[...]).astype(BF16)
    right = jnp.where(first_half, other[...], mine[...]).astype(BF16)
    attn = mm(left, full[0:inner, :]) + mm(right, full[inner:, :]) + line(out_bias)
    middle = seq[...] + attn
    middle_out[...] = middle
    hat, _ = normed(middle)
    second = (hat * line(gain) + line(shift)).astype(BF16)
    second_out[...] = second
    grad = dy[...].astype(BF16)
    small_out[...] = jnp.zeros_like(small_out)
    chunk = 768
    biases = line(up_bias)
    norm = jnp.zeros((rows, width), F32)
    for start in range(0, up.shape[1], chunk):
        cols = slice(start, start + chunk)
        upper = mm(second, up[:, cols]) + biases[:, cols]
        phi = 0.5 + 0.5 * lax.erf(upper * (0.5**0.5))
        hidden_out[:, cols] = (upper * phi).astype(BF16)
        slope = phi + upper * (jnp.exp(-0.5 * upper * upper) * 0.3989422804014327)
        back = (mm_nt(grad, down[cols, :]) * slope).astype(BF16)
        upper_out[:, cols] = back
        total = jnp.sum(back.astype(F32), 0, keepdims=True)
        for at in range(start, start + chunk, 256):
            row, place = divmod(at, width)
            small_out[row : row + 1, place : place + 256] = total[:, at - start : at - start + 256]
        norm = norm + mm_nt(back, up[:, cols])
    norm_out[...] = norm
    small_out[4:5, :] = jnp.sum(grad.astype(F32), 0, keepdims=True)


def backward_body(mine, other, middle, qkv, logs, seq, dy, gain, out_weight, weight, *refs):
    (*before, grad_out, attn_out, back, part_out, small_out, cross_out) = refs
    before = before[0] if before else None
    rows, width = middle.shape
    inner = out_weight.shape[0]
    hat, rate = normed(middle[...])
    total = mine[...] + other[...]
    grad = dy[...].astype(F32) + norm_back(total, hat, rate, line(gain))
    grad_out[...] = grad
    attn = grad.astype(BF16)
    attn_out[...] = attn
    small_out[...] = jnp.zeros_like(small_out)
    small_out[2:3, :] = jnp.sum(total * hat, 0, keepdims=True)
    small_out[3:4, :] = jnp.sum(total, 0, keepdims=True)
    small_out[5:6, :] = jnp.sum(attn.astype(F32), 0, keepdims=True)
    mixed = mm_nt(attn, out_weight[...]).astype(BF16)
    masks = side_masks()
    scaled = side_masks(HEAD_DIM**-0.5)
    lane = lax.broadcasted_iota(jnp.int32, (rows, PAIR), 1)
    scale = HEAD_DIM**-0.5
    for pair in range(inner // PAIR):
        cols = slice(pair * PAIR, (pair + 1) * PAIR)
        q = qkv[:, cols]
        k = qkv[:, inner + pair * PAIR : inner + (pair + 1) * PAIR]
        v = qkv[:, 2 * inner + pair * PAIR : 2 * inner + (pair + 1) * PAIR]
        dm = mixed[:, cols]
        q_t = q.astype(F32).T.astype(BF16)
        dm_t = dm.astype(F32).T.astype(BF16)
        dq, dk, dv = [], [], []
        for side in range(2):
            half = slice(side * HEAD_DIM, (side + 1) * HEAD_DIM)
            head = 2 * pair + side
            scores = mm_nt(q * scaled[side], k)
            probs = jnp.exp(scores - logs[:, head : head + 1])
            dv.append(mm(dm_t[half, :], probs.astype(BF16)))
            prob_grad = mm_nt(dm * masks[side], v)
            score = probs * (prob_grad - jnp.sum(prob_grad * probs, -1, keepdims=True))
            score = score.astype(BF16)
            dq.append(mm(score, k))
            dk.append(mm(q_t[half, :], score))
        parts = (
            jnp.where(lane < HEAD_DIM, dq[0], dq[1]) * scale,
            (jnp.concatenate(dk, 0) * scale).T,
            jnp.concatenate(dv, 0).T,
        )
        for j, value in enumerate(parts):
            start = j * inner + pair * PAIR
            back[:, start : start + PAIR] = value.astype(BF16)
    part = mm_nt(back[:, 0:inner], weight[0])
    for j in range(1, 3):
        part = part + mm_nt(back[:, j * inner : (j + 1) * inner], weight[j])
    part_out[...] = part
    first_hat, _ = normed(seq[...])
    cross_out[...] = jnp.zeros_like(cross_out) if before is None else before[...]
    cross_out[6:7, 0:width] += jnp.sum(part * first_hat, 0, keepdims=True)
    cross_out[7:8, 0:width] += jnp.sum(part, 0, keepdims=True)


def branch_body(*refs):
    (*hiddens, down, part_out) = refs
    rows, size = hiddens[0].shape[0], part_out.shape[0] // len(hiddens)
    for image, hidden in enumerate(hiddens):
        part_out[(image + 1) * size - 8 : (image + 1) * size, :] = jnp.zeros((8, part_out.shape[1]), F32)
        part_out[image * size : image * size + rows, :] = mm(hidden[...], down[...])


def output_body(images, down_mine, down_other, bias, *refs):
    middles, out = refs[:images], refs[images]
    rows, size = middles[0].shape[0], down_mine.shape[0] // images
    for image in range(images):
        own = slice(image * size, image * size + rows)
        branch = down_mine[own, :] + down_other[own, :] + line(bias)
        out[image] = (middles[image][...] + branch).astype(BF16)


def input_body(gain, seq, mine, other, grad, out):
    hat, rate = normed(seq[...])
    out[...] = grad[...] + norm_back(mine[...] + other[...], hat, rate, line(gain))


def grads_body(layout, order, chunk, smalls, ids, *refs):
    lefts, rights, at = [], [], 0
    for images, _ in layout:
        lefts.append(refs[at : at + images])
        rights.append(refs[at + images : at + 2 * images])
        at += 2 * images
    small_refs = refs[at : at + smalls]
    keep, send, turned, stacked, tail = refs[at + smalls :]
    width = lefts[0][0].shape[1]
    size, half = width // 16, width // 2
    main = lefts[0][0].shape[0] // 8 * 8
    spare = lefts[0][0].shape[0] - main
    step = pl.program_id(0)
    even = ids[0] == 0

    def turn(value, start):
        columns = value.T
        stop = start + value.shape[0]
        for place in range(8):
            source = 0
            for digit, bit in enumerate(order):
                source |= ((place >> (2 - digit)) & 1) << bit
            zero = columns[source * size : (source + 1) * size, :]
            one = columns[(source + 1) * size : (source + 2) * size, :]
            rows = slice(place * size, (place + 1) * size)
            turned[rows, start:stop] = jnp.where(even, zero, one).astype(BF16)
            rows = slice(half + place * size, half + (place + 1) * size)
            turned[rows, start:stop] = jnp.where(even, one, zero).astype(BF16)

    begin = 0
    for (images, steps), left, right in zip(layout, lefts, rights):
        @pl.when(step == begin)
        def _(left=left, images=images):
            tail[...] = jnp.zeros_like(tail)
            for i, ref in enumerate(left):
                turn(ref[0:main, :], i * main)
                tail[i * spare : (i + 1) * spare, 0:width] = ref[main:, :].astype(F32)
            turn(tail[:, 0:width], images * main)

        @pl.when((step >= begin) & (step < begin + steps))
        def _(right=right, images=images):
            tail[...] = jnp.zeros_like(tail)
            for i, ref in enumerate(right):
                stacked[i * main : (i + 1) * main, :] = ref[0:main, :].astype(BF16)
                tail[i * spare : (i + 1) * spare, 0:chunk] = ref[main:, :].astype(F32)
            stacked[images * main :, :] = tail[:, 0:chunk].astype(BF16)

        begin += steps
    total = mm(turned[...], stacked[...])
    keep[0:half, :] = total[0:half, :]
    send[0:half, :] = total[half:, :]
    if smalls:
        keep[half:, :] = jnp.zeros_like(keep[half:, :])
        send[half:, :] = jnp.zeros_like(send[half:, :])
        for place in range(width // chunk):
            @pl.when(step == place)
            def _(place=place):
                cols = slice(place * chunk, (place + 1) * chunk)
                small = small_refs[0][:, cols]
                for ref in small_refs[1:]:
                    small = small + ref[:, cols]
                keep[half:, :] = small
                send[half:, :] = small


def sum_body(count, smalls, ids, *refs):
    blocks, small_refs, outs = refs[:count], refs[count : count + smalls], refs[count + smalls :]
    size = blocks[0].shape[0]
    total = blocks[0][...] + blocks[1][...]
    for ref in blocks[2:]:
        total = total + ref[...]
    outs[0][0:size, :] = total
    if smalls:
        kept, got, near, far_one, *rest = (ref[...] for ref in small_refs)
        small = (kept + got) + (near + far_one)
        for one in rest:
            small = small + one
        if len(outs) == 1:
            outs[0][size:, :] = small
        else:
            outs[1][...] = small


class Part:
    def __init__(self, chain, ids, dp, name, order, arrays, columns, at, cross):
        self.chain, self.ids, self.dp, self.name, self.order = chain, ids, dp, name, order
        self.columns, self.at, self.cross = columns, at, cross
        self.arrays = [(array, 0) for array in arrays]
        self.half = arrays[0].shape[0] // 8 * 8 if cross is None else arrays[0].shape[0] - 8
        self.steps = 0

    def add(self, digits, flip, outs, name):
        size = self.half >> digits
        args, specs = [self.ids], []

        def rows_of(level):
            def index(j, ids):
                at = 0
                for digit in range(level, digits):
                    bit = ids[self.order[digit]]
                    at = 2 * at + ((1 - bit) if flip and digit == digits - 1 else bit)
                return (at, self.at if level == 0 else 0)
            return index

        for array, level in self.arrays:
            args.append(array)
            specs.append(pl.BlockSpec((size, self.columns), rows_of(level)))
        smalls = 0
        if self.cross is not None:
            small = [(array, (self.half >> level) // 8) for array, level in self.arrays]
            small[2:2] = [(array, 0) for array in self.cross]
            for array, row in small:
                args.append(array)
                specs.append(pl.BlockSpec((8, self.columns), lambda j, ids, row=row: (row, 0)))
            smalls = len(small)
        return self.chain.call(
            partial(sum_body, len(self.arrays), smalls), args, specs, outs, 16, f"{self.name}_{name}",
            scalar=1, deep=(1, 2) if digits == 1 else (1,),
        )

    def step(self):
        if self.arrays is None:
            return
        bit = self.order[self.steps]
        self.steps += 1
        extra = 0 if self.cross is None else 8
        out = shape(((self.half >> self.steps) + extra, self.columns))
        (send,) = self.add(self.steps, True, [out], f"step{bit}")
        self.arrays.append((lax.ppermute(send, "dp", flips(self.dp, bit)), self.steps))

    def finish(self):
        outs = [shape((self.half >> self.steps, self.columns))]
        if self.cross is not None:
            outs.append(shape((8, self.columns)))
        return self.add(self.steps, False, outs, "last")


class Plain:
    def __init__(self, full, small):
        self.full, self.small = full, small

    def step(self):
        pass

    def finish(self):
        total = lax.psum_scatter(self.full, "dp", scatter_dimension=0, tiled=True)
        return [total] if self.small is None else [total, lax.psum(self.small, "dp")]


def weight_sum(chain, ids, dp, name, chunk, sets, smalls=(), cross=None, beside=None, parts=1, order=(1, 2, 3)):
    width = sets[0][0].shape[-1] if not isinstance(sets[0][0], list) else sets[0][0][0].shape[1]
    columns = sum(rights[0].shape[1] for _, rights in sets)
    size = columns // parts
    if not folded(dp):
        products = [sum(mm_tn(left, right.astype(BF16)) for left, right in zip(*pair)) for pair in sets]
        full = jnp.concatenate(products, 1)
        small = sum(smalls) + lax.ppermute(cross[:, :width], "mp", SWAP) if smalls else None
        pieces = [
            Plain(full[:, i * size : (i + 1) * size], small if i == 0 else None) for i in range(parts)
        ]
        return pieces, beside() if beside else None
    args, specs, layout, begin = [], [], [], 0
    for lefts, rights in sets:
        steps = rights[0].shape[1] // chunk
        if isinstance(lefts, list):
            args += lefts
            specs += [whole(v) for v in lefts]
        else:
            args += [lefts] * lefts.shape[0]
            specs += [one_of(lefts, b) for b in range(lefts.shape[0])]
        args += rights
        for v in rights:
            block = lambda j, begin=begin, steps=steps: (0, jnp.clip(j - begin, 0, steps - 1))
            specs.append(pl.BlockSpec((v.shape[0], chunk), block))
        layout.append((len(rights), steps))
        begin += steps
    images, rows = len(sets[0][1]), sets[0][1][0].shape[0]
    spare = 8 * pl.cdiv(images * (rows % 8), 8)
    depth = images * (rows // 8 * 8) + spare
    dims = (width // 2 + (8 if smalls else 0), columns)
    block = pl.BlockSpec((dims[0], chunk), lambda j: (0, j))
    keep, send = chain.call(
        partial(grads_body, layout, order, chunk, len(smalls)), [ids, *args, *smalls],
        [scalars(), *specs] + [whole(v) for v in smalls], [far(dims), far(dims)], 32,
        f"{name}_grads", grid=begin, out_specs=[block, block],
        scratch=[
            pltpu.VMEM((width, depth), BF16),
            pltpu.VMEM((depth, chunk), BF16),
            pltpu.VMEM((spare, max(width, chunk)), F32),
        ],
        deep=range(1, 1 + len(args)),
    )
    swap = lambda v: lax.ppermute(v, "dp", flips(dp, 0))
    if cross is not None:
        pairs = [((d, m), (d ^ 1, m ^ 1)) for d in range(dp) for m in range(2)]
        corners = [(2 * p[0] + p[1], 2 * q[0] + q[1]) for p, q in pairs]
        moves = lambda v, c: (swap(v), lax.ppermute(c, "mp", SWAP), lax.ppermute(c, ("dp", "mp"), corners))
        got, *crosses = chain.at_once(ids, moves, send, cross)
        done = None
    elif beside:
        got, done = chain.at_once(ids, lambda v: (swap(v), beside()), send)
        crosses = None
    else:
        (got,) = chain.at_once(ids, lambda v: (swap(v),), send)
        crosses, done = None, None
    pieces = [
        Part(chain, ids, dp, f"{name}{i}", order, [keep, got], size, i, crosses if i == 0 else None)
        for i in range(parts)
    ]
    for piece in pieces:
        piece.half = width // 2
    return pieces, done


def folded(dp):
    return dp == 16


def flips(dp, bit):
    return [(i, i ^ (1 << bit)) for i in range(dp)]


def per_device(
    dp,
    patches,
    extra_tokens,
    visible,
    qkv_weight,
    out_weight,
    out_bias,
    up_weight,
    up_bias,
    down_weight,
    down_bias,
    first_gain,
    first_shift,
    second_gain,
    second_shift,
    cotangent,
):
    images, _, width = patches.shape
    rows = visible.shape[1] + extra_tokens.shape[1]
    inner = qkv_weight.shape[2]
    hidden_width = up_weight.shape[1]
    place = lax.axis_index("dp")
    core = place % 2
    ids = jnp.stack([core] + [(place >> bit) & 1 for bit in (1, 2, 3)] + [lax.axis_index("mp")])
    ids = lax.optimization_barrier(ids.astype(jnp.int32))
    across = lambda v: lax.ppermute(v, "mp", SWAP)

    chain = Chain()
    every = range(images)

    quarter = inner // 4
    piece = lax.dynamic_slice_in_dim(out_weight, place % 4 * quarter, quarter, 0).astype(F32)
    near = across(piece)

    seqs, firsts, qkvs, logs, mixeds, mixed_others = [], [], [], [], [], []
    for b in every:
        args = [visible, patches, extra_tokens, qkv_weight, first_gain, first_shift]
        got = chain.call(
            partial(attend_body, b), args,
            [whole(visible), one_of(patches, b)] + [whole(a) for a in args[2:]],
            [far((rows, width)), far((rows, width), BF16), far((rows, 3 * inner), BF16),
             far((rows, PAIR)), shape((rows, inner))],
            40, f"attend{b}", deep=range(6),
        )
        for kept, one in zip((seqs, firsts, qkvs, logs, mixeds), got):
            kept.append(one)
        mixed_others.append(across(mixeds[b]))
        if b == 0:
            near = chain.hold(near)
            beyond = lax.ppermute(near, "dp", flips(dp, 1))
    swaps = lambda *vs: tuple(lax.ppermute(v, "dp", flips(dp, 0)) for v in vs)
    quarters = [near, beyond, *chain.at_once(ids, swaps, near, beyond)]
    (full,) = chain.call(
        join_body, [ids, out_weight, *quarters],
        [scalars(), whole(out_weight)] + [whole(q) for q in quarters],
        [shape((2 * inner, width), BF16)], 16, "join",
    )

    middles, seconds, hiddens, uppers, norms, smalls, norm_others = [], [], [], [], [], [], []
    for b in every:
        args = [ids, seqs[b], cotangent, out_bias, second_gain, second_shift, up_bias,
                mixeds[b], mixed_others[b], full, up_weight, down_weight]
        got = chain.call(
            forward_body, args,
            [scalars(), whole(seqs[b]), one_of(cotangent, b)] + [whole(a) for a in args[3:]],
            [far((rows, width)), far((rows, width), BF16), far((rows, hidden_width), BF16),
             far((rows, hidden_width), BF16), shape((rows, width)), far((8, width))],
            44, f"forward{b}", cost=32, deep=(1, 3, 4, 5, 6),
        )
        for kept, one in zip((middles, seconds, hiddens, uppers, norms, smalls), got):
            kept.append(one)
        norm_others.append(across(norms[b]))

    padded = images * 8 * pl.cdiv(rows, 8)

    def branch():
        return kernel(
            branch_body, [*hiddens, down_weight], [whole(a) for a in (*hiddens, down_weight)],
            [shape((padded, width))], 32, "branch",
        )[0]

    (down_sum,), down_part = weight_sum(chain, ids, dp, "down", 768, [(cotangent, hiddens)], beside=branch)
    down_sum.step()

    grads, attns, backs, firsts_part, crosses, part_others = [], [], [], [], [], []
    for b in every:
        args = [norms[b], norm_others[b], middles[b], qkvs[b], logs[b], seqs[b], cotangent, second_gain,
                out_weight, qkv_weight, *crosses[-1:]]
        specs = [whole(a) for a in args]
        specs[6] = one_of(cotangent, b)
        got = chain.call(
            backward_body, args, specs,
            [far((rows, width)), far((rows, width), BF16), far((rows, 3 * inner), BF16),
             shape((rows, width)), far((8, width)), shape((8, hidden_width))],
            44, f"backward{b}", deep=(2, 3, 4, 5, 7), cost=33,
        )
        for kept, one in zip((grads, attns, backs, firsts_part, smalls, crosses), got):
            kept.append(one)
        part_others.append(across(firsts_part[b]))
        if b == 0:
            (up_sum,), _ = weight_sum(chain, ids, dp, "up", 768, [(seconds, uppers)])
            up_sum.step()
    part_others[0] = chain.hold(part_others[0])
    down_sum.step()
    sets = [(attns, mixeds), (firsts, backs)]
    (out_sum, qkv_sum), _ = weight_sum(
        chain, ids, dp, "last", 384, sets, [*smalls, crosses[-1][:, :width]], crosses[-1], parts=2,
    )

    def input_of(b):
        args = [first_gain, seqs[b], firsts_part[b], part_others[b], grads[b]]
        return chain.call(
            input_body, args, [whole(a) for a in args], [shape((rows, width))], 32, f"input{b}", deep=(0, 1, 4)
        )[0]

    out_sum.step()
    up_sum.step()
    down_sum.step()
    qkv_sum.step()
    input_grads = [input_of(b) for b in range(images - 1)]
    out_sum.step()
    input_grads.append(input_of(images - 1))
    down_part = chain.hold(down_part)
    down_other = across(down_part)
    (down_total,) = down_sum.finish()
    up_sum.step()
    qkv_sum.step()
    out_sum.step()
    (up_total,) = up_sum.finish()
    qkv_sum.step()
    out_total, small = out_sum.finish()
    args = [down_part, down_other, down_bias, *middles]
    (output,) = chain.call(
        partial(output_body, images), args, [whole(a) for a in args],
        [shape((images, rows, width), BF16)], 32, "output", deep=(2, 3, 4),
    )
    (qkv_total,) = qkv_sum.finish()
    small = small[:, :width]
    return (
        output,
        jnp.stack(input_grads),
        jnp.stack([out_total[:, inner:], qkv_total[:, :inner], qkv_total[:, inner:]]),
        out_total[:, :inner].T,
        small[5],
        up_total,
        small[0:2].reshape(-1),
        down_total.T,
        small[4],
        small[6],
        small[7],
        small[2],
        small[3],
    )


def solution(mesh):
    return jax.shard_map(
        partial(per_device, mesh.shape["dp"]),
        mesh=mesh,
        in_specs=(
            P("dp", None, None),
            P("dp", None, None),
            P("dp", None),
            P(None, None, "mp"),
            P("mp", None),
            P(),
            P(None, "mp"),
            P("mp"),
            P("mp", None),
            P(),
            P(),
            P(),
            P(),
            P(),
            P("dp", None, None),
        ),
        out_specs=(
            P("dp", None, None),
            P("dp", None, None),
            P(None, "dp", "mp"),
            P("mp", "dp"),
            P(),
            P("dp", "mp"),
            P("mp"),
            P("mp", "dp"),
            P(),
            P(),
            P(),
            P(),
            P(),
        ),
        check_vma=False,
    )
```

```python
from functools import partial

import jax
import jax.numpy as jnp
from jax import lax
from jax.experimental import pallas as pl
from jax.experimental.pallas import tpu as pltpu
from jax.sharding import PartitionSpec as P

HEAD_DIM = 64
PAIR = 2 * HEAD_DIM
F32 = jnp.float32
BF16 = jnp.bfloat16
MIB = 1 << 20
SWAP = ((0, 1), (1, 0))


def mm(a, b):
    return lax.dot_general(a, b, (((1,), (0,)), ((), ())), preferred_element_type=F32)


def mm_nt(a, b):
    return lax.dot_general(a, b, (((1,), (1,)), ((), ())), preferred_element_type=F32)


def mm_tn(a, b):
    return lax.dot_general(a, b, (((0,), (0,)), ((), ())), preferred_element_type=F32)


def normed(values):
    center = values - jnp.mean(values, -1, keepdims=True)
    rate = lax.rsqrt(jnp.mean(center * center, -1, keepdims=True) + 1e-06)
    return center * rate, rate


def norm_back(grad, hat, rate, gain):
    scaled = grad * gain
    return rate * (
        scaled
        - jnp.mean(scaled, -1, keepdims=True)
        - hat * jnp.mean(scaled * hat, -1, keepdims=True)
    )


def shape(dims, dtype=F32):
    return jax.ShapeDtypeStruct(tuple(dims), dtype)


def far(dims, dtype=F32):
    return pltpu.HBM(tuple(dims), dtype)


def whole(x):
    return pl.BlockSpec(x.shape, lambda i, *_: (0,) * len(x.shape))


def one_of(x, image):
    return pl.BlockSpec((None,) + x.shape[1:], lambda i, *_: (image,) + (0,) * (x.ndim - 1))


def scalars():
    return pl.BlockSpec(memory_space=pltpu.SMEM)


ANYWHERE = pl.BlockSpec(memory_space=pl.ANY)


def kernel(body, args, specs, outs, vmem, name, grid=1, out_specs=None, scratch=(), deep=(), scalar=0, cost=31):
    args = [pltpu.with_memory_space_constraint(a, pltpu.HBM) if i in deep else a for i, a in enumerate(args)]
    return pl.pallas_call(
        body,
        out_shape=tuple(outs),
        grid_spec=pltpu.PrefetchScalarGridSpec(
            num_scalar_prefetch=scalar,
            grid=(grid,),
            in_specs=specs,
            out_specs=tuple(out_specs or [whole(o) for o in outs]),
            scratch_shapes=list(scratch),
        ),
        compiler_params=pltpu.CompilerParams(vmem_limit_bytes=vmem * MIB),
        cost_estimate=pl.CostEstimate(flops=1 << cost, bytes_accessed=1, transcendentals=0),
        name=name,
    )(*args)


class Chain:
    def __init__(self):
        self.token = jnp.zeros((8, 128), F32)

    def call(self, body, args, specs, outs, vmem, name, out_specs=None, **more):
        taken, given = len(args), len(outs)

        def without_tokens(*refs):
            return body(*refs[:taken], *refs[taken + 1 : taken + 1 + given], *refs[taken + 2 + given :])

        *got, self.token = kernel(
            without_tokens, [*args, self.token], [*specs, ANYWHERE], [*outs, shape((8, 128))], vmem, name,
            out_specs=[*(out_specs or [whole(o) for o in outs]), ANYWHERE], **more,
        )
        return got

    def hold(self, value):
        value, self.token = lax.optimization_barrier((value, self.token))
        return value

    def at_once(self, ids, moves, *values):
        outs = jax.eval_shape(moves, *values)
        moved = lambda token, *vs: (token, *moves(*vs))
        never = lambda token, *vs: (token, *(jnp.zeros(o.shape, o.dtype) for o in outs))
        self.token, *got = lax.cond(ids[0] >= 0, moved, never, self.token, *values)
        return got


def line(vector):
    return vector[...].reshape(1, -1)


def side_masks(value=1.0):
    lane = lax.broadcasted_iota(jnp.int32, (1, PAIR), 1)
    low = jnp.where(lane < HEAD_DIM, value, 0.0)
    return low.astype(BF16), (value - low).astype(BF16)


def attend_body(image, pick, patch, extra, weight, gain, shift, seq_out, first_out, qkv_out, log_out, mixed_out):
    rows, width = seq_out.shape
    inner = mixed_out.shape[1]
    extras, picks = extra.shape[1], pick.shape[1]
    spread = jnp.broadcast_to(pick[image : image + 1, :].astype(F32), (128, picks))
    column = spread.T[:, 0:1].astype(jnp.int32)
    hot = lax.broadcasted_iota(jnp.int32, (picks, patch.shape[0]), 1) == column
    seq_out[extras:, :] = mm(jnp.where(hot, 1.0, 0.0).astype(BF16), patch[...])
    seq_out[0:extras, :] = extra[image].astype(F32)
    hat, _ = normed(seq_out[...])
    first = (hat * line(gain) + line(shift)).astype(BF16)
    first_out[...] = first
    for j in range(3):
        qkv_out[:, j * inner : (j + 1) * inner] = mm(first, weight[j]).astype(BF16)
    masks = side_masks(HEAD_DIM**-0.5)
    lane = lax.broadcasted_iota(jnp.int32, (rows, PAIR), 1)
    logs = jnp.zeros((rows, PAIR), F32)
    for pair in range(inner // PAIR):
        q = qkv_out[:, pair * PAIR : (pair + 1) * PAIR]
        k = qkv_out[:, inner + pair * PAIR : inner + (pair + 1) * PAIR]
        v = qkv_out[:, 2 * inner + pair * PAIR : 2 * inner + (pair + 1) * PAIR]
        sides = []
        for side in range(2):
            scores = mm_nt(q * masks[side], k)
            top = jnp.max(scores, -1, keepdims=True)
            expo = jnp.exp(scores - top)
            total = jnp.sum(expo, -1, keepdims=True)
            sides.append(mm((expo * (1.0 / total)).astype(BF16), v))
            logs = jnp.where(lane == 2 * pair + side, top + jnp.log(total), logs)
        mixed = jnp.where(lane < HEAD_DIM, sides[0], sides[1]).astype(BF16).astype(F32)
        mixed_out[:, pair * PAIR : (pair + 1) * PAIR] = mixed
    log_out[...] = logs


def join_body(ids, mine, *refs):
    *quarters, full_out = refs
    half = mine.shape[0]
    part = quarters[0].shape[0]
    other = (1 - ids[4]) * half
    full_out[pl.ds(pl.multiple_of(ids[4] * half, part), half), :] = mine[...]
    for i, quarter in enumerate(quarters):
        place = ((ids[1] ^ (i & 1)) * 2 + (ids[0] ^ (i >> 1))) * part
        full_out[pl.ds(pl.multiple_of(other + place, part), part), :] = quarter[...].astype(BF16)


def forward_body(
    ids, seq, dy, out_bias, gain, shift, up_bias, mine, other, full, up, down,
    middle_out, second_out, hidden_out, upper_out, norm_out, small_out,
):
    rows, width = seq.shape
    inner = mine.shape[1]
    first_half = ids[4] == 0
    left = jnp.where(first_half, mine[...], other[...]).astype(BF16)
    right = jnp.where(first_half, other[...], mine[...]).astype(BF16)
    attn = mm(left, full[0:inner, :]) + mm(right, full[inner:, :]) + line(out_bias)
    middle = seq[...] + attn
    middle_out[...] = middle
    hat, _ = normed(middle)
    second = (hat * line(gain) + line(shift)).astype(BF16)
    second_out[...] = second
    grad = dy[...].astype(BF16)
    small_out[...] = jnp.zeros_like(small_out)
    chunk = 768
    biases = line(up_bias)
    norm = jnp.zeros((rows, width), F32)
    for start in range(0, up.shape[1], chunk):
        cols = slice(start, start + chunk)
        upper = mm(second, up[:, cols]) + biases[:, cols]
        phi = 0.5 + 0.5 * lax.erf(upper * (0.5**0.5))
        hidden_out[:, cols] = (upper * phi).astype(BF16)
        slope = phi + upper * (jnp.exp(-0.5 * upper * upper) * 0.3989422804014327)
        back = (mm_nt(grad, down[cols, :]) * slope).astype(BF16)
        upper_out[:, cols] = back
        total = jnp.sum(back.astype(F32), 0, keepdims=True)
        for at in range(start, start + chunk, 256):
            row, place = divmod(at, width)
            small_out[row : row + 1, place : place + 256] = total[:, at - start : at - start + 256]
        norm = norm + mm_nt(back, up[:, cols])
    norm_out[...] = norm
    small_out[4:5, :] = jnp.sum(grad.astype(F32), 0, keepdims=True)


def backward_body(mine, other, middle, qkv, logs, seq, dy, gain, out_weight, weight, *refs):
    (*before, grad_out, attn_out, back, part_out, small_out, cross_out) = refs
    before = before[0] if before else None
    rows, width = middle.shape
    inner = out_weight.shape[0]
    hat, rate = normed(middle[...])
    total = mine[...] + other[...]
    grad = dy[...].astype(F32) + norm_back(total, hat, rate, line(gain))
    grad_out[...] = grad
    attn = grad.astype(BF16)
    attn_out[...] = attn
    small_out[...] = jnp.zeros_like(small_out)
    small_out[2:3, :] = jnp.sum(total * hat, 0, keepdims=True)
    small_out[3:4, :] = jnp.sum(total, 0, keepdims=True)
    small_out[5:6, :] = jnp.sum(attn.astype(F32), 0, keepdims=True)
    mixed = mm_nt(attn, out_weight[...]).astype(BF16)
    masks = side_masks()
    scaled = side_masks(HEAD_DIM**-0.5)
    lane = lax.broadcasted_iota(jnp.int32, (rows, PAIR), 1)
    scale = HEAD_DIM**-0.5
    for pair in range(inner // PAIR):
        cols = slice(pair * PAIR, (pair + 1) * PAIR)
        q = qkv[:, cols]
        k = qkv[:, inner + pair * PAIR : inner + (pair + 1) * PAIR]
        v = qkv[:, 2 * inner + pair * PAIR : 2 * inner + (pair + 1) * PAIR]
        dm = mixed[:, cols]
        q_t = q.astype(F32).T.astype(BF16)
        dm_t = dm.astype(F32).T.astype(BF16)
        dq, dk, dv = [], [], []
        for side in range(2):
            half = slice(side * HEAD_DIM, (side + 1) * HEAD_DIM)
            head = 2 * pair + side
            scores = mm_nt(q * scaled[side], k)
            probs = jnp.exp(scores - logs[:, head : head + 1])
            dv.append(mm(dm_t[half, :], probs.astype(BF16)))
            prob_grad = mm_nt(dm * masks[side], v)
            score = probs * (prob_grad - jnp.sum(prob_grad * probs, -1, keepdims=True))
            score = score.astype(BF16)
            dq.append(mm(score, k))
            dk.append(mm(q_t[half, :], score))
        parts = (
            jnp.where(lane < HEAD_DIM, dq[0], dq[1]) * scale,
            (jnp.concatenate(dk, 0) * scale).T,
            jnp.concatenate(dv, 0).T,
        )
        for j, value in enumerate(parts):
            start = j * inner + pair * PAIR
            back[:, start : start + PAIR] = value.astype(BF16)
    part = mm_nt(back[:, 0:inner], weight[0])
    for j in range(1, 3):
        part = part + mm_nt(back[:, j * inner : (j + 1) * inner], weight[j])
    part_out[...] = part
    first_hat, _ = normed(seq[...])
    cross_out[...] = jnp.zeros_like(cross_out) if before is None else before[...]
    cross_out[6:7, 0:width] += jnp.sum(part * first_hat, 0, keepdims=True)
    cross_out[7:8, 0:width] += jnp.sum(part, 0, keepdims=True)


def branch_body(*refs):
    (*hiddens, down, part_out) = refs
    rows, size = hiddens[0].shape[0], part_out.shape[0] // len(hiddens)
    for image, hidden in enumerate(hiddens):
        part_out[(image + 1) * size - 8 : (image + 1) * size, :] = jnp.zeros((8, part_out.shape[1]), F32)
        part_out[image * size : image * size + rows, :] = mm(hidden[...], down[...])


def output_body(images, down_mine, down_other, bias, *refs):
    middles, out = refs[:images], refs[images]
    rows, size = middles[0].shape[0], down_mine.shape[0] // images
    for image in range(images):
        own = slice(image * size, image * size + rows)
        branch = down_mine[own, :] + down_other[own, :] + line(bias)
        out[image] = (middles[image][...] + branch).astype(BF16)


def input_body(gain, seq, mine, other, grad, out):
    hat, rate = normed(seq[...])
    out[...] = grad[...] + norm_back(mine[...] + other[...], hat, rate, line(gain))


def grads_body(layout, order, chunk, smalls, ids, *refs):
    lefts, rights, at = [], [], 0
    for images, _ in layout:
        lefts.append(refs[at : at + images])
        rights.append(refs[at + images : at + 2 * images])
        at += 2 * images
    small_refs = refs[at : at + smalls]
    keep, send, turned, stacked, tail = refs[at + smalls :]
    width = lefts[0][0].shape[1]
    size, half = width // 16, width // 2
    main = lefts[0][0].shape[0] // 8 * 8
    spare = lefts[0][0].shape[0] - main
    step = pl.program_id(0)
    even = ids[0] == 0

    def turn(value, start):
        columns = value.T
        stop = start + value.shape[0]
        for place in range(8):
            source = 0
            for digit, bit in enumerate(order):
                source |= ((place >> (2 - digit)) & 1) << bit
            zero = columns[source * size : (source + 1) * size, :]
            one = columns[(source + 1) * size : (source + 2) * size, :]
            rows = slice(place * size, (place + 1) * size)
            turned[rows, start:stop] = jnp.where(even, zero, one).astype(BF16)
            rows = slice(half + place * size, half + (place + 1) * size)
            turned[rows, start:stop] = jnp.where(even, one, zero).astype(BF16)

    begin = 0
    for (images, steps), left, right in zip(layout, lefts, rights):
        @pl.when(step == begin)
        def _(left=left, images=images):
            tail[...] = jnp.zeros_like(tail)
            for i, ref in enumerate(left):
                turn(ref[0:main, :], i * main)
                tail[i * spare : (i + 1) * spare, 0:width] = ref[main:, :].astype(F32)
            turn(tail[:, 0:width], images * main)

        @pl.when((step >= begin) & (step < begin + steps))
        def _(right=right, images=images):
            tail[...] = jnp.zeros_like(tail)
            for i, ref in enumerate(right):
                stacked[i * main : (i + 1) * main, :] = ref[0:main, :].astype(BF16)
                tail[i * spare : (i + 1) * spare, 0:chunk] = ref[main:, :].astype(F32)
            stacked[images * main :, :] = tail[:, 0:chunk].astype(BF16)

        begin += steps
    total = mm(turned[...], stacked[...])
    keep[0:half, :] = total[0:half, :]
    send[0:half, :] = total[half:, :]
    if smalls:
        keep[half:, :] = jnp.zeros_like(keep[half:, :])
        send[half:, :] = jnp.zeros_like(send[half:, :])
        for place in range(width // chunk):
            @pl.when(step == place)
            def _(place=place):
                cols = slice(place * chunk, (place + 1) * chunk)
                small = small_refs[0][:, cols]
                for ref in small_refs[1:]:
                    small = small + ref[:, cols]
                keep[half:, :] = small
                send[half:, :] = small


def sum_body(count, smalls, ids, *refs):
    blocks, small_refs, outs = refs[:count], refs[count : count + smalls], refs[count + smalls :]
    size = blocks[0].shape[0]
    total = blocks[0][...] + blocks[1][...]
    for ref in blocks[2:]:
        total = total + ref[...]
    outs[0][0:size, :] = total
    if smalls:
        kept, got, near, far_one, *rest = (ref[...] for ref in small_refs)
        small = (kept + got) + (near + far_one)
        for one in rest:
            small = small + one
        if len(outs) == 1:
            outs[0][size:, :] = small
        else:
            outs[1][...] = small


class Part:
    def __init__(self, chain, ids, dp, name, order, arrays, columns, at, cross):
        self.chain, self.ids, self.dp, self.name, self.order = chain, ids, dp, name, order
        self.columns, self.at, self.cross = columns, at, cross
        self.arrays = [(array, 0) for array in arrays]
        self.half = arrays[0].shape[0] // 8 * 8 if cross is None else arrays[0].shape[0] - 8
        self.steps = 0

    def add(self, digits, flip, outs, name):
        size = self.half >> digits
        args, specs = [self.ids], []

        def rows_of(level):
            def index(j, ids):
                at = 0
                for digit in range(level, digits):
                    bit = ids[self.order[digit]]
                    at = 2 * at + ((1 - bit) if flip and digit == digits - 1 else bit)
                return (at, self.at if level == 0 else 0)
            return index

        for array, level in self.arrays:
            args.append(array)
            specs.append(pl.BlockSpec((size, self.columns), rows_of(level)))
        smalls = 0
        if self.cross is not None:
            small = [(array, (self.half >> level) // 8) for array, level in self.arrays]
            small[2:2] = [(array, 0) for array in self.cross]
            for array, row in small:
                args.append(array)
                specs.append(pl.BlockSpec((8, self.columns), lambda j, ids, row=row: (row, 0)))
            smalls = len(small)
        return self.chain.call(
            partial(sum_body, len(self.arrays), smalls), args, specs, outs, 16, f"{self.name}_{name}",
            scalar=1, deep=(1, 2) if digits == 1 else (1,),
        )

    def step(self):
        if self.arrays is None:
            return
        bit = self.order[self.steps]
        self.steps += 1
        extra = 0 if self.cross is None else 8
        out = shape(((self.half >> self.steps) + extra, self.columns))
        (send,) = self.add(self.steps, True, [out], f"step{bit}")
        self.arrays.append((lax.ppermute(send, "dp", flips(self.dp, bit)), self.steps))

    def finish(self):
        outs = [shape((self.half >> self.steps, self.columns))]
        if self.cross is not None:
            outs.append(shape((8, self.columns)))
        return self.add(self.steps, False, outs, "last")


class Plain:
    def __init__(self, full, small):
        self.full, self.small = full, small

    def step(self):
        pass

    def finish(self):
        total = lax.psum_scatter(self.full, "dp", scatter_dimension=0, tiled=True)
        return [total] if self.small is None else [total, lax.psum(self.small, "dp")]


def weight_sum(chain, ids, dp, name, chunk, sets, smalls=(), cross=None, beside=None, parts=1, order=(1, 2, 3)):
    width = sets[0][0].shape[-1] if not isinstance(sets[0][0], list) else sets[0][0][0].shape[1]
    columns = sum(rights[0].shape[1] for _, rights in sets)
    size = columns // parts
    if not folded(dp):
        products = [sum(mm_tn(left, right.astype(BF16)) for left, right in zip(*pair)) for pair in sets]
        full = jnp.concatenate(products, 1)
        small = sum(smalls) + lax.ppermute(cross[:, :width], "mp", SWAP) if smalls else None
        pieces = [
            Plain(full[:, i * size : (i + 1) * size], small if i == 0 else None) for i in range(parts)
        ]
        return pieces, beside() if beside else None
    args, specs, layout, begin = [], [], [], 0
    for lefts, rights in sets:
        steps = rights[0].shape[1] // chunk
        if isinstance(lefts, list):
            args += lefts
            specs += [whole(v) for v in lefts]
        else:
            args += [lefts] * lefts.shape[0]
            specs += [one_of(lefts, b) for b in range(lefts.shape[0])]
        args += rights
        for v in rights:
            block = lambda j, begin=begin, steps=steps: (0, jnp.clip(j - begin, 0, steps - 1))
            specs.append(pl.BlockSpec((v.shape[0], chunk), block))
        layout.append((len(rights), steps))
        begin += steps
    images, rows = len(sets[0][1]), sets[0][1][0].shape[0]
    spare = 8 * pl.cdiv(images * (rows % 8), 8)
    depth = images * (rows // 8 * 8) + spare
    dims = (width // 2 + (8 if smalls else 0), columns)
    block = pl.BlockSpec((dims[0], chunk), lambda j: (0, j))
    keep, send = chain.call(
        partial(grads_body, layout, order, chunk, len(smalls)), [ids, *args, *smalls],
        [scalars(), *specs] + [whole(v) for v in smalls], [far(dims), far(dims)], 32,
        f"{name}_grads", cost=32, grid=begin, out_specs=[block, block],
        scratch=[
            pltpu.VMEM((width, depth), BF16),
            pltpu.VMEM((depth, chunk), BF16),
            pltpu.VMEM((spare, max(width, chunk)), F32),
        ],
        deep=range(1, 1 + len(args)),
    )
    swap = lambda v: lax.ppermute(v, "dp", flips(dp, 0))
    if cross is not None:
        pairs = [((d, m), (d ^ 1, m ^ 1)) for d in range(dp) for m in range(2)]
        corners = [(2 * p[0] + p[1], 2 * q[0] + q[1]) for p, q in pairs]
        moves = lambda v, c: (swap(v), lax.ppermute(c, "mp", SWAP), lax.ppermute(c, ("dp", "mp"), corners))
        got, *crosses = chain.at_once(ids, moves, send, cross)
        done = None
    elif beside:
        got, done = chain.at_once(ids, lambda v: (swap(v), beside()), send)
        crosses = None
    else:
        (got,) = chain.at_once(ids, lambda v: (swap(v),), send)
        crosses, done = None, None
    pieces = [
        Part(chain, ids, dp, f"{name}{i}", order, [keep, got], size, i, crosses if i == 0 else None)
        for i in range(parts)
    ]
    for piece in pieces:
        piece.half = width // 2
    return pieces, done


def folded(dp):
    return dp == 16


def flips(dp, bit):
    return [(i, i ^ (1 << bit)) for i in range(dp)]


def per_device(
    dp,
    patches,
    extra_tokens,
    visible,
    qkv_weight,
    out_weight,
    out_bias,
    up_weight,
    up_bias,
    down_weight,
    down_bias,
    first_gain,
    first_shift,
    second_gain,
    second_shift,
    cotangent,
):
    images, _, width = patches.shape
    rows = visible.shape[1] + extra_tokens.shape[1]
    inner = qkv_weight.shape[2]
    hidden_width = up_weight.shape[1]
    place = lax.axis_index("dp")
    core = place % 2
    ids = jnp.stack([core] + [(place >> bit) & 1 for bit in (1, 2, 3)] + [lax.axis_index("mp")])
    ids = lax.optimization_barrier(ids.astype(jnp.int32))
    across = lambda v: lax.ppermute(v, "mp", SWAP)

    chain = Chain()
    every = range(images)

    quarter = inner // 4
    piece = lax.dynamic_slice_in_dim(out_weight, place % 4 * quarter, quarter, 0).astype(F32)
    near = across(piece)

    seqs, firsts, qkvs, logs, mixeds, mixed_others = [], [], [], [], [], []
    for b in every:
        args = [visible, patches, extra_tokens, qkv_weight, first_gain, first_shift]
        got = chain.call(
            partial(attend_body, b), args,
            [whole(visible), one_of(patches, b)] + [whole(a) for a in args[2:]],
            [far((rows, width)), far((rows, width), BF16), far((rows, 3 * inner), BF16),
             far((rows, PAIR)), shape((rows, inner))],
            40, f"attend{b}", deep=range(6),
        )
        for kept, one in zip((seqs, firsts, qkvs, logs, mixeds), got):
            kept.append(one)
        mixed_others.append(across(mixeds[b]))
        if b == 0:
            near = chain.hold(near)
            beyond = lax.ppermute(near, "dp", flips(dp, 1))
    swaps = lambda *vs: tuple(lax.ppermute(v, "dp", flips(dp, 0)) for v in vs)
    quarters = [near, beyond, *chain.at_once(ids, swaps, near, beyond)]
    (full,) = chain.call(
        join_body, [ids, out_weight, *quarters],
        [scalars(), whole(out_weight)] + [whole(q) for q in quarters],
        [shape((2 * inner, width), BF16)], 16, "join",
    )

    middles, seconds, hiddens, uppers, norms, smalls, norm_others = [], [], [], [], [], [], []
    for b in every:
        args = [ids, seqs[b], cotangent, out_bias, second_gain, second_shift, up_bias,
                mixeds[b], mixed_others[b], full, up_weight, down_weight]
        got = chain.call(
            forward_body, args,
            [scalars(), whole(seqs[b]), one_of(cotangent, b)] + [whole(a) for a in args[3:]],
            [far((rows, width)), far((rows, width), BF16), far((rows, hidden_width), BF16),
             far((rows, hidden_width), BF16), shape((rows, width)), far((8, width))],
            44, f"forward{b}", cost=32, deep=(1, 3, 4, 5, 6),
        )
        for kept, one in zip((middles, seconds, hiddens, uppers, norms, smalls), got):
            kept.append(one)
        norm_others.append(across(norms[b]))

    padded = images * 8 * pl.cdiv(rows, 8)

    def branch():
        return kernel(
            branch_body, [*hiddens, down_weight], [whole(a) for a in (*hiddens, down_weight)],
            [shape((padded, width))], 32, "branch",
        )[0]

    (down_sum,), down_part = weight_sum(chain, ids, dp, "down", 768, [(cotangent, hiddens)], beside=branch)
    down_sum.step()

    grads, attns, backs, firsts_part, crosses, part_others = [], [], [], [], [], []
    for b in every:
        args = [norms[b], norm_others[b], middles[b], qkvs[b], logs[b], seqs[b], cotangent, second_gain,
                out_weight, qkv_weight, *crosses[-1:]]
        specs = [whole(a) for a in args]
        specs[6] = one_of(cotangent, b)
        got = chain.call(
            backward_body, args, specs,
            [far((rows, width)), far((rows, width), BF16), far((rows, 3 * inner), BF16),
             shape((rows, width)), far((8, width)), shape((8, hidden_width))],
            44, f"backward{b}", deep=(2, 3, 4, 5, 7), cost=33,
        )
        for kept, one in zip((grads, attns, backs, firsts_part, smalls, crosses), got):
            kept.append(one)
        part_others.append(across(firsts_part[b]))
        if b == 0:
            (up_sum,), _ = weight_sum(chain, ids, dp, "up", 768, [(seconds, uppers)])
            up_sum.step()
    part_others[0] = chain.hold(part_others[0])
    down_sum.step()
    sets = [(attns, mixeds), (firsts, backs)]
    (out_sum, qkv_sum), _ = weight_sum(
        chain, ids, dp, "last", 384, sets, [*smalls, crosses[-1][:, :width]], crosses[-1], parts=2,
    )

    def input_of(b):
        args = [first_gain, seqs[b], firsts_part[b], part_others[b], grads[b]]
        return chain.call(
            input_body, args, [whole(a) for a in args], [shape((rows, width))], 32, f"input{b}", deep=(0, 1, 4)
        )[0]

    out_sum.step()
    up_sum.step()
    down_sum.step()
    qkv_sum.step()
    input_grads = [input_of(b) for b in range(images - 1)]
    out_sum.step()
    input_grads.append(input_of(images - 1))
    down_part = chain.hold(down_part)
    down_other = across(down_part)
    (down_total,) = down_sum.finish()
    up_sum.step()
    qkv_sum.step()
    out_sum.step()
    (up_total,) = up_sum.finish()
    qkv_sum.step()
    out_total, small = out_sum.finish()
    args = [down_part, down_other, down_bias, *middles]
    (output,) = chain.call(
        partial(output_body, images), args, [whole(a) for a in args],
        [shape((images, rows, width), BF16)], 32, "output", deep=(2, 3, 4),
    )
    (qkv_total,) = qkv_sum.finish()
    small = small[:, :width]
    return (
        output,
        jnp.stack(input_grads),
        jnp.stack([out_total[:, inner:], qkv_total[:, :inner], qkv_total[:, inner:]]),
        out_total[:, :inner].T,
        small[5],
        up_total,
        small[0:2].reshape(-1),
        down_total.T,
        small[4],
        small[6],
        small[7],
        small[2],
        small[3],
    )


def solution(mesh):
    return jax.shard_map(
        partial(per_device, mesh.shape["dp"]),
        mesh=mesh,
        in_specs=(
            P("dp", None, None),
            P("dp", None, None),
            P("dp", None),
            P(None, None, "mp"),
            P("mp", None),
            P(),
            P(None, "mp"),
            P("mp"),
            P("mp", None),
            P(),
            P(),
            P(),
            P(),
            P(),
            P("dp", None, None),
        ),
        out_specs=(
            P("dp", None, None),
            P("dp", None, None),
            P(None, "dp", "mp"),
            P("mp", "dp"),
            P(),
            P("dp", "mp"),
            P("mp"),
            P("mp", "dp"),
            P(),
            P(),
            P(),
            P(),
            P(),
        ),
        check_vma=False,
    )
```
